32 devices in a mesh: dp: 4 (over z), fsdp: 8 (over y, x, core).
Axes of the slice: x: 2, y: 2, z: 4, core: 2. Of those that a mesh axis runs over, the one named last changes fastest.
Arguments:
- hidden: bfloat16 [65536, 768], P(('dp', 'fsdp')), may hold values from -6 to 6
- long_flags: int32 [128], P(('dp', 'fsdp')), may hold values 0 or 1
- norm1_gain: float32 [768], P(('dp', 'fsdp')), may hold values from 0.1 to 1.9
- query_w: float32 [768, 768], P(('dp', 'fsdp')), may hold values from -0.0546875 to 0.0546875
- key_w: float32 [768, 768], P(('dp', 'fsdp')), may hold values from -0.21875 to 0.21875
- value_w: float32 [768, 768], P(('dp', 'fsdp')), may hold values from -0.21875 to 0.21875
- out_w: float32 [768, 768], P(None, ('dp', 'fsdp')), may hold values from -0.875 to 0.875
- bias_table: float32 [32, 12], replicated, may hold values from -4 to 4
- norm2_gain: float32 [768], P(('dp', 'fsdp')), may hold values from 0.1 to 1.9
- ffn_in: float32 [768, 3072], P(('dp', 'fsdp')), may hold values from -0.21875 to 0.21875
- ffn_out: float32 [3072, 768], P(None, ('dp', 'fsdp')), may hold values from -0.109375 to 0.109375
- out_grad: bfloat16 [65536, 768], P(('dp', 'fsdp')), may hold values from -6 to 6
Outputs:
- output: bfloat16 [65536, 768], P(('dp', 'fsdp'))
- input_grad: bfloat16 [65536, 768], P(('dp', 'fsdp'))
- norm1_gain_grad: float32 [768], P(('dp', 'fsdp'))
- query_grad: float32 [768, 768], P(('dp', 'fsdp'))
- key_grad: float32 [768, 768], P(('dp', 'fsdp'))
- value_grad: float32 [768, 768], P(('dp', 'fsdp'))
- out_proj_grad: float32 [768, 768], P(None, ('dp', 'fsdp'))
- table_grad: float32 [32, 12], replicated
- norm2_gain_grad: float32 [768], P(('dp', 'fsdp'))
- ffn_in_grad: float32 [768, 3072], P(('dp', 'fsdp'))
- ffn_out_grad: float32 [3072, 768], P(None, ('dp', 'fsdp'))
The draws below stay inside these ranges and needn't reach their ends.
Inputs may be any that keep to these rules, and one draw needn't show every extreme that they name: `long_flags`: 1 where the 512 slots of a block hold one passage of 500 tokens, 0 where they hold two passages of 250 tokens; the slots after the passages are padding that forms a segment of its own.
All inputs are finite; a program needn't handle non-finite values.
Results may differ from the reference program's by a relative error of at most 0.013.
The reference program's roundings to bfloat16 on the way count: a program that leaves them out, or rounds other values in their place, can miss the bound.
Values may be sent and summed in bfloat16 or wider, within the bound.
No kernel may reach another device: no remote copies, remote signals or barrier semaphores. Data moves between devices by JAX's collectives and lax.ppermute only.
A program may use at most 256 MiB of HBM per device.

```python
import math
import jax
import jax.numpy as jnp
from jax import lax

D = 768
HEADS = 12
HEAD_DIM = 64
FF = 3072
BUCKETS = 32
MAX_DIST = 128
BLOCK = 512
LONG = 500
SHORT = 250
TOKENS = 65536


def plant(entries, rng, least, largest):
    longest = entries.shape.index(max(entries.shape))
    spots = []
    for shift in (0, 1):
        where = [jax.random.randint(jax.random.fold_in(rng, axis), (), 0, length) for axis, length in enumerate(entries.shape)]
        where[longest] = (where[longest] + shift) % entries.shape[longest]
        spots.append(tuple(where))
    return entries.at[spots[0]].set(least).at[spots[1]].set(largest)


def spiked(drawn, rng, source, target, parts, factor):
    def block_of(position):
        return (jnp.arange(drawn.shape[position]) // (drawn.shape[position] // parts)).reshape((-1,) + (1,) * (drawn.ndim - 1 - position))

    first = jax.random.permutation(rng, parts)[block_of(target)]
    other_side = (block_of(target) + parts // 2) % parts
    return jnp.where((block_of(source) == first) | (block_of(source) == other_side), factor * drawn, drawn)


def steps_of(key, shape, cuts, least, top_value):
    loudness, own = 1.0, jax.random.fold_in(key, 6)
    for position, shards_of in cuts:
        steps = jnp.exp(jax.random.uniform(jax.random.fold_in(own, position), (shards_of,), jnp.float32, least / len(cuts), top_value / len(cuts)))
        loudness = loudness * jnp.repeat(steps, shape[position] // shards_of).reshape([-1 if axis == position else 1 for axis in range(len(shape))])
    return loudness


def gaussian(own_key, dims, scale, limit, split=(), kind=jnp.bfloat16):
    gain = steps_of(own_key, dims, split, -0.22, 0.18) if split else 1.0
    values = jax.random.normal(own_key, dims, jnp.float32) * scale * gain
    return jnp.minimum(jnp.maximum(values, -limit), limit).astype(kind)


def bell_draw_with(own_key, extent, deviation, limit, split, heavy, kind=jnp.bfloat16):
    entries = deviation * jax.random.normal(own_key, extent, jnp.float32)
    if split:
        entries = entries * steps_of(own_key, extent, split, -0.22, 0.18)
    return jnp.clip(spiked(entries, jax.random.fold_in(own_key, 3), *heavy), -limit, limit).astype(kind)


def setup_inputs(seed: int = 0) -> dict:
    splits = jax.random.split(jax.random.key(seed), 13)
    return {
        "hidden": bell_draw_with(splits[0], (TOKENS, D), 1.0, 6.0, ((0, 32),), (0, 1, 32, 2.75)),
        "long_flags": plant((jax.random.randint(splits[1], (TOKENS // BLOCK,), 0, 2) < 1).astype(jnp.int32), jax.random.fold_in(splits[1], 1), 0, 1),
        "norm1_gain": jnp.clip(1.0 + 0.18 * jax.random.normal(splits[2], (D,), jnp.float32), 0.1, 1.9),
        "query_w": gaussian(splits[3], (D, D), (16 * D) ** -0.5, 0.0546875, ((0, 32),), jnp.float32),
        "key_w": gaussian(splits[4], (D, D), D ** -0.5, 0.21875, ((0, 32),), jnp.float32),
        "value_w": gaussian(splits[5], (D, D), D ** -0.5, 0.21875, ((0, 32),), jnp.float32),
        "out_w": gaussian(splits[6], (D, D), (D // 16) ** -0.5, 0.875, ((1, 32),), jnp.float32),
        "bias_table": gaussian(splits[7], (BUCKETS, HEADS), 1.0, 4.0, (), jnp.float32),
        "norm2_gain": jnp.clip(1.0 + 0.18 * jax.random.normal(splits[8], (D,), jnp.float32), 0.1, 1.9),
        "ffn_in": gaussian(splits[9], (D, FF), D ** -0.5, 0.21875, ((0, 32),), jnp.float32),
        "ffn_out": gaussian(splits[10], (FF, D), FF ** -0.5, 0.109375, ((1, 32),), jnp.float32),
        "out_grad": bell_draw_with(splits[11], (TOKENS, D), 1.0, 6.0, ((0, 32),), (0, 1, 32, 2.75)),
    }


norm_eps = 1e-06
masked_score = -1000000000.0

@jax.custom_vjp
def low(v):
    return lax.optimization_barrier(v.astype(jnp.bfloat16)).astype(jnp.float32)

@jax.custom_vjp
def low_back(v):
    return v

def low_keep(v):
    return (low(v), None)

def low_pass(kept, grad):
    return (grad,)

def back_keep(v):
    return (v, None)

def back_low(kept, grad):
    return (low(grad),)
low.defvjp(low_keep, low_pass)
low_back.defvjp(back_keep, back_low)

def bucket_limits():
    exact_count = BUCKETS // 4
    half_count = BUCKETS // 2
    scale_log = math.log(MAX_DIST / exact_count)
    thresholds = []
    for target in range(1, half_count - exact_count):
        distance = exact_count
        while int(math.log(distance / exact_count) / scale_log * (half_count - exact_count)) < target:
            distance += 1
        thresholds.append(distance)
    return thresholds

def bucket_grid():
    slot_ids = jnp.arange(BLOCK, dtype=jnp.int32)
    relative = slot_ids[None, :] - slot_ids[:, None]
    distance = jnp.abs(relative)
    exact_count = BUCKETS // 4
    beyond = jnp.full_like(distance, exact_count)
    for threshold in bucket_limits():
        beyond = beyond + (distance >= threshold).astype(jnp.int32)
    inside = jnp.where(distance < exact_count, distance, beyond)
    return inside + (relative > 0).astype(jnp.int32) * (BUCKETS // 2)

def segment_mask(long_flag):
    slot_ids = jnp.arange(BLOCK, dtype=jnp.int32)
    long_ids = (slot_ids >= LONG).astype(jnp.int32)
    short_ids = (slot_ids >= SHORT).astype(jnp.int32) + (slot_ids >= 2 * SHORT).astype(jnp.int32)
    segment = jnp.where(long_flag == 1, long_ids, short_ids)
    return segment[:, None] == segment[None, :]

def matmul_high(left, right):
    return jnp.dot(left, right, precision=lax.Precision.HIGHEST)

def rms_scale(values):
    return lax.rsqrt(lax.optimization_barrier(jnp.mean(values * values, axis=-1, keepdims=True)) + norm_eps)

def norm_piece(values, gain_full):
    return values * rms_scale(values) * gain_full

def unit_layer(weights, position_bias, packed):
    gain_one, weight_q, weight_k, weight_v, weight_o, gain_two, weight_in, weight_out = weights
    block_in, long_flag = packed
    normed = low(norm_piece(block_in, gain_one))
    queries = low(low_back(matmul_high(normed, weight_q))).reshape(BLOCK, HEADS, HEAD_DIM)
    key_heads = low(low_back(matmul_high(normed, weight_k))).reshape(BLOCK, HEADS, HEAD_DIM)
    value_heads = low(low_back(matmul_high(normed, weight_v))).reshape(BLOCK, HEADS, HEAD_DIM)
    scores = jnp.einsum('ihd,jhd->hij', queries, key_heads, precision=lax.Precision.HIGHEST) + position_bias
    scores = low_back(scores)
    masked = jnp.where(segment_mask(long_flag)[None], scores, masked_score)
    row_top = lax.optimization_barrier(jnp.max(masked, axis=-1, keepdims=True))
    exp_scores = jnp.exp(masked - row_top)
    attn_probs = low(exp_scores / lax.optimization_barrier(jnp.sum(exp_scores, axis=-1, keepdims=True)))
    attended = jnp.einsum('hij,jhd->ihd', attn_probs, value_heads, precision=lax.Precision.HIGHEST)
    attended = low(low_back(attended.reshape(BLOCK, HEADS * HEAD_DIM)))
    middle = block_in + low_back(matmul_high(attended, weight_o))
    normed_two = low(norm_piece(middle, gain_two))
    ffn_inner = low_back(matmul_high(normed_two, weight_in))
    activated = low(jax.nn.gelu(ffn_inner, approximate=False))
    return middle + low_back(matmul_high(activated, weight_out))

def layer(hidden, norm1_gain, query_w, key_w, value_w, out_w, bias_table, norm2_gain, ffn_in, ffn_out, long_flags):
    onehot = (bucket_grid()[:, :, None] == jnp.arange(BUCKETS, dtype=jnp.int32)[None, None, :]).astype(jnp.float32)
    position_bias = jnp.einsum('ijb,bh->hij', onehot, bias_table, precision=lax.Precision.HIGHEST)
    weights = (low(norm1_gain), low(query_w), low(key_w), low(value_w), low(out_w), low(norm2_gain), low(ffn_in), low(ffn_out))
    step_fn = jax.checkpoint(unit_layer)
    blocks_in = hidden.reshape(-1, BLOCK, hidden.shape[1])
    result = lax.map(lambda packed: step_fn(weights, position_bias, packed), (blocks_in, long_flags))
    return result.reshape(hidden.shape)

def reference(hidden, long_flags, norm1_gain, query_w, key_w, value_w, out_w, bias_table, norm2_gain, ffn_in, ffn_out, out_grad):
    primals = (hidden.astype(jnp.float32), norm1_gain, query_w, key_w, value_w, out_w, bias_table, norm2_gain, ffn_in, ffn_out)

    def forward(*floats):
        return layer(*floats, long_flags)
    result, pullback = jax.vjp(forward, *primals)
    grads = pullback(out_grad.astype(jnp.float32))
    return (result.astype(jnp.bfloat16), grads[0].astype(jnp.bfloat16), grads[1], grads[2], grads[3], grads[4], grads[5], grads[6], grads[7], grads[8], grads[9])
```

```python
import math, functools
import jax, jax.numpy as jnp
from jax import lax
from jax.experimental import pallas as pl
from jax.experimental.pallas import tpu as pltpu
HEADS=12; HEAD_DIM=64; BUCKETS=32; MAX_DIST=128; BLOCK=512; LONG=500; SHORT=250
F32=jnp.float32; BF16=jnp.bfloat16
far=-2.0**30
NN=(((1,),(0,)),((),())); NT=(((1,),(1,)),((),())); TN=(((0,),(0,)),((),()))
def dot(a,b,dn=NN): return lax.dot_general(a,b,dn,preferred_element_type=F32)

def bucket_limits():
    exact_count = BUCKETS // 4
    half_count = BUCKETS // 2
    scale_log = math.log(MAX_DIST / exact_count)
    thresholds = []
    for target in range(1, half_count - exact_count):
        distance = exact_count
        while int(math.log(distance / exact_count) / scale_log * (half_count - exact_count)) < target:
            distance += 1
        thresholds.append(distance)
    return thresholds
def bucket_of(relative):
    distance=jnp.abs(relative)
    exact=BUCKETS//4
    beyond=jnp.full_like(distance,exact)
    for t in bucket_limits():
        beyond=beyond+jnp.where(distance>=t,1,0)
    inside=jnp.where(distance<exact,distance,beyond)
    return inside+jnp.where(relative>0,BUCKETS//2,0)

def bias_kernel(tT_ref, out_ref, ext_ref):
    h=pl.program_id(0)
    @pl.when(h==0)
    def _():
        t=lax.broadcasted_iota(jnp.int32,(1,2*BLOCK),1)
        rel=-jnp.where(t<BLOCK,t,t-2*BLOCK)
        b=bucket_of(rel)
        acc=jnp.zeros((HEADS,2*BLOCK),F32)
        for c in range(BUCKETS):
            acc=jnp.where(b==c,tT_ref[:,c:c+1],acc)
        ext_ref[...]=acc
    row=ext_ref[pl.ds(h,1),:]
    for s in range(4):
        x=jnp.broadcast_to(row,(128,2*BLOCK))
        y=pltpu.roll(x,128*s,axis=1,stride=1,stride_axis=0)
        out_ref[0,pl.ds(128*s,128),:]=y[:,:BLOCK]
def bias_call(table):
    return pl.pallas_call(bias_kernel,grid=(HEADS,),
        in_specs=[pl.BlockSpec((HEADS,BUCKETS),lambda h:(0,0))],
        out_specs=pl.BlockSpec((1,BLOCK,BLOCK),lambda h:(h,0,0)),
        out_shape=jax.ShapeDtypeStruct((HEADS,BLOCK,BLOCK),F32),
        scratch_shapes=[pltpu.VMEM((HEADS,2*BLOCK),F32)],name="bias")(table.T)

def seg_ids(flag):
    s=lax.broadcasted_iota(jnp.int32,(1,BLOCK),1)
    long_ids=jnp.where(s>=LONG,1,0)
    short_ids=jnp.where(s>=SHORT,1,0)+jnp.where(s>=2*SHORT,1,0)
    return jnp.where(flag==1,long_ids,short_ids)
def masks(flag):
    seg=seg_ids(flag)
    c=lax.broadcasted_iota(jnp.int32,(HEAD_DIM,BLOCK),0)
    qm=jnp.where(seg==c,1.0,0.0).astype(BF16)
    km=jnp.where((seg!=c)&(c<3),far,0.0).astype(BF16)
    return qm,km

def fwd_kernel(flags_ref,q_ref,k_ref,v_ref,bias_ref,o_ref,lse_ref,*,CH):
    n=pl.program_id(1)
    qm,km=masks(flags_ref[n])
    qa=jnp.concatenate([q_ref[...],qm],0)
    ka=jnp.concatenate([k_ref[...],km],0).T
    vT=v_ref[...]
    for c in range(BLOCK//CH):
        sl=slice(c*CH,(c+1)*CH)
        s=dot(ka,qa[:,sl])+bias_ref[0,:,sl]
        m=jnp.max(s,axis=0,keepdims=True)
        e=jnp.exp(s-m)
        l=jnp.sum(e,axis=0,keepdims=True)
        p=(e*(1.0/l)).astype(BF16)
        o_ref[:,sl]=dot(vT,p).astype(BF16)
        lse_ref[0,:,sl]=m+jnp.log(l)
def fwd_call(flags,qkvT,bias,CH=256):
    T=qkvT.shape[1]; n=T//BLOCK
    sp=lambda off: pl.BlockSpec((HEAD_DIM,BLOCK),lambda h,n,f:(h+off,n))
    return pl.pallas_call(functools.partial(fwd_kernel,CH=CH),
        grid_spec=pltpu.PrefetchScalarGridSpec(num_scalar_prefetch=1,grid=(HEADS,n),
        in_specs=[sp(0),sp(HEADS),sp(2*HEADS),pl.BlockSpec((1,BLOCK,BLOCK),lambda h,n,f:(h,0,0))],
        out_specs=[pl.BlockSpec((HEAD_DIM,BLOCK),lambda h,n,f:(h,n)),pl.BlockSpec((1,1,BLOCK),lambda h,n,f:(h,0,n))]),
        out_shape=[jax.ShapeDtypeStruct((HEADS*HEAD_DIM,T),BF16),jax.ShapeDtypeStruct((HEADS,1,T),F32)],
        name="attend",
        compiler_params=pltpu.CompilerParams(vmem_limit_bytes=48*2**20))(flags,qkvT,qkvT,qkvT,bias)

def bwd_kernel(flags_ref,q_ref,k_ref,v_ref,do_ref,lse_ref,bias_ref,dq_ref,dk_ref,dv_ref,tab_ref,acc_ref,*,CH,nb):
    n=pl.program_id(1)
    qm,km=masks(flags_ref[n])
    q=q_ref[...]; kT=k_ref[...]; doT=do_ref[...]
    qa=jnp.concatenate([q,qm],0)
    ka=jnp.concatenate([kT,km],0).T
    v=v_ref[...].T
    @pl.when(n==0)
    def _(): acc_ref[...]=jnp.zeros_like(acc_ref)
    dk=None; dv=None
    for c in range(BLOCK//CH):
        sl=slice(c*CH,(c+1)*CH)
        s=dot(ka,qa[:,sl])+bias_ref[0,:,sl]
        p=jnp.exp(s-lse_ref[0,:,sl])
        pb=p.astype(BF16)
        dvc=dot(doT[:,sl],pb,NT)
        dp=dot(v,doT[:,sl])
        t=p*dp
        d=jnp.sum(t,axis=0,keepdims=True)
        ds=(t-p*d).astype(BF16)
        dq_ref[:,sl]=dot(kT,ds).astype(BF16)
        dkc=dot(q[:,sl],ds,NT)
        dk=dkc if dk is None else dk+dkc
        dv=dvc if dv is None else dv+dvc
        acc_ref[:,sl]+=ds.astype(F32)
    dk_ref[...]=dk.astype(BF16); dv_ref[...]=dv.astype(BF16)
    @pl.when(n==nb-1)
    def _():
        tot=None
        zero=jnp.zeros((128,BLOCK),F32)
        for g in range(4):
            x=jnp.concatenate([acc_ref[pl.ds(128*g,128),:],zero],1)
            y=pltpu.roll(x,(2*BLOCK-128*g)%(2*BLOCK),axis=1,stride=2*BLOCK-1,stride_axis=0)
            r=jnp.sum(y,axis=0,keepdims=True)
            tot=r if tot is None else tot+r
        t=lax.broadcasted_iota(jnp.int32,(1,2*BLOCK),1)
        rel=-jnp.where(t<BLOCK,t,t-2*BLOCK)
        b=bucket_of(rel)
        cc=lax.broadcasted_iota(jnp.int32,(BUCKETS,2*BLOCK),0)
        tab_ref[0]=jnp.broadcast_to(jnp.sum(jnp.where(b==cc,tot,0.0),axis=1,keepdims=True),(BUCKETS,128))
def bwd_call(flags,qkvT,doT,lse,bias,CH=256):
    T=qkvT.shape[1]; n=T//BLOCK
    sp=lambda off: pl.BlockSpec((HEAD_DIM,BLOCK),lambda h,n,f:(h+off,n))
    D=HEADS*HEAD_DIM
    return pl.pallas_call(functools.partial(bwd_kernel,CH=CH,nb=n),
        grid_spec=pltpu.PrefetchScalarGridSpec(num_scalar_prefetch=1,grid=(HEADS,n),
        in_specs=[sp(0),sp(HEADS),sp(2*HEADS),sp(0),pl.BlockSpec((1,1,BLOCK),lambda h,n,f:(h,0,n)),pl.BlockSpec((1,BLOCK,BLOCK),lambda h,n,f:(h,0,0))],
        out_specs=[sp(0),sp(0),sp(0),pl.BlockSpec((1,BUCKETS,128),lambda h,n,f:(h,0,0))],
        scratch_shapes=[pltpu.VMEM((BLOCK,BLOCK),F32)]),
        out_shape=[jax.ShapeDtypeStruct((D,T),BF16)]*3+[jax.ShapeDtypeStruct((HEADS,BUCKETS,128),F32)],
        name="attend_back",
        compiler_params=pltpu.CompilerParams(vmem_limit_bytes=48*2**20))(flags,qkvT,qkvT,qkvT,doT,lse,bias)

def fwd2_kernel(flags_ref,q_ref,k_ref,v_ref,bias_ref,o_ref,lse_ref,*,HP,mode):
    n=pl.program_id(1)
    qm,km=masks(flags_ref[n])
    S=[]
    for u in range(HP):
        r=slice(u*64,(u+1)*64)
        qa=jnp.concatenate([q_ref[r,:],qm],0)
        ka=jnp.concatenate([k_ref[r,:],km],0).T
        S.append(dot(ka,qa))
    for u in range(HP):
        r=slice(u*64,(u+1)*64)
        s=S[u]+bias_ref[u]
        m=jnp.max(s,axis=0,keepdims=True)
        e=jnp.exp(s-m)
        if mode=="def":
            l=jnp.sum(e,axis=0,keepdims=True)
            o_ref[r,:]=(dot(v_ref[r,:],e.astype(BF16))*(1.0/l)).astype(BF16)
        elif mode=="ones":
            va=jnp.concatenate([v_ref[r,:],jnp.ones((16,BLOCK),BF16)],0)
            oa=dot(va,e.astype(BF16))
            l=oa[64:65,:]
            o_ref[r,:]=(oa[:64]*(1.0/l)).astype(BF16)
        elif mode=="nomm":
            l=jnp.sum(e,axis=0,keepdims=True)
            o_ref[r,:]=e[:64].astype(BF16)
        else:
            l=jnp.sum(e,axis=0,keepdims=True)
            p=(e*(1.0/l)).astype(BF16)
            o_ref[r,:]=dot(v_ref[r,:],p).astype(BF16)
        lse_ref[u,:,:]=m+jnp.log(l)
def fwd2_call(flags,qkvT,bias,HP=2,mode="norm"):
    T=qkvT.shape[1]; n=T//BLOCK
    G=HEADS//HP
    sp=lambda off: pl.BlockSpec((HP*HEAD_DIM,BLOCK),lambda h,n,f:(h+off,n))
    return pl.pallas_call(functools.partial(fwd2_kernel,HP=HP,mode=mode),
        grid_spec=pltpu.PrefetchScalarGridSpec(num_scalar_prefetch=1,grid=(G,n),
        in_specs=[sp(0),sp(G),sp(2*G),pl.BlockSpec((HP,BLOCK,BLOCK),lambda h,n,f:(h,0,0))],
        out_specs=[pl.BlockSpec((HP*HEAD_DIM,BLOCK),lambda h,n,f:(h,n)),pl.BlockSpec((HP,1,BLOCK),lambda h,n,f:(h,0,n))]),
        out_shape=[jax.ShapeDtypeStruct((HEADS*HEAD_DIM,T),BF16),jax.ShapeDtypeStruct((HEADS,1,T),F32)],
        name="attend",
        compiler_params=pltpu.CompilerParams(vmem_limit_bytes=56*2**20))(flags,qkvT,qkvT,qkvT,bias)
def fwdN_kernel(flags_ref,q_ref,k_ref,v_ref,bias_ref,o_ref,lse_ref,*,HP):
    n=pl.program_id(1)
    qm,km=masks(flags_ref[n])
    for u in range(HP):
        r=slice(u*64,(u+1)*64)
        qa=jnp.concatenate([q_ref[r,:],qm],0)
        ka=jnp.concatenate([k_ref[r,:],km],0).T
        s=dot(ka,qa)+bias_ref[u]
        m=jnp.max(s,axis=0,keepdims=True)
        e=jnp.exp(s-m)
        l=jnp.sum(e,axis=0,keepdims=True)
        o=lax.dot_general(e.astype(BF16),v_ref[r,:],(((0,),(1,)),((),())),preferred_element_type=F32)
        o_ref[r,:]=(o.T*(1.0/l)).astype(BF16)
        lse_ref[u,:,:]=m+jnp.log(l)

def left_by_row(x,width):
    row=lax.broadcasted_iota(jnp.int32,x.shape,0)
    for b in range(7):
        y=pltpu.roll(x,width-(1<<b),axis=1)
        x=jnp.where((row>>b)&1==1,y,x)
    return x
def bwd2_kernel(flags_ref,q_ref,k_ref,v_ref,do_ref,lse_ref,bias_ref,dq_ref,dk_ref,dv_ref,tab_ref,band_ref,far_ref,*,HP,nb,tabmode):
    n=pl.program_id(1)
    qm,km=masks(flags_ref[n])
    @pl.when(n==0)
    def _():
        band_ref[...]=jnp.zeros_like(band_ref); far_ref[...]=jnp.zeros_like(far_ref)
    R=[slice(u*64,(u+1)*64) for u in range(HP)]
    S=[];DP=[]
    for u in range(HP):
        r=R[u]
        qa=jnp.concatenate([q_ref[r,:],qm],0)
        ka=jnp.concatenate([k_ref[r,:],km],0).T
        S.append(dot(ka,qa))
        DP.append(dot(v_ref[r,:].T,do_ref[r,:]))
    for u in range(HP):
        r=R[u]
        p=jnp.exp(S[u]+bias_ref[u]-lse_ref[u])
        pb=p.astype(BF16)
        dv_ref[r,:]=dot(do_ref[r,:],pb,NT).astype(BF16)
        t=p*DP[u]
        d=jnp.sum(t,axis=0,keepdims=True)
        dsf=t-p*d
        ds=dsf.astype(BF16)
        dq_ref[r,:]=dot(k_ref[r,:],ds).astype(BF16)
        dk_ref[r,:]=dot(q_ref[r,:],ds,NT).astype(BF16)
        if tabmode:
            lo=None;hi=None;bl=[None]*3
            for g in range(4):
                for c in range(4):
                    tile=dsf[128*g:128*(g+1),128*c:128*(c+1)]
                    w=c-g+1
                    if 0<=w<3:
                        bl[w]=tile if bl[w] is None else bl[w]+tile
                    elif w<0:
                        lo=tile if lo is None else lo+tile
                    else:
                        hi=tile if hi is None else hi+tile
            for w in range(3): band_ref[u,:,128*w:128*(w+1)]+=bl[w]
            far_ref[u,0]+=jnp.sum(lo.reshape(16,8,128),axis=0)
            far_ref[u,1]+=jnp.sum(hi.reshape(16,8,128),axis=0)
    @pl.when(n==nb-1)
    def _():
        t=lax.broadcasted_iota(jnp.int32,(1,BLOCK),1)
        b=bucket_of(-jnp.where(t<384,t-128,t-640))
        cc=lax.broadcasted_iota(jnp.int32,(BUCKETS,BLOCK),0)
        c1=lax.broadcasted_iota(jnp.int32,(BUCKETS,128),0)
        for u in range(HP):
            x=jnp.concatenate([band_ref[u],jnp.zeros((128,128),F32)],1)
            tot=jnp.sum(left_by_row(x,BLOCK),axis=0,keepdims=True)
            lo=jnp.sum(far_ref[u,0],axis=0,keepdims=True); hi=jnp.sum(far_ref[u,1],axis=0,keepdims=True)
            val=jnp.where(b==cc,tot,0.0)
            val=val[:,:128]+val[:,128:256]+val[:,256:384]+val[:,384:]
            val=val+jnp.where(c1==BUCKETS-1,lo,0.0)+jnp.where(c1==BUCKETS//2-1,hi,0.0)
            tab_ref[u]=jnp.broadcast_to(jnp.sum(val,axis=1,keepdims=True),(BUCKETS,128))
def bwd2_call(flags,qkvT,doT,lse,bias,HP=2,tabmode=1):
    T=qkvT.shape[1]; n=T//BLOCK; G=HEADS//HP
    sp=lambda off: pl.BlockSpec((HP*HEAD_DIM,BLOCK),lambda h,n,f:(h+off,n))
    D=HEADS*HEAD_DIM
    return pl.pallas_call(functools.partial(bwd2_kernel,HP=HP,nb=n,tabmode=tabmode),
        grid_spec=pltpu.PrefetchScalarGridSpec(num_scalar_prefetch=1,grid=(G,n),
        in_specs=[sp(0),sp(G),sp(2*G),sp(0),pl.BlockSpec((HP,1,BLOCK),lambda h,n,f:(h,0,n)),pl.BlockSpec((HP,BLOCK,BLOCK),lambda h,n,f:(h,0,0))],
        out_specs=[sp(0),sp(0),sp(0),pl.BlockSpec((HP,BUCKETS,128),lambda h,n,f:(h,0,0))],
        scratch_shapes=[pltpu.VMEM((HP,128,384),F32),pltpu.VMEM((HP,2,8,128),F32)]),
        out_shape=[jax.ShapeDtypeStruct((D,T),BF16)]*3+[jax.ShapeDtypeStruct((HEADS,BUCKETS,128),F32)],
        name="attend_back",
        compiler_params=pltpu.CompilerParams(vmem_limit_bytes=60*2**20))(flags,qkvT,qkvT,qkvT,doT,lse,bias)

D=768
norm_eps=1e-6
def rms(x): return lax.rsqrt(jnp.mean(x*x,axis=-1,keepdims=True)+norm_eps)
GA=128
def row_of(gains,which):
    return gains.astype(F32).T[which:which+1,:]
def qkv_kernel(x_ref,w_ref,aT_ref,qkvT_ref,wT_ref):
    @pl.when(pl.program_id(0)==0)
    def _():
        for c in range(3):
            wT_ref[pl.ds(c*D,D),:]=w_ref[:,c*D:(c+1)*D].T
    x=x_ref[...].astype(F32)
    g=row_of(w_ref[:,3*D:3*D+GA],0)
    a=(x*rms(x)*g).astype(BF16)
    aT=a.T
    aT_ref[...]=aT
    qkvT_ref[...]=dot(wT_ref[...],aT).astype(BF16)
def qkv_call(x,w):
    T=x.shape[0]
    return pl.pallas_call(qkv_kernel,grid=(T//BLOCK,),
        in_specs=[pl.BlockSpec((BLOCK,D),lambda t:(t,0)),pl.BlockSpec(w.shape,lambda t:(0,0),pipeline_mode=pl.Buffered(1))],
        out_specs=[pl.BlockSpec((D,BLOCK),lambda t:(0,t)),pl.BlockSpec((3*D,BLOCK),lambda t:(0,t))],
        out_shape=[jax.ShapeDtypeStruct((D,T),BF16),jax.ShapeDtypeStruct((3*D,T),BF16)],
        scratch_shapes=[pltpu.VMEM((3*D,D),BF16)],name="project",
        compiler_params=pltpu.CompilerParams(vmem_limit_bytes=56*2**20))(x,w)
def mid_kernel(x_ref,oT_ref,wo_ref,ga_ref,m_ref,b_ref,bT_ref,*_):
    o=oT_ref[...].T
    m=x_ref[...].astype(F32)+dot(o,wo_ref[...],NT)
    m_ref[...]=m
    b=(m*rms(m)*row_of(ga_ref[...],1)).astype(BF16)
    b_ref[...]=b
    bT_ref[0]=b.T
def mid_call(x,oT,woT,gains):
    T=x.shape[0]
    return pl.pallas_call(mid_kernel,grid=(T//BLOCK,),
        in_specs=[pl.BlockSpec((BLOCK,D),lambda t:(t,0)),pl.BlockSpec((D,BLOCK),lambda t:(0,t)),
                  pl.BlockSpec((D,D),lambda t:(0,woT[1])),pl.BlockSpec((D,GA),lambda t:(0,gains[1]))],
        out_specs=[pl.BlockSpec((BLOCK,D),lambda t:(t,0)),pl.BlockSpec((BLOCK,D),lambda t:(t,0)),pl.BlockSpec((1,D,BLOCK),lambda t:(t,0,0))],
        out_shape=[jax.ShapeDtypeStruct((T,D),F32),jax.ShapeDtypeStruct((T,D),BF16),jax.ShapeDtypeStruct((T//BLOCK,D,BLOCK),BF16)],
        name="middle",
        compiler_params=pltpu.CompilerParams(vmem_limit_bytes=48*2**20))(x,oT,woT[0],gains[0])
def gate(u,mode):
    if mode=="erf":
        P=0.5*(1.0+lax.erf(u*(0.5**0.5)))
        z=jnp.exp(-0.5*u*u)
    else:
        z=jnp.exp(-0.5*u*u)
        t=1.0/(1.0+(0.3275911*0.5**0.5)*jnp.abs(u))
        q=((((0.5*1.061405429*t-0.5*1.453152027)*t+0.5*1.421413741)*t-0.5*0.284496736)*t+0.5*0.254829592)*t*z
        P=jnp.where(u>=0,1.0-q,q)
    return u*P, P+u*z*(2*math.pi)**-0.5
def ffn_kernel(b_ref,bT_ref,dy_ref,m_ref,win_ref,wout_ref,out_ref,db_ref,dwin_ref,dwout_ref,
               oacc,dacc,dyT,ain,aout,*,FC,SUB,nc,nt,mode,TB,order):
    c=pl.program_id(0); t=pl.program_id(1)
    rows=pl.ds(t*TB,TB)
    @pl.when(c==0)
    def _():
        oacc[rows,:]=m_ref[...]
        dacc[rows,:]=jnp.zeros((TB,D),F32)
        dyT[t]=dy_ref[rows,:].T
    b=b_ref[rows,:]; dy=dy_ref[rows,:]
    G=[];DU=[]
    U=[dot(b,win_ref[:,s*SUB:(s+1)*SUB]) for s in range(FC//SUB)]
    DG=[dot(dy,wout_ref[:,s*SUB:(s+1)*SUB]) for s in range(FC//SUB)]
    @pl.when(t==0)
    def _():
        ain[...]=jnp.zeros_like(ain); aout[...]=jnp.zeros_like(aout)
    for s in range(FC//SUB):
        g,pull=gate(U[s],mode)
        g=g.astype(BF16)
        du=(DG[s]*pull).astype(BF16)
        sl=slice(s*SUB,(s+1)*SUB)
        aout[:,sl]+=dot(dyT[t],g)
        ain[:,sl]+=dot(bT_ref[t],du)
        G.append(g);DU.append(du)
    g=jnp.concatenate(G,1);du=jnp.concatenate(DU,1)
    oacc[rows,:]+=dot(g,wout_ref[...],NT)
    dacc[rows,:]+=dot(du,win_ref[...],NT)
    @pl.when(t==nt-1)
    def _():
        dwin_ref[...]=ain[...].astype(BF16)
        dwout_ref[...]=aout[...].astype(BF16)
    @pl.when(c==nc-1)
    def _():
        out_ref[...]=oacc[rows,:].astype(BF16)
        db_ref[...]=dacc[rows,:]
def ffn_call(b,bT,dy,m,win,wout,FC=768,SUB=256,mode="erf",TB=512,order=0):
    T=b.shape[0]; nt=T//TB; FF=3072; nc=FF//FC
    bT3=bT
    last=lambda c,t:(jnp.where(c==nc-1,t,0),0)
    first=lambda c,t:(jnp.where(c==0,t,nt-1),0)
    one=pl.Buffered(1)
    return pl.pallas_call(functools.partial(ffn_kernel,FC=FC,SUB=SUB,nc=nc,nt=nt,mode=mode,TB=TB,order=order),grid=(nc,nt),
        in_specs=[pl.BlockSpec((T,D),lambda c,t:(0,0),pipeline_mode=one),pl.BlockSpec((nt,D,TB),lambda c,t:(0,0,0),pipeline_mode=one),
            pl.BlockSpec((T,D),lambda c,t:(0,0),pipeline_mode=one),
            pl.BlockSpec((TB,D),first),pl.BlockSpec((D,FC),lambda c,t:(0,c+win[1]*D//FC)),pl.BlockSpec((D,FC),lambda c,t:(0,c+wout[1]*D//FC))],
        out_specs=[pl.BlockSpec((TB,D),last),pl.BlockSpec((TB,D),last),pl.BlockSpec((D,FC),lambda c,t:(0,c)),pl.BlockSpec((D,FC),lambda c,t:(0,c))],
        out_shape=[jax.ShapeDtypeStruct((T,D),BF16),jax.ShapeDtypeStruct((T,D),F32),jax.ShapeDtypeStruct((D,FF),BF16),jax.ShapeDtypeStruct((D,FF),BF16)],
        scratch_shapes=[pltpu.VMEM((T,D),F32),pltpu.VMEM((T,D),F32),pltpu.VMEM((nt,D,TB),BF16),pltpu.VMEM((D,FC),F32),pltpu.VMEM((D,FC),F32)],
        name="feed_forward",
        compiler_params=pltpu.CompilerParams(vmem_limit_bytes=62*2**20))(b,bT3,dy,m,win[0],wout[0])

def post_kernel(dy_ref,db_ref,m_ref,oT_ref,wo_ref,ga_ref,dm_ref,doT_ref,dwo_ref,dg_ref,acc_ref,*,nt):
    t=pl.program_id(0)
    @pl.when(t==0)
    def _():
        acc_ref[...]=jnp.zeros_like(acc_ref); dg_ref[...]=jnp.zeros_like(dg_ref)
    m=m_ref[...]; db=db_ref[...]
    r=rms(m); n2=m*r
    dn=db*row_of(ga_ref[...],1)
    dg_ref[...]+=jnp.sum(db*n2,axis=0,keepdims=True)
    dm=dy_ref[...].astype(F32)+r*(dn-n2*jnp.mean(dn*n2,axis=-1,keepdims=True))
    dm_ref[...]=dm
    dmb=dm.astype(BF16)
    acc_ref[...]+=dot(dmb.T,oT_ref[...],NT)
    doT_ref[...]=dot(dmb,wo_ref[...]).astype(BF16).T
    @pl.when(t==nt-1)
    def _(): dwo_ref[...]=acc_ref[...].astype(BF16)
def post_call(dy,db,m,oT,woT,gains):
    T=dy.shape[0]; nt=T//BLOCK
    row=pl.BlockSpec((BLOCK,D),lambda t:(t,0)); col=pl.BlockSpec((D,BLOCK),lambda t:(0,t))
    return pl.pallas_call(functools.partial(post_kernel,nt=nt),grid=(nt,),
        in_specs=[row,row,row,col,pl.BlockSpec((D,D),lambda t:(0,woT[1])),pl.BlockSpec((D,GA),lambda t:(0,gains[1]))],
        out_specs=[row,col,pl.BlockSpec((D,D),lambda t:(0,0)),pl.BlockSpec((1,D),lambda t:(0,0))],
        out_shape=[jax.ShapeDtypeStruct((T,D),F32),jax.ShapeDtypeStruct((D,T),BF16),jax.ShapeDtypeStruct((D,D),BF16),jax.ShapeDtypeStruct((1,D),F32)],
        scratch_shapes=[pltpu.VMEM((D,D),F32)],name="middle_back",
        compiler_params=pltpu.CompilerParams(vmem_limit_bytes=48*2**20))(dy,db,m,oT,woT[0],gains[0])
def last_kernel(x_ref,dm_ref,aT_ref,dq_ref,dk_ref,dv_ref,w_ref,dx_ref,dw_ref,dg_ref,acc_ref,*,nt):
    t=pl.program_id(0)
    @pl.when(t==0)
    def _():
        acc_ref[...]=jnp.zeros_like(acc_ref); dg_ref[...]=jnp.zeros_like(dg_ref)
    aT=aT_ref[...]
    da=None
    for c,ref in enumerate((dq_ref,dk_ref,dv_ref)):
        y=ref[...]
        sl=slice(c*D,(c+1)*D)
        acc_ref[:,sl]+=dot(aT,y,NT)
        z=dot(w_ref[:,sl],y)
        da=z if da is None else da+z
    da=da.T
    x=x_ref[...].astype(F32)
    r=rms(x); n1=x*r
    dn=da*row_of(w_ref[:,3*D:3*D+GA],0)
    dg_ref[...]+=jnp.sum(da*n1,axis=0,keepdims=True)
    dx_ref[...]=(dm_ref[...]+r*(dn-n1*jnp.mean(dn*n1,axis=-1,keepdims=True))).astype(BF16)
    @pl.when(t==nt-1)
    def _(): dw_ref[...]=acc_ref[...].astype(BF16)
def last_call(x,dm,aT,dqT,dkT,dvT,w):
    T=x.shape[0]; nt=T//BLOCK
    row=pl.BlockSpec((BLOCK,D),lambda t:(t,0)); col=pl.BlockSpec((D,BLOCK),lambda t:(0,t))
    return pl.pallas_call(functools.partial(last_kernel,nt=nt),grid=(nt,),
        in_specs=[row,row,col,col,col,col,pl.BlockSpec(w.shape,lambda t:(0,0),pipeline_mode=pl.Buffered(1))],
        out_specs=[row,pl.BlockSpec((D,3*D),lambda t:(0,0)),pl.BlockSpec((1,D),lambda t:(0,0))],
        out_shape=[jax.ShapeDtypeStruct((T,D),BF16),jax.ShapeDtypeStruct((D,3*D),BF16),jax.ShapeDtypeStruct((1,D),F32)],
        scratch_shapes=[pltpu.VMEM((D,3*D),F32)],name="project_back",
        compiler_params=pltpu.CompilerParams(vmem_limit_bytes=56*2**20))(x,dm,aT,dqT,dkT,dvT,w)

BOTH=("dp","fsdp")
def body(hidden,long_flags,norm1_gain,query_w,key_w,value_w,out_w,bias_table,norm2_gain,ffn_in,ffn_out,out_grad):
    rows=norm1_gain.shape[0]
    gains=jnp.concatenate([norm1_gain[:,None],norm2_gain[:,None],jnp.zeros((rows,GA-2),F32)],1)
    pa=jnp.concatenate([query_w,key_w,value_w,gains],1).astype(BF16)
    pb=jnp.concatenate([out_w.T,ffn_in,ffn_out.T],1).astype(BF16)
    wa=lax.all_gather(pa,BOTH,axis=0,tiled=True)
    wb=lax.all_gather(pb,BOTH,axis=0,tiled=True)
    bias=bias_call(bias_table)
    aT,qkvT=qkv_call(hidden,wa)
    oT,lse=fwd2_call(long_flags,qkvT,bias,HP=4,mode="norm")
    GB=3*D//GA
    m,b,bT=mid_call(hidden,oT,(wb,0),(wa,GB))
    out,db,dwin,dwoutT=ffn_call(b,bT,out_grad,m,(wb,1),(wb,5))
    dm,doT,dwoT,dg2=post_call(out_grad,db,m,oT,(wb,0),(wa,GB))
    dqT,dkT,dvT,tab=bwd2_call(long_flags,qkvT,doT,lse,bias,HP=4)
    dx,dwqkv,dg1=last_call(hidden,dm,aT,dqT,dkT,dvT,wa)
    ndev=D//rows
    def rs(x): return lax.psum_scatter(x,BOTH,scatter_dimension=0,tiled=True)
    fsum=rs(jnp.concatenate([dwoT,dwin,dwoutT],1)).astype(F32)
    tabv=tab[:,:,0].T
    ex=jnp.concatenate([dg1.T,dg2.T],1)
    tb=jnp.tile(tabv.reshape(rows,-1),(ndev,1))
    pad=jnp.zeros((D,GA-2-tb.shape[1]%GA),F32)
    asum=rs(jnp.concatenate([dwqkv,jnp.concatenate([ex,tb,pad],1).astype(BF16)],1)).astype(F32)
    table=asum[:,3*D+2:3*D+2+tb.shape[1]].reshape(BUCKETS,HEADS)
    return (out,dx,asum[:,3*D],asum[:,:D],asum[:,D:2*D],asum[:,2*D:3*D],fsum[:,:D].T,table,asum[:,3*D+1],fsum[:,D:D+3072],fsum[:,D+3072:].T)

def solution(mesh):
    P=jax.sharding.PartitionSpec
    r=P(BOTH,None); v=P(BOTH); c=P(None,BOTH)
    return jax.shard_map(body,mesh=mesh,in_specs=(r,v,v,r,r,r,c,P(),v,r,c,r),out_specs=(r,r,v,r,r,r,c,P(),v,r,c),check_vma=False)
```

```python
import math, functools
import jax, jax.numpy as jnp
from jax import lax
from jax.experimental import pallas as pl
from jax.experimental.pallas import tpu as pltpu
HEADS=12; HEAD_DIM=64; BUCKETS=32; MAX_DIST=128; BLOCK=512; LONG=500; SHORT=250
F32=jnp.float32; BF16=jnp.bfloat16
far=-2.0**30
NN=(((1,),(0,)),((),())); NT=(((1,),(1,)),((),())); TN=(((0,),(0,)),((),()))
def dot(a,b,dn=NN): return lax.dot_general(a,b,dn,preferred_element_type=F32)

def bucket_limits():
    exact_count = BUCKETS // 4
    half_count = BUCKETS // 2
    scale_log = math.log(MAX_DIST / exact_count)
    thresholds = []
    for target in range(1, half_count - exact_count):
        distance = exact_count
        while int(math.log(distance / exact_count) / scale_log * (half_count - exact_count)) < target:
            distance += 1
        thresholds.append(distance)
    return thresholds
def bucket_of(relative):
    distance=jnp.abs(relative)
    exact=BUCKETS//4
    beyond=jnp.full_like(distance,exact)
    for t in bucket_limits():
        beyond=beyond+jnp.where(distance>=t,1,0)
    inside=jnp.where(distance<exact,distance,beyond)
    return inside+jnp.where(relative>0,BUCKETS//2,0)

def bias_kernel(tT_ref, out_ref, ext_ref):
    h=pl.program_id(0)
    @pl.when(h==0)
    def _():
        t=lax.broadcasted_iota(jnp.int32,(1,2*BLOCK),1)
        rel=-jnp.where(t<BLOCK,t,t-2*BLOCK)
        b=bucket_of(rel)
        acc=jnp.zeros((HEADS,2*BLOCK),F32)
        for c in range(BUCKETS):
            acc=jnp.where(b==c,tT_ref[:,c:c+1],acc)
        ext_ref[...]=acc
    row=ext_ref[pl.ds(h,1),:]
    for s in range(4):
        x=jnp.broadcast_to(row,(128,2*BLOCK))
        y=pltpu.roll(x,128*s,axis=1,stride=1,stride_axis=0)
        out_ref[0,pl.ds(128*s,128),:]=y[:,:BLOCK]
def bias_call(table):
    return pl.pallas_call(bias_kernel,grid=(HEADS,),
        in_specs=[pl.BlockSpec((HEADS,BUCKETS),lambda h:(0,0))],
        out_specs=pl.BlockSpec((1,BLOCK,BLOCK),lambda h:(h,0,0)),
        out_shape=jax.ShapeDtypeStruct((HEADS,BLOCK,BLOCK),F32),
        scratch_shapes=[pltpu.VMEM((HEADS,2*BLOCK),F32)],name="bias")(table.T)

def seg_ids(flag):
    s=lax.broadcasted_iota(jnp.int32,(1,BLOCK),1)
    long_ids=jnp.where(s>=LONG,1,0)
    short_ids=jnp.where(s>=SHORT,1,0)+jnp.where(s>=2*SHORT,1,0)
    return jnp.where(flag==1,long_ids,short_ids)
def masks(flag):
    seg=seg_ids(flag)
    c=lax.broadcasted_iota(jnp.int32,(HEAD_DIM,BLOCK),0)
    qm=jnp.where(seg==c,1.0,0.0).astype(BF16)
    km=jnp.where((seg!=c)&(c<3),far,0.0).astype(BF16)
    return qm,km

def fwd_kernel(flags_ref,q_ref,k_ref,v_ref,bias_ref,o_ref,lse_ref,*,CH):
    n=pl.program_id(1)
    qm,km=masks(flags_ref[n])
    qa=jnp.concatenate([q_ref[...],qm],0)
    ka=jnp.concatenate([k_ref[...],km],0).T
    vT=v_ref[...]
    for c in range(BLOCK//CH):
        sl=slice(c*CH,(c+1)*CH)
        s=dot(ka,qa[:,sl])+bias_ref[0,:,sl]
        m=jnp.max(s,axis=0,keepdims=True)
        e=jnp.exp(s-m)
        l=jnp.sum(e,axis=0,keepdims=True)
        p=(e*(1.0/l)).astype(BF16)
        o_ref[:,sl]=dot(vT,p).astype(BF16)
        lse_ref[0,:,sl]=m+jnp.log(l)
def fwd_call(flags,qkvT,bias,CH=256):
    T=qkvT.shape[1]; n=T//BLOCK
    sp=lambda off: pl.BlockSpec((HEAD_DIM,BLOCK),lambda h,n,f:(h+off,n))
    return pl.pallas_call(functools.partial(fwd_kernel,CH=CH),
        grid_spec=pltpu.PrefetchScalarGridSpec(num_scalar_prefetch=1,grid=(HEADS,n),
        in_specs=[sp(0),sp(HEADS),sp(2*HEADS),pl.BlockSpec((1,BLOCK,BLOCK),lambda h,n,f:(h,0,0))],
        out_specs=[pl.BlockSpec((HEAD_DIM,BLOCK),lambda h,n,f:(h,n)),pl.BlockSpec((1,1,BLOCK),lambda h,n,f:(h,0,n))]),
        out_shape=[jax.ShapeDtypeStruct((HEADS*HEAD_DIM,T),BF16),jax.ShapeDtypeStruct((HEADS,1,T),F32)],
        name="attend",
        compiler_params=pltpu.CompilerParams(vmem_limit_bytes=48*2**20))(flags,qkvT,qkvT,qkvT,bias)

def bwd_kernel(flags_ref,q_ref,k_ref,v_ref,do_ref,lse_ref,bias_ref,dq_ref,dk_ref,dv_ref,tab_ref,acc_ref,*,CH,nb):
    n=pl.program_id(1)
    qm,km=masks(flags_ref[n])
    q=q_ref[...]; kT=k_ref[...]; doT=do_ref[...]
    qa=jnp.concatenate([q,qm],0)
    ka=jnp.concatenate([kT,km],0).T
    v=v_ref[...].T
    @pl.when(n==0)
    def _(): acc_ref[...]=jnp.zeros_like(acc_ref)
    dk=None; dv=None
    for c in range(BLOCK//CH):
        sl=slice(c*CH,(c+1)*CH)
        s=dot(ka,qa[:,sl])+bias_ref[0,:,sl]
        p=jnp.exp(s-lse_ref[0,:,sl])
        pb=p.astype(BF16)
        dvc=dot(doT[:,sl],pb,NT)
        dp=dot(v,doT[:,sl])
        t=p*dp
        d=jnp.sum(t,axis=0,keepdims=True)
        ds=(t-p*d).astype(BF16)
        dq_ref[:,sl]=dot(kT,ds).astype(BF16)
        dkc=dot(q[:,sl],ds,NT)
        dk=dkc if dk is None else dk+dkc
        dv=dvc if dv is None else dv+dvc
        acc_ref[:,sl]+=ds.astype(F32)
    dk_ref[...]=dk.astype(BF16); dv_ref[...]=dv.astype(BF16)
    @pl.when(n==nb-1)
    def _():
        tot=None
        zero=jnp.zeros((128,BLOCK),F32)
        for g in range(4):
            x=jnp.concatenate([acc_ref[pl.ds(128*g,128),:],zero],1)
            y=pltpu.roll(x,(2*BLOCK-128*g)%(2*BLOCK),axis=1,stride=2*BLOCK-1,stride_axis=0)
            r=jnp.sum(y,axis=0,keepdims=True)
            tot=r if tot is None else tot+r
        t=lax.broadcasted_iota(jnp.int32,(1,2*BLOCK),1)
        rel=-jnp.where(t<BLOCK,t,t-2*BLOCK)
        b=bucket_of(rel)
        cc=lax.broadcasted_iota(jnp.int32,(BUCKETS,2*BLOCK),0)
        tab_ref[0]=jnp.broadcast_to(jnp.sum(jnp.where(b==cc,tot,0.0),axis=1,keepdims=True),(BUCKETS,128))
def bwd_call(flags,qkvT,doT,lse,bias,CH=256):
    T=qkvT.shape[1]; n=T//BLOCK
    sp=lambda off: pl.BlockSpec((HEAD_DIM,BLOCK),lambda h,n,f:(h+off,n))
    D=HEADS*HEAD_DIM
    return pl.pallas_call(functools.partial(bwd_kernel,CH=CH,nb=n),
        grid_spec=pltpu.PrefetchScalarGridSpec(num_scalar_prefetch=1,grid=(HEADS,n),
        in_specs=[sp(0),sp(HEADS),sp(2*HEADS),sp(0),pl.BlockSpec((1,1,BLOCK),lambda h,n,f:(h,0,n)),pl.BlockSpec((1,BLOCK,BLOCK),lambda h,n,f:(h,0,0))],
        out_specs=[sp(0),sp(0),sp(0),pl.BlockSpec((1,BUCKETS,128),lambda h,n,f:(h,0,0))],
        scratch_shapes=[pltpu.VMEM((BLOCK,BLOCK),F32)]),
        out_shape=[jax.ShapeDtypeStruct((D,T),BF16)]*3+[jax.ShapeDtypeStruct((HEADS,BUCKETS,128),F32)],
        name="attend_back",
        compiler_params=pltpu.CompilerParams(vmem_limit_bytes=48*2**20))(flags,qkvT,qkvT,qkvT,doT,lse,bias)

def fwd2_kernel(flags_ref,q_ref,k_ref,v_ref,bias_ref,o_ref,lse_ref,*,HP,mode):
    n=pl.program_id(1)
    qm,km=masks(flags_ref[n])
    S=[]
    for u in range(HP):
        r=slice(u*64,(u+1)*64)
        qa=jnp.concatenate([q_ref[r,:],qm],0)
        ka=jnp.concatenate([k_ref[r,:],km],0).T
        S.append(dot(ka,qa))
    for u in range(HP):
        r=slice(u*64,(u+1)*64)
        s=S[u]+bias_ref[u]
        m=jnp.max(s,axis=0,keepdims=True)
        e=jnp.exp(s-m)
        if mode=="def":
            l=jnp.sum(e,axis=0,keepdims=True)
            o_ref[r,:]=(dot(v_ref[r,:],e.astype(BF16))*(1.0/l)).astype(BF16)
        elif mode=="ones":
            va=jnp.concatenate([v_ref[r,:],jnp.ones((16,BLOCK),BF16)],0)
            oa=dot(va,e.astype(BF16))
            l=oa[64:65,:]
            o_ref[r,:]=(oa[:64]*(1.0/l)).astype(BF16)
        elif mode=="nomm":
            l=jnp.sum(e,axis=0,keepdims=True)
            o_ref[r,:]=e[:64].astype(BF16)
        else:
            l=jnp.sum(e,axis=0,keepdims=True)
            p=(e*(1.0/l)).astype(BF16)
            o_ref[r,:]=dot(v_ref[r,:],p).astype(BF16)
        lse_ref[u,:,:]=m+jnp.log(l)
def fwd2_call(flags,qkvT,bias,HP=2,mode="norm"):
    T=qkvT.shape[1]; n=T//BLOCK
    G=HEADS//HP
    sp=lambda off: pl.BlockSpec((HP*HEAD_DIM,BLOCK),lambda h,n,f:(h+off,n))
    return pl.pallas_call(functools.partial(fwd2_kernel,HP=HP,mode=mode),
        grid_spec=pltpu.PrefetchScalarGridSpec(num_scalar_prefetch=1,grid=(G,n),
        in_specs=[sp(0),sp(G),sp(2*G),pl.BlockSpec((HP,BLOCK,BLOCK),lambda h,n,f:(h,0,0))],
        out_specs=[pl.BlockSpec((HP*HEAD_DIM,BLOCK),lambda h,n,f:(h,n)),pl.BlockSpec((HP,1,BLOCK),lambda h,n,f:(h,0,n))]),
        out_shape=[jax.ShapeDtypeStruct((HEADS*HEAD_DIM,T),BF16),jax.ShapeDtypeStruct((HEADS,1,T),F32)],
        name="attend",
        compiler_params=pltpu.CompilerParams(vmem_limit_bytes=56*2**20))(flags,qkvT,qkvT,qkvT,bias)
def fwdN_kernel(flags_ref,q_ref,k_ref,v_ref,bias_ref,o_ref,lse_ref,*,HP):
    n=pl.program_id(1)
    qm,km=masks(flags_ref[n])
    for u in range(HP):
        r=slice(u*64,(u+1)*64)
        qa=jnp.concatenate([q_ref[r,:],qm],0)
        ka=jnp.concatenate([k_ref[r,:],km],0).T
        s=dot(ka,qa)+bias_ref[u]
        m=jnp.max(s,axis=0,keepdims=True)
        e=jnp.exp(s-m)
        l=jnp.sum(e,axis=0,keepdims=True)
        o=lax.dot_general(e.astype(BF16),v_ref[r,:],(((0,),(1,)),((),())),preferred_element_type=F32)
        o_ref[r,:]=(o.T*(1.0/l)).astype(BF16)
        lse_ref[u,:,:]=m+jnp.log(l)

def left_by_row(x,width):
    row=lax.broadcasted_iota(jnp.int32,x.shape,0)
    for b in range(7):
        y=pltpu.roll(x,width-(1<<b),axis=1)
        x=jnp.where((row>>b)&1==1,y,x)
    return x
def bwd2_kernel(flags_ref,q_ref,k_ref,v_ref,do_ref,lse_ref,bias_ref,g_ref,tab_ref,band_ref,far_ref,*,HP,nb,tabmode):
    n=pl.program_id(1)
    qm,km=masks(flags_ref[n])
    @pl.when(n==0)
    def _():
        band_ref[...]=jnp.zeros_like(band_ref); far_ref[...]=jnp.zeros_like(far_ref)
    R=[slice(u*64,(u+1)*64) for u in range(HP)]
    S=[];DP=[]
    for u in range(HP):
        r=R[u]
        qa=jnp.concatenate([q_ref[r,:],qm],0)
        ka=jnp.concatenate([k_ref[r,:],km],0).T
        S.append(dot(ka,qa))
        DP.append(dot(v_ref[r,:].T,do_ref[r,:]))
    for u in range(HP):
        r=R[u]
        p=jnp.exp(S[u]+bias_ref[u]-lse_ref[u])
        pb=p.astype(BF16)
        g_ref[2,r,:]=dot(do_ref[r,:],pb,NT).astype(BF16)
        t=p*DP[u]
        d=jnp.sum(t,axis=0,keepdims=True)
        dsf=t-p*d
        ds=dsf.astype(BF16)
        g_ref[0,r,:]=dot(k_ref[r,:],ds).astype(BF16)
        g_ref[1,r,:]=dot(q_ref[r,:],ds,NT).astype(BF16)
        if tabmode:
            lo=None;hi=None;bl=[None]*3
            for g in range(4):
                for c in range(4):
                    tile=dsf[128*g:128*(g+1),128*c:128*(c+1)]
                    w=c-g+1
                    if 0<=w<3:
                        bl[w]=tile if bl[w] is None else bl[w]+tile
                    elif w<0:
                        lo=tile if lo is None else lo+tile
                    else:
                        hi=tile if hi is None else hi+tile
            for w in range(3): band_ref[u,:,128*w:128*(w+1)]+=bl[w]
            far_ref[u,0]+=jnp.sum(lo.reshape(16,8,128),axis=0)
            far_ref[u,1]+=jnp.sum(hi.reshape(16,8,128),axis=0)
    @pl.when(n==nb-1)
    def _():
        t=lax.broadcasted_iota(jnp.int32,(1,BLOCK),1)
        b=bucket_of(-jnp.where(t<384,t-128,t-640))
        cc=lax.broadcasted_iota(jnp.int32,(BUCKETS,BLOCK),0)
        c1=lax.broadcasted_iota(jnp.int32,(BUCKETS,128),0)
        for u in range(HP):
            x=jnp.concatenate([band_ref[u],jnp.zeros((128,128),F32)],1)
            tot=jnp.sum(left_by_row(x,BLOCK),axis=0,keepdims=True)
            lo=jnp.sum(far_ref[u,0],axis=0,keepdims=True); hi=jnp.sum(far_ref[u,1],axis=0,keepdims=True)
            val=jnp.where(b==cc,tot,0.0)
            val=val[:,:128]+val[:,128:256]+val[:,256:384]+val[:,384:]
            val=val+jnp.where(c1==BUCKETS-1,lo,0.0)+jnp.where(c1==BUCKETS//2-1,hi,0.0)
            col=jnp.broadcast_to(jnp.sum(val,axis=1,keepdims=True),(BUCKETS,128))
            col=jnp.concatenate([col,jnp.zeros((128-BUCKETS,128),F32)],0)
            tab_ref[u]=col.T[:8]
def bwd2_call(flags,qkvT,doT,lse,bias,HP=2,tabmode=1):
    T=qkvT.shape[1]; n=T//BLOCK; G=HEADS//HP
    sp=lambda off: pl.BlockSpec((HP*HEAD_DIM,BLOCK),lambda h,n,f:(h+off,n))
    D=HEADS*HEAD_DIM
    return pl.pallas_call(functools.partial(bwd2_kernel,HP=HP,nb=n,tabmode=tabmode),
        grid_spec=pltpu.PrefetchScalarGridSpec(num_scalar_prefetch=1,grid=(G,n),
        in_specs=[sp(0),sp(G),sp(2*G),sp(0),pl.BlockSpec((HP,1,BLOCK),lambda h,n,f:(h,0,n)),pl.BlockSpec((HP,BLOCK,BLOCK),lambda h,n,f:(h,0,0))],
        out_specs=[pl.BlockSpec((3,HP*HEAD_DIM,BLOCK),lambda h,n,f:(0,h,n)),pl.BlockSpec((HP,8,128),lambda h,n,f:(h,0,0))],
        scratch_shapes=[pltpu.VMEM((HP,128,384),F32),pltpu.VMEM((HP,2,8,128),F32)]),
        out_shape=[jax.ShapeDtypeStruct((3,D,T),BF16),jax.ShapeDtypeStruct((HEADS,8,128),F32)],
        name="attend_back",
        compiler_params=pltpu.CompilerParams(vmem_limit_bytes=60*2**20))(flags,qkvT,qkvT,qkvT,doT,lse,bias)

D=768
norm_eps=1e-6
def rms(x): return lax.rsqrt(jnp.mean(x*x,axis=-1,keepdims=True)+norm_eps)
GA=128
def row_of(gains,which):
    return gains.astype(F32).T[which:which+1,:]
def qkv_kernel(x_ref,w_ref,aT_ref,qkvT_ref,wT_ref):
    @pl.when(pl.program_id(0)==0)
    def _():
        for c in range(3):
            wT_ref[pl.ds(c*D,D),:]=w_ref[:,c*D:(c+1)*D].T
    x=x_ref[...].astype(F32)
    g=row_of(w_ref[:,3*D:3*D+GA],0)
    a=(x*rms(x)*g).astype(BF16)
    aT=a.T
    aT_ref[...]=aT
    qkvT_ref[...]=dot(wT_ref[...],aT).astype(BF16)
def qkv_call(x,w):
    T=x.shape[0]
    return pl.pallas_call(qkv_kernel,grid=(T//BLOCK,),
        in_specs=[pl.BlockSpec((BLOCK,D),lambda t:(t,0)),pl.BlockSpec(w.shape,lambda t:(0,0),pipeline_mode=pl.Buffered(1))],
        out_specs=[pl.BlockSpec((D,BLOCK),lambda t:(0,t)),pl.BlockSpec((3*D,BLOCK),lambda t:(0,t))],
        out_shape=[jax.ShapeDtypeStruct((D,T),BF16),jax.ShapeDtypeStruct((3*D,T),BF16)],
        scratch_shapes=[pltpu.VMEM((3*D,D),BF16)],name="project",
        compiler_params=pltpu.CompilerParams(vmem_limit_bytes=56*2**20))(x,w)
def mid_kernel(x_ref,oT_ref,wo_ref,ga_ref,m_ref,b_ref,bT_ref,*_):
    o=oT_ref[...].T
    m=x_ref[...].astype(F32)+dot(o,wo_ref[...],NT)
    m_ref[...]=m
    b=(m*rms(m)*row_of(ga_ref[...],1)).astype(BF16)
    b_ref[...]=b
    bT_ref[0]=b.T
def mid_call(x,oT,woT,gains):
    T=x.shape[0]
    return pl.pallas_call(mid_kernel,grid=(T//BLOCK,),
        in_specs=[pl.BlockSpec((BLOCK,D),lambda t:(t,0)),pl.BlockSpec((D,BLOCK),lambda t:(0,t)),
                  pl.BlockSpec((D,D),lambda t:(0,woT[1])),pl.BlockSpec((D,GA),lambda t:(0,gains[1]))],
        out_specs=[pl.BlockSpec((BLOCK,D),lambda t:(t,0)),pl.BlockSpec((BLOCK,D),lambda t:(t,0)),pl.BlockSpec((1,D,BLOCK),lambda t:(t,0,0))],
        out_shape=[jax.ShapeDtypeStruct((T,D),F32),jax.ShapeDtypeStruct((T,D),BF16),jax.ShapeDtypeStruct((T//BLOCK,D,BLOCK),BF16)],
        name="middle",
        compiler_params=pltpu.CompilerParams(vmem_limit_bytes=48*2**20))(x,oT,woT[0],gains[0])
def gate(u,mode):
    if mode=="erf":
        P=0.5*(1.0+lax.erf(u*(0.5**0.5)))
        z=jnp.exp(-0.5*u*u)
    else:
        z=jnp.exp(-0.5*u*u)
        t=1.0/(1.0+(0.3275911*0.5**0.5)*jnp.abs(u))
        q=((((0.5*1.061405429*t-0.5*1.453152027)*t+0.5*1.421413741)*t-0.5*0.284496736)*t+0.5*0.254829592)*t*z
        P=jnp.where(u>=0,1.0-q,q)
    return u*P, P+u*z*(2*math.pi)**-0.5
def ffn_kernel(b_ref,bT_ref,dy_ref,m_ref,win_ref,wout_ref,out_ref,db_ref,dw_ref,
               oacc,dacc,dyT,ain,aout,*,FC,SUB,nc,nt,mode,TB,order):
    c=pl.program_id(0); t=pl.program_id(1)
    rows=pl.ds(t*TB,TB)
    @pl.when(c==0)
    def _():
        oacc[rows,:]=m_ref[...]
        dacc[rows,:]=jnp.zeros((TB,D),F32)
        dyT[t]=dy_ref[rows,:].T
    b=b_ref[rows,:]; dy=dy_ref[rows,:]
    G=[];DU=[]
    U=[dot(b,win_ref[:,s*SUB:(s+1)*SUB]) for s in range(FC//SUB)]
    DG=[dot(dy,wout_ref[:,s*SUB:(s+1)*SUB]) for s in range(FC//SUB)]
    @pl.when(t==0)
    def _():
        ain[...]=jnp.zeros_like(ain); aout[...]=jnp.zeros_like(aout)
    for s in range(FC//SUB):
        g,pull=gate(U[s],mode)
        g=g.astype(BF16)
        du=(DG[s]*pull).astype(BF16)
        sl=slice(s*SUB,(s+1)*SUB)
        aout[:,sl]+=dot(dyT[t],g)
        ain[:,sl]+=dot(bT_ref[t],du)
        G.append(g);DU.append(du)
    g=jnp.concatenate(G,1);du=jnp.concatenate(DU,1)
    oacc[rows,:]+=dot(g,wout_ref[...],NT)
    dacc[rows,:]+=dot(du,win_ref[...],NT)
    @pl.when(t==nt-1)
    def _():
        dw_ref[:,:FC]=ain[...].astype(BF16)
        dw_ref[:,FC:]=aout[...].astype(BF16)
    @pl.when(c==nc-1)
    def _():
        out_ref[...]=oacc[rows,:].astype(BF16)
        db_ref[...]=dacc[rows,:]
def ffn_call(b,bT,dy,m,win,wout,FC=768,SUB=256,mode="erf",TB=512,order=0):
    T=b.shape[0]; nt=T//TB; FF=3072; nc=FF//FC
    bT3=bT
    last=lambda c,t:(jnp.where(c==nc-1,t,0),0)
    first=lambda c,t:(jnp.where(c==0,t,nt-1),0)
    one=pl.Buffered(1)
    return pl.pallas_call(functools.partial(ffn_kernel,FC=FC,SUB=SUB,nc=nc,nt=nt,mode=mode,TB=TB,order=order),grid=(nc,nt),
        in_specs=[pl.BlockSpec((T,D),lambda c,t:(0,0),pipeline_mode=one),pl.BlockSpec((nt,D,TB),lambda c,t:(0,0,0),pipeline_mode=one),
            pl.BlockSpec((T,D),lambda c,t:(0,0),pipeline_mode=one),
            pl.BlockSpec((TB,D),first),pl.BlockSpec((D,FC),lambda c,t:(0,c+win[1]*D//FC)),pl.BlockSpec((D,FC),lambda c,t:(0,c+wout[1]*D//FC))],
        out_specs=[pl.BlockSpec((TB,D),last),pl.BlockSpec((TB,D),last),pl.BlockSpec((D,2*FC),lambda c,t:(0,c))],
        out_shape=[jax.ShapeDtypeStruct((T,D),BF16),jax.ShapeDtypeStruct((T,D),F32),jax.ShapeDtypeStruct((D,2*FF),BF16)],
        scratch_shapes=[pltpu.VMEM((T,D),F32),pltpu.VMEM((T,D),F32),pltpu.VMEM((nt,D,TB),BF16),pltpu.VMEM((D,FC),F32),pltpu.VMEM((D,FC),F32)],
        name="feed_forward",
        compiler_params=pltpu.CompilerParams(vmem_limit_bytes=62*2**20))(b,bT3,dy,m,win[0],wout[0])

def post_kernel(dy_ref,db_ref,m_ref,oT_ref,wo_ref,ga_ref,dm_ref,doT_ref,dwo_ref,acc_ref,*,nt):
    t=pl.program_id(0)
    @pl.when(t==0)
    def _():
        acc_ref[...]=jnp.zeros_like(acc_ref)
    m=m_ref[...]; db=db_ref[...]
    r=rms(m); n2=m*r
    dn=db*row_of(ga_ref[...],1)
    dm=dy_ref[...].astype(F32)+r*(dn-n2*jnp.mean(dn*n2,axis=-1,keepdims=True))
    dm_ref[...]=dm
    dmb=dm.astype(BF16)
    acc_ref[...]+=dot(dmb.T,oT_ref[...],NT)
    doT_ref[...]=dot(dmb,wo_ref[...]).astype(BF16).T
    @pl.when(t==nt-1)
    def _(): dwo_ref[...]=acc_ref[...].astype(BF16)
def post_call(dy,db,m,oT,woT,gains):
    T=dy.shape[0]; nt=T//BLOCK
    row=pl.BlockSpec((BLOCK,D),lambda t:(t,0)); col=pl.BlockSpec((D,BLOCK),lambda t:(0,t))
    return pl.pallas_call(functools.partial(post_kernel,nt=nt),grid=(nt,),
        in_specs=[row,row,row,col,pl.BlockSpec((D,D),lambda t:(0,woT[1])),pl.BlockSpec((D,GA),lambda t:(0,gains[1]))],
        out_specs=[row,col,pl.BlockSpec((D,D),lambda t:(0,0))],
        out_shape=[jax.ShapeDtypeStruct((T,D),F32),jax.ShapeDtypeStruct((D,T),BF16),jax.ShapeDtypeStruct((D,D),BF16)],
        scratch_shapes=[pltpu.VMEM((D,D),F32)],name="middle_back",
        compiler_params=pltpu.CompilerParams(vmem_limit_bytes=48*2**20))(dy,db,m,oT,woT[0],gains[0])
def last_kernel(x_ref,dm_ref,g_ref,w_ref,dx_ref):
    da=None
    for c in range(3):
        z=dot(w_ref[:,c*D:(c+1)*D],g_ref[c])
        da=z if da is None else da+z
    da=da.T
    x=x_ref[...].astype(F32)
    r=rms(x); n1=x*r
    dn=da*row_of(w_ref[:,3*D:3*D+GA],0)
    dx_ref[...]=(dm_ref[...]+r*(dn-n1*jnp.mean(dn*n1,axis=-1,keepdims=True))).astype(BF16)
def last_call(x,dm,gT,w):
    T=x.shape[0]; nt=T//BLOCK
    row=pl.BlockSpec((BLOCK,D),lambda t:(t,0))
    return pl.pallas_call(last_kernel,grid=(nt,),
        in_specs=[row,row,pl.BlockSpec((3,D,BLOCK),lambda t:(0,0,t)),pl.BlockSpec(w.shape,lambda t:(0,0),pipeline_mode=pl.Buffered(1))],
        out_specs=row,out_shape=jax.ShapeDtypeStruct((T,D),BF16),name="project_back",
        cost_estimate=pl.CostEstimate(flops=2*T*D*3*D,bytes_accessed=20*T*D,transcendentals=0),
        compiler_params=pltpu.CompilerParams(vmem_limit_bytes=56*2**20))(x,dm,gT,w)

GW=3*D+GA
def pack_a_kernel(q_ref,k_ref,v_ref,g1_ref,g2_ref,o_ref):
    for c,ref in enumerate((q_ref,k_ref,v_ref)):
        o_ref[:,c*D:(c+1)*D]=ref[...].astype(BF16)
    rows=o_ref.shape[0]
    g=jnp.concatenate([g1_ref[...],g2_ref[...],jnp.zeros((GA-2,rows),F32)],0)
    o_ref[:,3*D:]=g.T.astype(BF16)
def pack_a(q,k,v,g1,g2):
    return pl.pallas_call(pack_a_kernel,out_shape=jax.ShapeDtypeStruct((q.shape[0],GW),BF16),name="pack_attention")(q,k,v,g1[None],g2[None])
def pack_b_kernel(wo_ref,wi_ref,wu_ref,o_ref):
    F=wi_ref.shape[1]
    o_ref[:,:D]=wo_ref[...].astype(BF16)
    o_ref[:,D:D+F]=wi_ref[...].astype(BF16)
    o_ref[:,D+F:]=wu_ref[...].astype(BF16)
def pack_b(wo,wi,wu):
    return pl.pallas_call(pack_b_kernel,out_shape=jax.ShapeDtypeStruct((wi.shape[0],D+2*wi.shape[1]),BF16),name="pack_feed_forward")(wo.T,wi,wu.T)

def swap(x,axis,mask):
    n=8 if axis=="fsdp" else 4
    f=mask if callable(mask) else (lambda i:mask)
    return lax.ppermute(x,axis,[(i,i^f(i)) for i in range(n)])
first_leg=lambda i: 4 if i&1 else 2
second_leg=lambda i: 2 if i&1 else 4
def gather_pieces(shard,beside):
    a=shard[None]
    a=jnp.concatenate([a,swap(a,"dp",2)],0)
    got=swap(a,"dp",1)
    got,beside=lax.optimization_barrier((got,beside))
    a=jnp.concatenate([a,got],0)
    a=jnp.concatenate([a,swap(a,"fsdp",first_leg)],0)
    b=swap(a,"fsdp",second_leg)
    c=swap(a,"fsdp",1)
    d=swap(b,"fsdp",1)
    return (a,b,c,d),beside
def place():
    f=lax.axis_index("fsdp"); z=lax.axis_index("dp")
    return jnp.stack([f,z]).astype(jnp.int32)
def assemble_rows(at_ref,pieces,put):
    f=at_ref[0]; z=at_ref[1]
    core=f&1; x=(f>>1)&1; y=f>>2
    for j in range(16):
        zj,yj,xj=j>>2,(j>>1)&1,j&1
        dz=zj^z; dx=xj^x; dy=yj^y
        low=(dz&1)*2+(dz>>1)
        halves=[]
        for cj in range(2):
            far_core=core^cj
            one=jnp.where(cj==0,dx,dy)
            two=jnp.where(cj==0,dy,dx)
            slot=one*4+low
            which=far_core*2+two
            halves.append((which,slot))
        put(j,halves)
def project2_kernel(at_ref,x_ref,a_ref,b_ref,c_ref,d_ref,aT_ref,qkvT_ref,w_ref,all_ref,wT_ref):
    R=a_ref.shape[1]
    @pl.when(pl.program_id(0)==0)
    def _():
        for i,ref in enumerate((a_ref,b_ref,c_ref,d_ref)): all_ref[pl.ds(8*i,8)]=ref[...]
        def put(j,halves):
            v=jnp.concatenate([all_ref[w*8+s].astype(F32) for w,s in halves],0)
            w_ref[pl.ds(j*2*R,2*R),:]=v.astype(BF16)
        assemble_rows(at_ref,None,put)
        for c in range(3):
            wT_ref[pl.ds(c*D,D),:]=w_ref[:,c*D:(c+1)*D].T
    x=x_ref[...].astype(F32)
    g=row_of(w_ref[:,3*D:3*D+GA],0)
    a=(x*rms(x)*g).astype(BF16)
    aT=a.T
    aT_ref[...]=aT
    qkvT_ref[...]=dot(wT_ref[...],aT).astype(BF16)
def project2_call(x,pieces,at):
    T=x.shape[0]; R=pieces[0].shape[1]
    one=pl.Buffered(1)
    ps=pl.BlockSpec((8,R,GW),lambda t,at:(0,0,0),pipeline_mode=one)
    return pl.pallas_call(project2_kernel,
        grid_spec=pltpu.PrefetchScalarGridSpec(num_scalar_prefetch=1,grid=(T//BLOCK,),
        in_specs=[pl.BlockSpec((BLOCK,D),lambda t,at:(t,0)),ps,ps,ps,ps],
        out_specs=[pl.BlockSpec((D,BLOCK),lambda t,at:(0,t)),pl.BlockSpec((3*D,BLOCK),lambda t,at:(0,t)),pl.BlockSpec((D,GW),lambda t,at:(0,0))],
        scratch_shapes=[pltpu.VMEM((32,R,GW),BF16),pltpu.VMEM((3*D,D),BF16)]),
        out_shape=[jax.ShapeDtypeStruct((D,T),BF16),jax.ShapeDtypeStruct((3*D,T),BF16),jax.ShapeDtypeStruct((D,GW),BF16)],
        name="project",
        compiler_params=pltpu.CompilerParams(vmem_limit_bytes=60*2**20))(at,x,*pieces)


def add(a,b): return (a.astype(F32)+b.astype(F32)).astype(BF16)
WB=256
GN=4*D+WB
def slot_rows(s,f,z,core):
    x=(f>>1)&1; y=f>>2
    one=s>>3; two=(s>>2)&1
    dx=jnp.where(core==0,one,two); dy=jnp.where(core==0,two,one)
    zz=z^((s>>1)&1)^((s&1)<<1)
    return (zz*8+(y^dy)*4+(x^dx)*2+core)
def grads_kernel(at_ref,aT_ref,g_ref,wo_ref,tab_ref,keep_ref,send_ref,v_ref):
    c=pl.program_id(0)
    R=keep_ref.shape[1]
    @pl.when(c<9)
    def _(): v_ref[...]=dot(aT_ref[...],g_ref[0],NT)
    @pl.when((c>=9)&(c<12))
    def _(): v_ref[...]=wo_ref[...].astype(F32)
    @pl.when(c<12)
    def _():
        f=at_ref[0]; z=at_ref[1]; core=f&1
        for s in range(16):
            for ref,cc in ((keep_ref,core),(send_ref,1-core)):
                j=slot_rows(s,f,z,cc)
                ref[s]=v_ref[pl.ds(pl.multiple_of(j*R,8),R),:].astype(BF16)
    @pl.when(c==12)
    def _():
        t=jnp.concatenate([tab_ref[h,:1,:] for h in range(HEADS)]+[jnp.zeros((R-HEADS,128),F32)],0)
        t=jnp.concatenate([t,jnp.zeros((R,WB-128),F32)],1).astype(BF16)
        for s in range(16):
            keep_ref[s]=t; send_ref[s]=t
def grads_call(at,aT,gT,dwoT,tab):
    T=aT.shape[1]; R=D//32
    nb=D//WB
    out=pl.BlockSpec((16,R,WB),lambda c,at:(0,0,c))
    return pl.pallas_call(grads_kernel,
        grid_spec=pltpu.PrefetchScalarGridSpec(num_scalar_prefetch=1,grid=(GN//WB,),
        in_specs=[pl.BlockSpec((D,T),lambda c,at:(0,0),pipeline_mode=pl.Buffered(1)),
                  pl.BlockSpec((1,WB,T),lambda c,at:(jnp.minimum(c,8)//nb,jnp.minimum(c,8)%nb,0)),
                  pl.BlockSpec((D,WB),lambda c,at:(0,jnp.clip(c-9,0,2))),
                  pl.BlockSpec((HEADS,8,128),lambda c,at:(0,0,0))],
        out_specs=[out,out],scratch_shapes=[pltpu.VMEM((D,WB),F32)]),
        out_shape=[jax.ShapeDtypeStruct((16,R,GN),BF16)]*2,name="weight_grads",
        compiler_params=pltpu.CompilerParams(vmem_limit_bytes=48*2**20))(at,aT,gT,dwoT,tab)
def scatter_sum(keep,send,beside):
    r=swap(send,"fsdp",1)
    for half,axis,leg in ((8,"fsdp",first_leg),(4,"fsdp",second_leg),(2,"dp",1),(1,"dp",2)):
        out=add(keep[half:],r[half:])
        keep=add(keep[:half],r[:half])
        r=swap(out,axis,leg)
        if half==8: r,beside=lax.optimization_barrier((r,beside))
    return keep[0],r[0],beside
def finish_kernel(a_ref,b_ref,wq_ref,wk_ref,wv_ref,g_ref,q_ref,k_ref,v_ref,o_ref,tab_ref,dg_ref):
    R=a_ref.shape[0]
    tot=None
    for c,(w,out) in enumerate(((wq_ref,q_ref),(wk_ref,k_ref),(wv_ref,v_ref),(None,o_ref))):
        sl=slice(c*D,(c+1)*D)
        s=a_ref[:,sl].astype(F32)+b_ref[:,sl].astype(F32)
        out[...]=s
        if w is not None:
            y=jnp.sum(s*w[...].astype(BF16).astype(F32),axis=1,keepdims=True)
            tot=y if tot is None else tot+y
    t=a_ref[:,4*D:4*D+128].astype(F32)+b_ref[:,4*D:4*D+128].astype(F32)
    t=jnp.concatenate([t,jnp.zeros((128-R,128),F32)],0).T
    tab_ref[...]=t[:BUCKETS,:HEADS]
    rowv=jnp.broadcast_to(tot,(R,128))
    rowv=jnp.concatenate([rowv,jnp.zeros((128-R,128),F32)],0).T[:1,:R]
    dg_ref[...]=rowv/g_ref[...].astype(BF16).astype(F32)
def finish_call(a,b,wq,wk,wv,g1):
    R=a.shape[0]; sd=jax.ShapeDtypeStruct
    return pl.pallas_call(finish_kernel,out_shape=[sd((R,D),F32)]*4+[sd((BUCKETS,HEADS),F32),sd((1,R),F32)],name="finish_attention")(a,b,wq,wk,wv,g1[None])
def finish_ffn_kernel(s_ref,w_ref,g_ref,i_ref,o_ref,dg_ref,*,FC):
    R=s_ref.shape[0]
    tot=None
    for c in range(w_ref.shape[1]//FC):
        sl=slice(c*FC,(c+1)*FC)
        s=s_ref[:,2*c*FC:(2*c+1)*FC].astype(F32)
        i_ref[:,sl]=s
        o_ref[:,sl]=s_ref[:,(2*c+1)*FC:(2*c+2)*FC].astype(F32)
        y=jnp.sum(s*w_ref[:,sl].astype(BF16).astype(F32),axis=1,keepdims=True)
        tot=y if tot is None else tot+y
    rowv=jnp.broadcast_to(tot,(R,128))
    rowv=jnp.concatenate([rowv,jnp.zeros((128-R,128),F32)],0).T[:1,:R]
    dg_ref[...]=rowv/g_ref[...].astype(BF16).astype(F32)
def finish_ffn_call(s,w,g2,FC):
    R,F=w.shape; sd=jax.ShapeDtypeStruct
    return pl.pallas_call(functools.partial(finish_ffn_kernel,FC=FC),out_shape=[sd((R,F),F32),sd((R,F),F32),sd((1,R),F32)],name="finish_feed_forward")(s,w,g2[None])

BOTH=("dp","fsdp")
FC=768
def low(v): return v.astype(BF16).astype(F32)
def body(sizes,hidden,long_flags,norm1_gain,query_w,key_w,value_w,out_w,bias_table,norm2_gain,ffn_in,ffn_out,out_grad):
    rows=norm1_gain.shape[0]
    FF=ffn_in.shape[1]
    legs=sizes==(4,8)
    if legs:
        pa=pack_a(query_w,key_w,value_w,norm1_gain,norm2_gain)
        pb=pack_b(out_w,ffn_in,ffn_out)
        wb=lax.all_gather(pb,BOTH,axis=0,tiled=True)
        at=place()
        pieces,bias=gather_pieces(pa,bias_call(bias_table))
        aT,qkvT,wa=project2_call(hidden,pieces,at)
    else:
        bias=bias_call(bias_table)
        gains=jnp.concatenate([norm1_gain[:,None],norm2_gain[:,None],jnp.zeros((rows,GA-2),F32)],1)
        pa=jnp.concatenate([query_w,key_w,value_w,gains],1).astype(BF16)
        pb=jnp.concatenate([out_w.T,ffn_in,ffn_out.T],1).astype(BF16)
        wa=lax.all_gather(pa,BOTH,axis=0,tiled=True)
        wb=lax.all_gather(pb,BOTH,axis=0,tiled=True)
        aT,qkvT=qkv_call(hidden,wa)
    oT,lse=fwd2_call(long_flags,qkvT,bias,HP=4,mode="norm")
    GB=3*D//GA
    m,b,bT=mid_call(hidden,oT,(wb,0),(wa,GB))
    out,db,dffn=ffn_call(b,bT,out_grad,m,(wb,1),(wb,5),FC=FC)
    def rs(x): return lax.psum_scatter(x,BOTH,scatter_dimension=0,tiled=True)
    fsum=rs(dffn)
    dm,doT,dwoT=post_call(out_grad,db,m,oT,(wb,0),(wa,GB))
    gT,tab=bwd2_call(long_flags,qkvT,doT,lse,bias,HP=4)
    if legs:
        keep,send=grads_call(at,aT,gT,dwoT,tab)
        a,b2,dx=scatter_sum(keep,send,last_call(hidden,dm,gT,wa))
        dq,dk,dv,do,table,dg1=finish_call(a,b2,query_w,key_w,value_w,norm1_gain)
        di,du,dg2=finish_ffn_call(fsum,ffn_in,norm2_gain,FC)
        dg1=dg1[0]; dg2=dg2[0]
    else:
        dx=last_call(hidden,dm,gT,wa)
        tabs=tab[:,0,:BUCKETS].reshape(-1)
        wide=tabs.shape[0]//rows
        tb=jnp.tile(tabs.reshape(rows,wide),(D//rows,1))
        parts=[lax.dot_general(aT,gT[c],NT,preferred_element_type=F32).astype(BF16) for c in range(3)]
        asum=rs(jnp.concatenate(parts+[dwoT,tb.astype(BF16)],1)).astype(F32)
        dq,dk,dv,do=[asum[:,c*D:(c+1)*D] for c in range(4)]
        table=asum[:,4*D:].reshape(HEADS,BUCKETS).T
        f=fsum.astype(F32).reshape(rows,FF//FC,2,FC)
        di=f[:,:,0].reshape(rows,FF); du=f[:,:,1].reshape(rows,FF)
        dg1=jnp.sum(dq*low(query_w)+dk*low(key_w)+dv*low(value_w),axis=1)/low(norm1_gain)
        dg2=jnp.sum(di*low(ffn_in),axis=1)/low(norm2_gain)
    return (out,dx,dg1,dq,dk,dv,do.T,table,dg2,di,du.T)

def solution(mesh):
    P=jax.sharding.PartitionSpec
    r=P(BOTH,None); v=P(BOTH); c=P(None,BOTH)
    return jax.shard_map(functools.partial(body,(mesh.shape["dp"],mesh.shape["fsdp"])),mesh=mesh,in_specs=(r,v,v,r,r,r,c,P(),v,r,c,r),out_specs=(r,r,v,r,r,r,c,P(),v,r,c),check_vma=False)
```

```python
import math, functools
import jax, jax.numpy as jnp
from jax import lax
from jax.experimental import pallas as pl
from jax.experimental.pallas import tpu as pltpu
HEADS=12; HEAD_DIM=64; BUCKETS=32; MAX_DIST=128; BLOCK=512; LONG=500; SHORT=250
F32=jnp.float32; BF16=jnp.bfloat16
far=-2.0**30
NN=(((1,),(0,)),((),())); NT=(((1,),(1,)),((),())); TN=(((0,),(0,)),((),()))
def dot(a,b,dn=NN): return lax.dot_general(a,b,dn,preferred_element_type=F32)

def bucket_limits():
    exact_count = BUCKETS // 4
    half_count = BUCKETS // 2
    scale_log = math.log(MAX_DIST / exact_count)
    thresholds = []
    for target in range(1, half_count - exact_count):
        distance = exact_count
        while int(math.log(distance / exact_count) / scale_log * (half_count - exact_count)) < target:
            distance += 1
        thresholds.append(distance)
    return thresholds
def bucket_of(relative):
    distance=jnp.abs(relative)
    exact=BUCKETS//4
    beyond=jnp.full_like(distance,exact)
    for t in bucket_limits():
        beyond=beyond+jnp.where(distance>=t,1,0)
    inside=jnp.where(distance<exact,distance,beyond)
    return inside+jnp.where(relative>0,BUCKETS//2,0)

def bias_kernel(tT_ref, out_ref, ext_ref):
    h=pl.program_id(0)
    @pl.when(h==0)
    def _():
        t=lax.broadcasted_iota(jnp.int32,(1,2*BLOCK),1)
        rel=-jnp.where(t<BLOCK,t,t-2*BLOCK)
        b=bucket_of(rel)
        acc=jnp.zeros((HEADS,2*BLOCK),F32)
        for c in range(BUCKETS):
            acc=jnp.where(b==c,tT_ref[:,c:c+1],acc)
        ext_ref[...]=acc
    row=ext_ref[pl.ds(h,1),:]
    for s in range(4):
        x=jnp.broadcast_to(row,(128,2*BLOCK))
        y=pltpu.roll(x,128*s,axis=1,stride=1,stride_axis=0)
        out_ref[0,pl.ds(128*s,128),:]=y[:,:BLOCK]
def bias_call(table):
    return pl.pallas_call(bias_kernel,grid=(HEADS,),
        in_specs=[pl.BlockSpec((HEADS,BUCKETS),lambda h:(0,0))],
        out_specs=pl.BlockSpec((1,BLOCK,BLOCK),lambda h:(h,0,0)),
        out_shape=jax.ShapeDtypeStruct((HEADS,BLOCK,BLOCK),F32),
        scratch_shapes=[pltpu.VMEM((HEADS,2*BLOCK),F32)],name="bias")(table.T)

def seg_ids(flag):
    s=lax.broadcasted_iota(jnp.int32,(1,BLOCK),1)
    long_ids=jnp.where(s>=LONG,1,0)
    short_ids=jnp.where(s>=SHORT,1,0)+jnp.where(s>=2*SHORT,1,0)
    return jnp.where(flag==1,long_ids,short_ids)
def masks(flag):
    seg=seg_ids(flag)
    c=lax.broadcasted_iota(jnp.int32,(HEAD_DIM,BLOCK),0)
    qm=jnp.where(seg==c,1.0,0.0).astype(BF16)
    km=jnp.where((seg!=c)&(c<3),far,0.0).astype(BF16)
    return qm,km

def fwd_kernel(flags_ref,q_ref,k_ref,v_ref,bias_ref,o_ref,lse_ref,*,CH):
    n=pl.program_id(1)
    qm,km=masks(flags_ref[n])
    qa=jnp.concatenate([q_ref[...],qm],0)
    ka=jnp.concatenate([k_ref[...],km],0).T
    vT=v_ref[...]
    for c in range(BLOCK//CH):
        sl=slice(c*CH,(c+1)*CH)
        s=dot(ka,qa[:,sl])+bias_ref[0,:,sl]
        m=jnp.max(s,axis=0,keepdims=True)
        e=jnp.exp(s-m)
        l=jnp.sum(e,axis=0,keepdims=True)
        p=(e*(1.0/l)).astype(BF16)
        o_ref[:,sl]=dot(vT,p).astype(BF16)
        lse_ref[0,:,sl]=m+jnp.log(l)
def fwd_call(flags,qkvT,bias,CH=256):
    T=qkvT.shape[1]; n=T//BLOCK
    sp=lambda off: pl.BlockSpec((HEAD_DIM,BLOCK),lambda h,n,f:(h+off,n))
    return pl.pallas_call(functools.partial(fwd_kernel,CH=CH),
        grid_spec=pltpu.PrefetchScalarGridSpec(num_scalar_prefetch=1,grid=(HEADS,n),
        in_specs=[sp(0),sp(HEADS),sp(2*HEADS),pl.BlockSpec((1,BLOCK,BLOCK),lambda h,n,f:(h,0,0))],
        out_specs=[pl.BlockSpec((HEAD_DIM,BLOCK),lambda h,n,f:(h,n)),pl.BlockSpec((1,1,BLOCK),lambda h,n,f:(h,0,n))]),
        out_shape=[jax.ShapeDtypeStruct((HEADS*HEAD_DIM,T),BF16),jax.ShapeDtypeStruct((HEADS,1,T),F32)],
        name="attend",
        compiler_params=pltpu.CompilerParams(vmem_limit_bytes=48*2**20))(flags,qkvT,qkvT,qkvT,bias)

def bwd_kernel(flags_ref,q_ref,k_ref,v_ref,do_ref,lse_ref,bias_ref,dq_ref,dk_ref,dv_ref,tab_ref,acc_ref,*,CH,nb):
    n=pl.program_id(1)
    qm,km=masks(flags_ref[n])
    q=q_ref[...]; kT=k_ref[...]; doT=do_ref[...]
    qa=jnp.concatenate([q,qm],0)
    ka=jnp.concatenate([kT,km],0).T
    v=v_ref[...].T
    @pl.when(n==0)
    def _(): acc_ref[...]=jnp.zeros_like(acc_ref)
    dk=None; dv=None
    for c in range(BLOCK//CH):
        sl=slice(c*CH,(c+1)*CH)
        s=dot(ka,qa[:,sl])+bias_ref[0,:,sl]
        p=jnp.exp(s-lse_ref[0,:,sl])
        pb=p.astype(BF16)
        dvc=dot(doT[:,sl],pb,NT)
        dp=dot(v,doT[:,sl])
        t=p*dp
        d=jnp.sum(t,axis=0,keepdims=True)
        ds=(t-p*d).astype(BF16)
        dq_ref[:,sl]=dot(kT,ds).astype(BF16)
        dkc=dot(q[:,sl],ds,NT)
        dk=dkc if dk is None else dk+dkc
        dv=dvc if dv is None else dv+dvc
        acc_ref[:,sl]+=ds.astype(F32)
    dk_ref[...]=dk.astype(BF16); dv_ref[...]=dv.astype(BF16)
    @pl.when(n==nb-1)
    def _():
        tot=None
        zero=jnp.zeros((128,BLOCK),F32)
        for g in range(4):
            x=jnp.concatenate([acc_ref[pl.ds(128*g,128),:],zero],1)
            y=pltpu.roll(x,(2*BLOCK-128*g)%(2*BLOCK),axis=1,stride=2*BLOCK-1,stride_axis=0)
            r=jnp.sum(y,axis=0,keepdims=True)
            tot=r if tot is None else tot+r
        t=lax.broadcasted_iota(jnp.int32,(1,2*BLOCK),1)
        rel=-jnp.where(t<BLOCK,t,t-2*BLOCK)
        b=bucket_of(rel)
        cc=lax.broadcasted_iota(jnp.int32,(BUCKETS,2*BLOCK),0)
        tab_ref[0]=jnp.broadcast_to(jnp.sum(jnp.where(b==cc,tot,0.0),axis=1,keepdims=True),(BUCKETS,128))
def bwd_call(flags,qkvT,doT,lse,bias,CH=256):
    T=qkvT.shape[1]; n=T//BLOCK
    sp=lambda off: pl.BlockSpec((HEAD_DIM,BLOCK),lambda h,n,f:(h+off,n))
    D=HEADS*HEAD_DIM
    return pl.pallas_call(functools.partial(bwd_kernel,CH=CH,nb=n),
        grid_spec=pltpu.PrefetchScalarGridSpec(num_scalar_prefetch=1,grid=(HEADS,n),
        in_specs=[sp(0),sp(HEADS),sp(2*HEADS),sp(0),pl.BlockSpec((1,1,BLOCK),lambda h,n,f:(h,0,n)),pl.BlockSpec((1,BLOCK,BLOCK),lambda h,n,f:(h,0,0))],
        out_specs=[sp(0),sp(0),sp(0),pl.BlockSpec((1,BUCKETS,128),lambda h,n,f:(h,0,0))],
        scratch_shapes=[pltpu.VMEM((BLOCK,BLOCK),F32)]),
        out_shape=[jax.ShapeDtypeStruct((D,T),BF16)]*3+[jax.ShapeDtypeStruct((HEADS,BUCKETS,128),F32)],
        name="attend_back",
        compiler_params=pltpu.CompilerParams(vmem_limit_bytes=48*2**20))(flags,qkvT,qkvT,qkvT,doT,lse,bias)

def fwd2_kernel(flags_ref,q_ref,k_ref,v_ref,bias_ref,o_ref,lse_ref,*,HP,mode):
    n=pl.program_id(1)
    qm,km=masks(flags_ref[n])
    S=[]
    for u in range(HP):
        r=slice(u*64,(u+1)*64)
        qa=jnp.concatenate([q_ref[r,:],qm],0)
        ka=jnp.concatenate([k_ref[r,:],km],0).T
        S.append(dot(ka,qa))
    for u in range(HP):
        r=slice(u*64,(u+1)*64)
        s=S[u]+bias_ref[u]
        m=jnp.max(s,axis=0,keepdims=True)
        e=jnp.exp(s-m)
        if mode=="def":
            l=jnp.sum(e,axis=0,keepdims=True)
            o_ref[r,:]=(dot(v_ref[r,:],e.astype(BF16))*(1.0/l)).astype(BF16)
        elif mode=="ones":
            va=jnp.concatenate([v_ref[r,:],jnp.ones((16,BLOCK),BF16)],0)
            oa=dot(va,e.astype(BF16))
            l=oa[64:65,:]
            o_ref[r,:]=(oa[:64]*(1.0/l)).astype(BF16)
        elif mode=="nomm":
            l=jnp.sum(e,axis=0,keepdims=True)
            o_ref[r,:]=e[:64].astype(BF16)
        else:
            l=jnp.sum(e,axis=0,keepdims=True)
            p=(e*(1.0/l)).astype(BF16)
            o_ref[r,:]=dot(v_ref[r,:],p).astype(BF16)
        lse_ref[u,:,:]=m+jnp.log(l)
def fwd2_call(flags,qkvT,bias,HP=2,mode="norm"):
    T=qkvT.shape[1]; n=T//BLOCK
    G=HEADS//HP
    sp=lambda off: pl.BlockSpec((HP*HEAD_DIM,BLOCK),lambda h,n,f:(h+off,n))
    return pl.pallas_call(functools.partial(fwd2_kernel,HP=HP,mode=mode),
        grid_spec=pltpu.PrefetchScalarGridSpec(num_scalar_prefetch=1,grid=(G,n),
        in_specs=[sp(0),sp(G),sp(2*G),pl.BlockSpec((HP,BLOCK,BLOCK),lambda h,n,f:(h,0,0))],
        out_specs=[pl.BlockSpec((HP*HEAD_DIM,BLOCK),lambda h,n,f:(h,n)),pl.BlockSpec((HP,1,BLOCK),lambda h,n,f:(h,0,n))]),
        out_shape=[jax.ShapeDtypeStruct((HEADS*HEAD_DIM,T),BF16),jax.ShapeDtypeStruct((HEADS,1,T),F32)],
        name="attend",
        compiler_params=pltpu.CompilerParams(vmem_limit_bytes=56*2**20))(flags,qkvT,qkvT,qkvT,bias)
def fwdN_kernel(flags_ref,q_ref,k_ref,v_ref,bias_ref,o_ref,lse_ref,*,HP):
    n=pl.program_id(1)
    qm,km=masks(flags_ref[n])
    for u in range(HP):
        r=slice(u*64,(u+1)*64)
        qa=jnp.concatenate([q_ref[r,:],qm],0)
        ka=jnp.concatenate([k_ref[r,:],km],0).T
        s=dot(ka,qa)+bias_ref[u]
        m=jnp.max(s,axis=0,keepdims=True)
        e=jnp.exp(s-m)
        l=jnp.sum(e,axis=0,keepdims=True)
        o=lax.dot_general(e.astype(BF16),v_ref[r,:],(((0,),(1,)),((),())),preferred_element_type=F32)
        o_ref[r,:]=(o.T*(1.0/l)).astype(BF16)
        lse_ref[u,:,:]=m+jnp.log(l)

def left_by_row(x,width):
    row=lax.broadcasted_iota(jnp.int32,x.shape,0)
    for b in range(7):
        y=pltpu.roll(x,width-(1<<b),axis=1)
        x=jnp.where((row>>b)&1==1,y,x)
    return x
def bwd2_kernel(flags_ref,q_ref,k_ref,v_ref,do_ref,lse_ref,bias_ref,g_ref,tab_ref,band_ref,far_ref,*,HP,nb,tabmode):
    n=pl.program_id(1)
    qm,km=masks(flags_ref[n])
    @pl.when(n==0)
    def _():
        band_ref[...]=jnp.zeros_like(band_ref); far_ref[...]=jnp.zeros_like(far_ref)
    R=[slice(u*64,(u+1)*64) for u in range(HP)]
    S=[];DP=[]
    for u in range(HP):
        r=R[u]
        qa=jnp.concatenate([q_ref[r,:],qm],0)
        ka=jnp.concatenate([k_ref[r,:],km],0).T
        S.append(dot(ka,qa))
        DP.append(dot(v_ref[r,:].T,do_ref[r,:]))
    for u in range(HP):
        r=R[u]
        p=jnp.exp(S[u]+bias_ref[u]-lse_ref[u])
        pb=p.astype(BF16)
        g_ref[2,r,:]=dot(do_ref[r,:],pb,NT).astype(BF16)
        t=p*DP[u]
        d=jnp.sum(t,axis=0,keepdims=True)
        dsf=t-p*d
        ds=dsf.astype(BF16)
        g_ref[0,r,:]=dot(k_ref[r,:],ds).astype(BF16)
        g_ref[1,r,:]=dot(q_ref[r,:],ds,NT).astype(BF16)
        if tabmode:
            lo=None;hi=None;bl=[None]*3
            for g in range(4):
                for c in range(4):
                    tile=dsf[128*g:128*(g+1),128*c:128*(c+1)]
                    w=c-g+1
                    if 0<=w<3:
                        bl[w]=tile if bl[w] is None else bl[w]+tile
                    elif w<0:
                        lo=tile if lo is None else lo+tile
                    else:
                        hi=tile if hi is None else hi+tile
            for w in range(3): band_ref[u,:,128*w:128*(w+1)]+=bl[w]
            far_ref[u,0]+=jnp.sum(lo.reshape(16,8,128),axis=0)
            far_ref[u,1]+=jnp.sum(hi.reshape(16,8,128),axis=0)
    @pl.when(n==nb-1)
    def _():
        t=lax.broadcasted_iota(jnp.int32,(1,BLOCK),1)
        b=bucket_of(-jnp.where(t<384,t-128,t-640))
        cc=lax.broadcasted_iota(jnp.int32,(BUCKETS,BLOCK),0)
        c1=lax.broadcasted_iota(jnp.int32,(BUCKETS,128),0)
        for u in range(HP):
            x=jnp.concatenate([band_ref[u],jnp.zeros((128,128),F32)],1)
            tot=jnp.sum(left_by_row(x,BLOCK),axis=0,keepdims=True)
            lo=jnp.sum(far_ref[u,0],axis=0,keepdims=True); hi=jnp.sum(far_ref[u,1],axis=0,keepdims=True)
            val=jnp.where(b==cc,tot,0.0)
            val=val[:,:128]+val[:,128:256]+val[:,256:384]+val[:,384:]
            val=val+jnp.where(c1==BUCKETS-1,lo,0.0)+jnp.where(c1==BUCKETS//2-1,hi,0.0)
            col=jnp.broadcast_to(jnp.sum(val,axis=1,keepdims=True),(BUCKETS,128))
            col=jnp.concatenate([col,jnp.zeros((128-BUCKETS,128),F32)],0)
            tab_ref[u]=col.T[:8]
def bwd2_call(flags,qkvT,doT,lse,bias,HP=2,tabmode=1):
    T=qkvT.shape[1]; n=T//BLOCK; G=HEADS//HP
    sp=lambda off: pl.BlockSpec((HP*HEAD_DIM,BLOCK),lambda h,n,f:(h+off,n))
    D=HEADS*HEAD_DIM
    return pl.pallas_call(functools.partial(bwd2_kernel,HP=HP,nb=n,tabmode=tabmode),
        grid_spec=pltpu.PrefetchScalarGridSpec(num_scalar_prefetch=1,grid=(G,n),
        in_specs=[sp(0),sp(G),sp(2*G),sp(0),pl.BlockSpec((HP,1,BLOCK),lambda h,n,f:(h,0,n)),pl.BlockSpec((HP,BLOCK,BLOCK),lambda h,n,f:(h,0,0))],
        out_specs=[pl.BlockSpec((3,HP*HEAD_DIM,BLOCK),lambda h,n,f:(0,h,n)),pl.BlockSpec((HP,8,128),lambda h,n,f:(h,0,0))],
        scratch_shapes=[pltpu.VMEM((HP,128,384),F32),pltpu.VMEM((HP,2,8,128),F32)]),
        out_shape=[jax.ShapeDtypeStruct((3,D,T),BF16),jax.ShapeDtypeStruct((HEADS,8,128),F32)],
        name="attend_back",
        compiler_params=pltpu.CompilerParams(vmem_limit_bytes=60*2**20))(flags,qkvT,qkvT,qkvT,doT,lse,bias)

D=768
norm_eps=1e-6
def rms(x): return lax.rsqrt(jnp.mean(x*x,axis=-1,keepdims=True)+norm_eps)
GA=128
def row_of(gains,which):
    return gains.astype(F32).T[which:which+1,:]
def qkv_kernel(x_ref,w_ref,aT_ref,qkvT_ref,wT_ref):
    @pl.when(pl.program_id(0)==0)
    def _():
        for c in range(3):
            wT_ref[pl.ds(c*D,D),:]=w_ref[:,c*D:(c+1)*D].T
    x=x_ref[...].astype(F32)
    g=row_of(w_ref[:,3*D:3*D+GA],0)
    a=(x*rms(x)*g).astype(BF16)
    aT=a.T
    aT_ref[...]=aT
    qkvT_ref[...]=dot(wT_ref[...],aT).astype(BF16)
def qkv_call(x,w):
    T=x.shape[0]
    return pl.pallas_call(qkv_kernel,grid=(T//BLOCK,),
        in_specs=[pl.BlockSpec((BLOCK,D),lambda t:(t,0)),pl.BlockSpec(w.shape,lambda t:(0,0),pipeline_mode=pl.Buffered(1))],
        out_specs=[pl.BlockSpec((D,BLOCK),lambda t:(0,t)),pl.BlockSpec((3*D,BLOCK),lambda t:(0,t))],
        out_shape=[jax.ShapeDtypeStruct((D,T),BF16),jax.ShapeDtypeStruct((3*D,T),BF16)],
        scratch_shapes=[pltpu.VMEM((3*D,D),BF16)],name="project",
        compiler_params=pltpu.CompilerParams(vmem_limit_bytes=56*2**20))(x,w)
def mid_kernel(x_ref,oT_ref,wo_ref,ga_ref,m_ref,b_ref,bT_ref,*_):
    o=oT_ref[...].T
    m=x_ref[...].astype(F32)+dot(o,wo_ref[...],NT)
    m_ref[...]=m
    b=(m*rms(m)*row_of(ga_ref[...],1)).astype(BF16)
    b_ref[...]=b
    bT_ref[0]=b.T
def mid_call(x,oT,woT,gains):
    T=x.shape[0]
    return pl.pallas_call(mid_kernel,grid=(T//BLOCK,),
        in_specs=[pl.BlockSpec((BLOCK,D),lambda t:(t,0)),pl.BlockSpec((D,BLOCK),lambda t:(0,t)),
                  pl.BlockSpec((D,D),lambda t:(0,woT[1])),pl.BlockSpec((D,GA),lambda t:(0,gains[1]))],
        out_specs=[pl.BlockSpec((BLOCK,D),lambda t:(t,0)),pl.BlockSpec((BLOCK,D),lambda t:(t,0)),pl.BlockSpec((1,D,BLOCK),lambda t:(t,0,0))],
        out_shape=[jax.ShapeDtypeStruct((T,D),F32),jax.ShapeDtypeStruct((T,D),BF16),jax.ShapeDtypeStruct((T//BLOCK,D,BLOCK),BF16)],
        name="middle",
        compiler_params=pltpu.CompilerParams(vmem_limit_bytes=48*2**20))(x,oT,woT[0],gains[0])
def gate(u,mode):
    if mode=="erf":
        P=0.5*(1.0+lax.erf(u*(0.5**0.5)))
        z=jnp.exp(-0.5*u*u)
    else:
        z=jnp.exp(-0.5*u*u)
        t=1.0/(1.0+(0.3275911*0.5**0.5)*jnp.abs(u))
        q=((((0.5*1.061405429*t-0.5*1.453152027)*t+0.5*1.421413741)*t-0.5*0.284496736)*t+0.5*0.254829592)*t*z
        P=jnp.where(u>=0,1.0-q,q)
    return u*P, P+u*z*(2*math.pi)**-0.5
def ffn_kernel(b_ref,bT_ref,dy_ref,m_ref,win_ref,wout_ref,out_ref,db_ref,dw_ref,
               oacc,dacc,dyT,ain,aout,*,FC,SUB,nc,nt,mode,TB,order):
    c=pl.program_id(0); t=pl.program_id(1)
    rows=pl.ds(t*TB,TB)
    @pl.when(c==0)
    def _():
        oacc[rows,:]=m_ref[...]
        dacc[rows,:]=jnp.zeros((TB,D),F32)
        dyT[t]=dy_ref[rows,:].T
    b=b_ref[rows,:]; dy=dy_ref[rows,:]
    G=[];DU=[]
    U=[dot(b,win_ref[:,s*SUB:(s+1)*SUB]) for s in range(FC//SUB)]
    DG=[dot(dy,wout_ref[:,s*SUB:(s+1)*SUB]) for s in range(FC//SUB)]
    @pl.when(t==0)
    def _():
        ain[...]=jnp.zeros_like(ain); aout[...]=jnp.zeros_like(aout)
    for s in range(FC//SUB):
        g,pull=gate(U[s],mode)
        g=g.astype(BF16)
        du=(DG[s]*pull).astype(BF16)
        sl=slice(s*SUB,(s+1)*SUB)
        aout[:,sl]+=dot(dyT[t],g)
        ain[:,sl]+=dot(bT_ref[t],du)
        G.append(g);DU.append(du)
    g=jnp.concatenate(G,1);du=jnp.concatenate(DU,1)
    oacc[rows,:]+=dot(g,wout_ref[...],NT)
    dacc[rows,:]+=dot(du,win_ref[...],NT)
    @pl.when(t==nt-1)
    def _():
        dw_ref[:,:FC]=ain[...].astype(BF16)
        dw_ref[:,FC:]=aout[...].astype(BF16)
    @pl.when(c==nc-1)
    def _():
        out_ref[...]=oacc[rows,:].astype(BF16)
        db_ref[...]=dacc[rows,:]
def ffn_call(b,bT,dy,m,win,wout,FC=768,SUB=256,mode="erf",TB=512,order=0):
    T=b.shape[0]; nt=T//TB; FF=3072; nc=FF//FC
    bT3=bT
    last=lambda c,t:(jnp.where(c==nc-1,t,0),0)
    first=lambda c,t:(jnp.where(c==0,t,nt-1),0)
    one=pl.Buffered(1)
    return pl.pallas_call(functools.partial(ffn_kernel,FC=FC,SUB=SUB,nc=nc,nt=nt,mode=mode,TB=TB,order=order),grid=(nc,nt),
        in_specs=[pl.BlockSpec((T,D),lambda c,t:(0,0),pipeline_mode=one),pl.BlockSpec((nt,D,TB),lambda c,t:(0,0,0),pipeline_mode=one),
            pl.BlockSpec((T,D),lambda c,t:(0,0),pipeline_mode=one),
            pl.BlockSpec((TB,D),first),pl.BlockSpec((D,FC),lambda c,t:(0,c+win[1]*D//FC)),pl.BlockSpec((D,FC),lambda c,t:(0,c+wout[1]*D//FC))],
        out_specs=[pl.BlockSpec((TB,D),last),pl.BlockSpec((TB,D),last),pl.BlockSpec((D,2*FC),lambda c,t:(0,c))],
        out_shape=[jax.ShapeDtypeStruct((T,D),BF16),jax.ShapeDtypeStruct((T,D),F32),jax.ShapeDtypeStruct((D,2*FF),BF16)],
        scratch_shapes=[pltpu.VMEM((T,D),F32),pltpu.VMEM((T,D),F32),pltpu.VMEM((nt,D,TB),BF16),pltpu.VMEM((D,FC),F32),pltpu.VMEM((D,FC),F32)],
        name="feed_forward",
        compiler_params=pltpu.CompilerParams(vmem_limit_bytes=62*2**20))(b,bT3,dy,m,win[0],wout[0])

def post_kernel(dy_ref,db_ref,m_ref,oT_ref,wo_ref,ga_ref,dm_ref,doT_ref,dwo_ref,acc_ref,*,nt):
    t=pl.program_id(0)
    @pl.when(t==0)
    def _():
        acc_ref[...]=jnp.zeros_like(acc_ref)
    m=m_ref[...]; db=db_ref[...]
    r=rms(m); n2=m*r
    dn=db*row_of(ga_ref[...],1)
    dm=dy_ref[...].astype(F32)+r*(dn-n2*jnp.mean(dn*n2,axis=-1,keepdims=True))
    dm_ref[...]=dm
    dmb=dm.astype(BF16)
    acc_ref[...]+=dot(dmb.T,oT_ref[...],NT)
    doT_ref[...]=dot(dmb,wo_ref[...]).astype(BF16).T
    @pl.when(t==nt-1)
    def _(): dwo_ref[...]=acc_ref[...].astype(BF16)
def post_call(dy,db,m,oT,woT,gains):
    T=dy.shape[0]; nt=T//BLOCK
    row=pl.BlockSpec((BLOCK,D),lambda t:(t,0)); col=pl.BlockSpec((D,BLOCK),lambda t:(0,t))
    return pl.pallas_call(functools.partial(post_kernel,nt=nt),grid=(nt,),
        in_specs=[row,row,row,col,pl.BlockSpec((D,D),lambda t:(0,woT[1])),pl.BlockSpec((D,GA),lambda t:(0,gains[1]))],
        out_specs=[row,col,pl.BlockSpec((D,D),lambda t:(0,0))],
        out_shape=[jax.ShapeDtypeStruct((T,D),F32),jax.ShapeDtypeStruct((D,T),BF16),jax.ShapeDtypeStruct((D,D),BF16)],
        scratch_shapes=[pltpu.VMEM((D,D),F32)],name="middle_back",
        compiler_params=pltpu.CompilerParams(vmem_limit_bytes=48*2**20))(dy,db,m,oT,woT[0],gains[0])
def last_kernel(x_ref,dm_ref,g_ref,w_ref,dx_ref):
    da=None
    for c in range(3):
        z=dot(w_ref[:,c*D:(c+1)*D],g_ref[c])
        da=z if da is None else da+z
    da=da.T
    x=x_ref[...].astype(F32)
    r=rms(x); n1=x*r
    dn=da*row_of(w_ref[:,3*D:3*D+GA],0)
    dx_ref[...]=(dm_ref[...]+r*(dn-n1*jnp.mean(dn*n1,axis=-1,keepdims=True))).astype(BF16)
def last_call(x,dm,gT,w):
    T=x.shape[0]; nt=T//BLOCK
    row=pl.BlockSpec((BLOCK,D),lambda t:(t,0))
    return pl.pallas_call(last_kernel,grid=(nt,),
        in_specs=[row,row,pl.BlockSpec((3,D,BLOCK),lambda t:(0,0,t)),pl.BlockSpec(w.shape,lambda t:(0,0),pipeline_mode=pl.Buffered(1))],
        out_specs=row,out_shape=jax.ShapeDtypeStruct((T,D),BF16),name="project_back",
        cost_estimate=pl.CostEstimate(flops=2*T*D*3*D,bytes_accessed=20*T*D,transcendentals=0),
        compiler_params=pltpu.CompilerParams(vmem_limit_bytes=56*2**20))(x,dm,gT,w)

def block_kernel(at_ref,x_ref,oT_ref,dy_ref,ga_ref,wo_ref,win_ref,wout_ref,
                 out_ref,dm_ref,doT_ref,dwo_ref,*rest,FC,SUB,nc,nt,legs):
    dw_ref,b_s,bT_s,dyT,oacc,dacc,ain,aout,awo=rest
    c=pl.program_id(0); t=pl.program_id(1)
    rows=pl.ds(t*BLOCK,BLOCK)
    def middle():
        return x_ref[...].astype(F32)+dot(oT_ref[...].T,wo_ref[...],NT)
    @pl.when(c==0)
    def _():
        m=middle()
        b=(m*rms(m)*row_of(ga_ref[...],1)).astype(BF16)
        b_s[t]=b
        bT_s[t]=b.T
        dyT[t]=dy_ref[rows,:].T
        oacc[rows,:]=m
        dacc[rows,:]=jnp.zeros((BLOCK,D),F32)
    b=b_s[t]; dy=dy_ref[rows,:]
    G=[];DU=[]
    n=FC//SUB
    U=[dot(b,win_ref[:,s*SUB:(s+1)*SUB]) for s in range(n)]
    DG=[dot(dy,wout_ref[:,s*SUB:(s+1)*SUB]) for s in range(n)]
    @pl.when(t==0)
    def _():
        ain[...]=jnp.zeros_like(ain); aout[...]=jnp.zeros_like(aout)
    for s in range(n):
        g,pull=gate(U[s],"erf")
        g=g.astype(BF16)
        du=(DG[s]*pull).astype(BF16)
        sl=slice(s*SUB,(s+1)*SUB)
        aout[:,sl]+=dot(dyT[t],g)
        ain[:,sl]+=dot(bT_s[t],du)
        G.append(g);DU.append(du)
    g=jnp.concatenate(G,1);du=jnp.concatenate(DU,1)
    oacc[rows,:]+=dot(g,wout_ref[...],NT)
    dacc[rows,:]+=dot(du,win_ref[...],NT)
    @pl.when(t==nt-1)
    def _():
        if legs:
            R=dw_ref.shape[1]
            for s in range(32):
                z=at_ref[0]^((s>>1)&1)^((s&1)<<1)
                at=pl.ds(pl.multiple_of((z*8+(s>>2))*R,8),R)
                dw_ref[s,:,:FC]=ain[at,:].astype(BF16)
                dw_ref[s,:,FC:]=aout[at,:].astype(BF16)
        else:
            dw_ref[:,:FC]=ain[...].astype(BF16)
            dw_ref[:,FC:]=aout[...].astype(BF16)
    @pl.when((c==nc-1)&(t==0))
    def _(): awo[...]=jnp.zeros_like(awo)
    @pl.when(c==nc-1)
    def _():
        out_ref[...]=oacc[rows,:].astype(BF16)
        m=middle()
        db=dacc[rows,:]
        r=rms(m); n2=m*r
        dn=db*row_of(ga_ref[...],1)
        dm=dy.astype(F32)+r*(dn-n2*jnp.mean(dn*n2,axis=-1,keepdims=True))
        dm_ref[...]=dm
        dmb=dm.astype(BF16)
        awo[...]+=dot(dmb.T,oT_ref[...],NT)
        doT_ref[...]=dot(dmb,wo_ref[...]).astype(BF16).T
    @pl.when((c==nc-1)&(t==nt-1))
    def _(): dwo_ref[...]=awo[...].astype(BF16)
def block_call(x,oT,dy,gains,wo,win,wout,core,legs,FC=768,SUB=256):
    T=x.shape[0]; nt=T//BLOCK; FF=3072; nc=FF//FC
    last=lambda c,t:jnp.where(c==nc-1,t,0)
    ends=lambda c,t:jnp.where((c==0)|(c==nc-1),t,nt-1)
    one=pl.Buffered(1)
    sd=jax.ShapeDtypeStruct; BS=pl.BlockSpec; R=D//32
    return pl.pallas_call(functools.partial(block_kernel,FC=FC,SUB=SUB,nc=nc,nt=nt,legs=legs),
        grid_spec=pltpu.PrefetchScalarGridSpec(num_scalar_prefetch=1,grid=(nc,nt),
        in_specs=[BS((BLOCK,D),lambda c,t,at:(ends(c,t),0)),BS((D,BLOCK),lambda c,t,at:(0,ends(c,t))),
            BS((T,D),lambda c,t,at:(0,0),pipeline_mode=one),
            BS((D,GA),lambda c,t,at:(0,gains[1]),pipeline_mode=one),BS((D,D),lambda c,t,at:(0,wo[1]),pipeline_mode=one),
            BS((D,FC),lambda c,t,at:(0,c+win[1]*D//FC)),BS((D,FC),lambda c,t,at:(0,c+wout[1]*D//FC))],
        out_specs=[BS((BLOCK,D),lambda c,t,at:(last(c,t),0)),BS((BLOCK,D),lambda c,t,at:(last(c,t),0)),BS((D,BLOCK),lambda c,t,at:(0,last(c,t))),
            BS((D,D),lambda c,t,at:(0,0))]+([BS((32,R,2*FC),lambda c,t,at:(0,0,c))] if legs else [BS((D,2*FC),lambda c,t,at:(0,c))]),
        scratch_shapes=[pltpu.VMEM((nt,BLOCK,D),BF16),pltpu.VMEM((nt,D,BLOCK),BF16),pltpu.VMEM((nt,D,BLOCK),BF16),
            pltpu.VMEM((T,D),F32),pltpu.VMEM((T,D),F32),pltpu.VMEM((D,FC),F32),pltpu.VMEM((D,FC),F32),pltpu.VMEM((D,D),F32)]),
        out_shape=[sd((T,D),BF16),sd((T,D),F32),sd((D,T),BF16),sd((D,D),BF16)]+([sd((32,R,2*FF),BF16)] if legs else [sd((D,2*FF),BF16)]),
        name="feed_forward",
        compiler_params=pltpu.CompilerParams(vmem_limit_bytes=62*2**20+2**19))(core,x,oT,dy,gains[0],wo[0],win[0],wout[0])

GW=3*D+GA
INNER=("yx","core")
def pack_a_kernel(q_ref,k_ref,v_ref,g1_ref,g2_ref,o_ref):
    for c,ref in enumerate((q_ref,k_ref,v_ref)):
        o_ref[:,c*D:(c+1)*D]=ref[...].astype(BF16)
    rows=o_ref.shape[0]
    g=jnp.concatenate([g1_ref[...],g2_ref[...],jnp.zeros((GA-2,rows),F32)],0)
    o_ref[:,3*D:]=g.T.astype(BF16)
def pack_a(q,k,v,g1,g2):
    return pl.pallas_call(pack_a_kernel,out_shape=jax.ShapeDtypeStruct((q.shape[0],GW),BF16),name="pack_attention")(q,k,v,g1[None],g2[None])
def pack_b_kernel(wo_ref,wi_ref,wu_ref,o_ref):
    F=wi_ref.shape[1]
    o_ref[:,:D]=wo_ref[...].astype(BF16)
    o_ref[:,D:D+F]=wi_ref[...].astype(BF16)
    o_ref[:,D+F:]=wu_ref[...].astype(BF16)
def pack_b(wo,wi,wu):
    return pl.pallas_call(pack_b_kernel,out_shape=jax.ShapeDtypeStruct((wi.shape[0],D+2*wi.shape[1]),BF16),name="pack_feed_forward")(wo.T,wi,wu.T)

def swap(x,axis,mask):
    n=8 if axis==INNER else 4
    f=mask if callable(mask) else (lambda i:mask)
    return lax.ppermute(x,axis,[(i,i^f(i)) for i in range(n)])
first_leg=lambda i: 4 if i&1 else 2
second_leg=lambda i: 2 if i&1 else 4
def gather_pieces(shard,beside):
    a=shard[None]
    a=jnp.concatenate([a,swap(a,"dp",2)],0)
    got=swap(a,"dp",1)
    got,beside=lax.optimization_barrier((got,beside))
    a=jnp.concatenate([a,got],0)
    a=jnp.concatenate([a,swap(a,INNER,first_leg)],0)
    b=swap(a,INNER,second_leg)
    c=swap(a,INNER,1)
    d=swap(b,INNER,1)
    return (a,b,c,d),beside
def place():
    f=lax.axis_index(INNER); z=lax.axis_index("dp")
    return jnp.stack([f,z]).astype(jnp.int32)
def assemble_rows(at_ref,pieces,put):
    f=at_ref[0]; z=at_ref[1]
    core=f&1; x=(f>>1)&1; y=f>>2
    for j in range(16):
        zj,yj,xj=j>>2,(j>>1)&1,j&1
        dz=zj^z; dx=xj^x; dy=yj^y
        low=(dz&1)*2+(dz>>1)
        halves=[]
        for cj in range(2):
            far_core=core^cj
            one=jnp.where(cj==0,dx,dy)
            two=jnp.where(cj==0,dy,dx)
            slot=one*4+low
            which=far_core*2+two
            halves.append((which,slot))
        put(j,halves)
def project2_kernel(at_ref,x_ref,a_ref,b_ref,c_ref,d_ref,aT_ref,qkvT_ref,w_ref,all_ref,wT_ref):
    R=a_ref.shape[1]
    @pl.when(pl.program_id(0)==0)
    def _():
        for i,ref in enumerate((a_ref,b_ref,c_ref,d_ref)): all_ref[pl.ds(8*i,8)]=ref[...]
        def put(j,halves):
            v=jnp.concatenate([all_ref[w*8+s].astype(F32) for w,s in halves],0)
            w_ref[pl.ds(j*2*R,2*R),:]=v.astype(BF16)
        assemble_rows(at_ref,None,put)
        for c in range(3):
            wT_ref[pl.ds(c*D,D),:]=w_ref[:,c*D:(c+1)*D].T
    x=x_ref[...].astype(F32)
    g=row_of(w_ref[:,3*D:3*D+GA],0)
    a=(x*rms(x)*g).astype(BF16)
    aT=a.T
    aT_ref[...]=aT
    qkvT_ref[...]=dot(wT_ref[...],aT).astype(BF16)
def project2_call(x,pieces,at):
    T=x.shape[0]; R=pieces[0].shape[1]
    one=pl.Buffered(1)
    ps=pl.BlockSpec((8,R,GW),lambda t,at:(0,0,0),pipeline_mode=one)
    return pl.pallas_call(project2_kernel,
        grid_spec=pltpu.PrefetchScalarGridSpec(num_scalar_prefetch=1,grid=(T//BLOCK,),
        in_specs=[pl.BlockSpec((BLOCK,D),lambda t,at:(t,0)),ps,ps,ps,ps],
        out_specs=[pl.BlockSpec((D,BLOCK),lambda t,at:(0,t)),pl.BlockSpec((3*D,BLOCK),lambda t,at:(0,t)),pl.BlockSpec((D,GW),lambda t,at:(0,0))],
        scratch_shapes=[pltpu.VMEM((32,R,GW),BF16),pltpu.VMEM((3*D,D),BF16)]),
        out_shape=[jax.ShapeDtypeStruct((D,T),BF16),jax.ShapeDtypeStruct((3*D,T),BF16),jax.ShapeDtypeStruct((D,GW),BF16)],
        name="project",
        compiler_params=pltpu.CompilerParams(vmem_limit_bytes=60*2**20))(at,x,*pieces)


def add(a,b): return (a.astype(F32)+b.astype(F32)).astype(BF16)
GN=4*D+128
def slot_rows(s,f,z,core):
    x=(f>>1)&1; y=f>>2
    one=s>>3; two=(s>>2)&1
    dx=jnp.where(core==0,one,two); dy=jnp.where(core==0,two,one)
    zz=z^((s>>1)&1)^((s&1)<<1)
    return (zz*8+(y^dy)*4+(x^dx)*2+core)
def slot_table():
    f=lax.axis_index(INNER); z=lax.axis_index("dp")
    s=jnp.arange(16,dtype=jnp.int32); core=f&1
    return jnp.stack([slot_rows(s,f,z,core),slot_rows(s,f,z,1-core)]).astype(jnp.int32)
def grads_kernel(at_ref,aT_ref,g_ref,wo_ref,tab_ref,keep_ref,send_ref,v_ref):
    c=pl.program_id(0)
    R=keep_ref.shape[1]
    @pl.when(c<3)
    def _(): v_ref[...]=dot(aT_ref[...],g_ref[0],NT)
    @pl.when(c==3)
    def _(): v_ref[...]=wo_ref[...].astype(F32)
    @pl.when(c<4)
    def _():
        for s in range(16):
            for q,ref in enumerate((keep_ref,send_ref)):
                ref[s]=v_ref[pl.ds(pl.multiple_of(at_ref[q,s]*R,8),R),:].astype(BF16)
    @pl.when(c==4)
    def _():
        t=jnp.concatenate([tab_ref[h,:1,:] for h in range(HEADS)]+[jnp.zeros((R-HEADS,128),F32)],0).astype(BF16)
        for s in range(16):
            keep_ref[s,:,:128]=t; send_ref[s,:,:128]=t
def grads_call(at,aT,gT,dwoT,tab):
    T=aT.shape[1]; R=D//32
    out=pl.BlockSpec((16,R,D),lambda c,at:(0,0,c))
    return pl.pallas_call(grads_kernel,
        grid_spec=pltpu.PrefetchScalarGridSpec(num_scalar_prefetch=1,grid=(5,),
        in_specs=[pl.BlockSpec((D,T),lambda c,at:(0,0),pipeline_mode=pl.Buffered(1)),
                  pl.BlockSpec((1,D,T),lambda c,at:(jnp.minimum(c,2),0,0)),
                  pl.BlockSpec((D,D),lambda c,at:(0,0),pipeline_mode=pl.Buffered(1)),
                  pl.BlockSpec((HEADS,8,128),lambda c,at:(0,0,0))],
        out_specs=[out,out],scratch_shapes=[pltpu.VMEM((D,D),F32)]),
        out_shape=[jax.ShapeDtypeStruct((16,R,GN),BF16)]*2,name="weight_grads",
        compiler_params=pltpu.CompilerParams(vmem_limit_bytes=48*2**20))(at,aT,gT,dwoT,tab)
def scatter_sum(keep,send,beside):
    r=swap(send,INNER,1)
    for half,axis,leg in ((8,INNER,first_leg),(4,INNER,second_leg),(2,"dp",1),(1,"dp",2)):
        out=add(keep[half:],r[half:])
        keep=add(keep[:half],r[:half])
        r=swap(out,axis,leg)
        if half==8: r,beside=lax.optimization_barrier((r,beside))
    return keep[0],r[0],beside
def finish_kernel(a_ref,b_ref,wq_ref,wk_ref,wv_ref,g_ref,q_ref,k_ref,v_ref,o_ref,tab_ref,dg_ref):
    R=a_ref.shape[0]
    tot=None
    for c,(w,out) in enumerate(((wq_ref,q_ref),(wk_ref,k_ref),(wv_ref,v_ref),(None,o_ref))):
        sl=slice(c*D,(c+1)*D)
        s=a_ref[:,sl].astype(F32)+b_ref[:,sl].astype(F32)
        out[...]=s
        if w is not None:
            y=jnp.sum(s*w[...].astype(BF16).astype(F32),axis=1,keepdims=True)
            tot=y if tot is None else tot+y
    t=a_ref[:,4*D:4*D+128].astype(F32)+b_ref[:,4*D:4*D+128].astype(F32)
    t=jnp.concatenate([t,jnp.zeros((128-R,128),F32)],0).T
    tab_ref[...]=t[:BUCKETS,:HEADS]
    rowv=jnp.broadcast_to(tot,(R,128))
    rowv=jnp.concatenate([rowv,jnp.zeros((128-R,128),F32)],0).T[:1,:R]
    dg_ref[...]=rowv/g_ref[...].astype(BF16).astype(F32)
def finish_call(a,b,wq,wk,wv,g1):
    R=a.shape[0]; sd=jax.ShapeDtypeStruct
    return pl.pallas_call(finish_kernel,out_shape=[sd((R,D),F32)]*4+[sd((BUCKETS,HEADS),F32),sd((1,R),F32)],name="finish_attention")(a,b,wq,wk,wv,g1[None])
def finish_ffn_kernel(s_ref,t_ref,w_ref,g_ref,i_ref,o_ref,dg_ref,*,FC):
    R=s_ref.shape[0]
    tot=None
    for c in range(w_ref.shape[1]//FC):
        sl=slice(c*FC,(c+1)*FC)
        one=slice(2*c*FC,(2*c+1)*FC); two=slice((2*c+1)*FC,(2*c+2)*FC)
        s=s_ref[:,one].astype(F32)+t_ref[:,one].astype(F32)
        i_ref[:,sl]=s
        o_ref[:,sl]=s_ref[:,two].astype(F32)+t_ref[:,two].astype(F32)
        y=jnp.sum(s*w_ref[:,sl].astype(BF16).astype(F32),axis=1,keepdims=True)
        tot=y if tot is None else tot+y
    rowv=jnp.broadcast_to(tot,(R,128))
    rowv=jnp.concatenate([rowv,jnp.zeros((128-R,128),F32)],0).T[:1,:R]
    dg_ref[...]=rowv/g_ref[...].astype(BF16).astype(F32)
def finish_ffn_call(s,t,w,g2,FC):
    R,F=w.shape; sd=jax.ShapeDtypeStruct
    return pl.pallas_call(functools.partial(finish_ffn_kernel,FC=FC),out_shape=[sd((R,F),F32),sd((R,F),F32),sd((1,R),F32)],name="finish_feed_forward")(s,t,w,g2[None])

BOTH=("dp","fsdp")
ALL=("dp","yx","core")
FC=768
def low(v): return v.astype(BF16).astype(F32)
def body(sizes,hidden,long_flags,norm1_gain,query_w,key_w,value_w,out_w,bias_table,norm2_gain,ffn_in,ffn_out,out_grad):
    rows=norm1_gain.shape[0]
    FF=ffn_in.shape[1]
    legs=sizes==(4,8)
    if legs:
        pa=pack_a(query_w,key_w,value_w,norm1_gain,norm2_gain)
        pb=pack_b(out_w,ffn_in,ffn_out)
        wb=lax.all_gather(pb,ALL,axis=0,tiled=True)
        at=place()
        pieces,bias=gather_pieces(pa,bias_call(bias_table))
        aT,qkvT,wa=project2_call(hidden,pieces,at)
    else:
        bias=bias_call(bias_table)
        gains=jnp.concatenate([norm1_gain[:,None],norm2_gain[:,None],jnp.zeros((rows,GA-2),F32)],1)
        pa=jnp.concatenate([query_w,key_w,value_w,gains],1).astype(BF16)
        pb=jnp.concatenate([out_w.T,ffn_in,ffn_out.T],1).astype(BF16)
        wa=lax.all_gather(pa,BOTH,axis=0,tiled=True)
        wb=lax.all_gather(pb,BOTH,axis=0,tiled=True)
        aT,qkvT=qkv_call(hidden,wa)
    oT,lse=fwd2_call(long_flags,qkvT,bias,HP=4,mode="norm")
    GB=3*D//GA
    z=(lax.axis_index("dp") if legs else jnp.zeros((),jnp.int32)).reshape(1)
    out,dm,doT,dwoT,dffn=block_call(hidden,oT,out_grad,(wa,GB),(wb,0),(wb,1),(wb,5),z,legs,FC=FC)
    def rs(x,axes=BOTH): return lax.psum_scatter(x,axes,scatter_dimension=0,tiled=True)
    fsum=rs(dffn.reshape(D,2*FF),INNER if legs else BOTH)
    gT,tab=bwd2_call(long_flags,qkvT,doT,lse,bias,HP=4)
    if legs:
        keep,send=grads_call(slot_table(),aT,gT,dwoT,tab)
        a,b2,dx=scatter_sum(keep,send,last_call(hidden,dm,gT,wa))
        h=fsum.reshape(4,rows,2*FF)
        r=swap(h[2:],"dp",1)
        fa,fb=add(h[0],r[0]),swap(add(h[1],r[1]),"dp",2)
        dq,dk,dv,do,table,dg1=finish_call(a,b2,query_w,key_w,value_w,norm1_gain)
        di,du,dg2=finish_ffn_call(fa,fb,ffn_in,norm2_gain,FC)
        dg1=dg1[0]; dg2=dg2[0]
    else:
        dx=last_call(hidden,dm,gT,wa)
        tabs=tab[:,0,:BUCKETS].reshape(-1)
        wide=tabs.shape[0]//rows
        tb=jnp.tile(tabs.reshape(rows,wide),(D//rows,1))
        parts=[lax.dot_general(aT,gT[c],NT,preferred_element_type=F32).astype(BF16) for c in range(3)]
        asum=rs(jnp.concatenate(parts+[dwoT,tb.astype(BF16)],1)).astype(F32)
        dq,dk,dv,do=[asum[:,c*D:(c+1)*D] for c in range(4)]
        table=asum[:,4*D:].reshape(HEADS,BUCKETS).T
        f=fsum.astype(F32).reshape(rows,FF//FC,2,FC)
        di=f[:,:,0].reshape(rows,FF); du=f[:,:,1].reshape(rows,FF)
        dg1=jnp.sum(dq*low(query_w)+dk*low(key_w)+dv*low(value_w),axis=1)/low(norm1_gain)
        dg2=jnp.sum(di*low(ffn_in),axis=1)/low(norm2_gain)
    return (out,dx,dg1,dq,dk,dv,do.T,table,dg2,di,du.T)

def solution(mesh):
    P=jax.sharding.PartitionSpec
    sizes=(mesh.shape["dp"],mesh.shape["fsdp"])
    axes=BOTH
    if sizes==(4,8):
        mesh=jax.sharding.Mesh(mesh.devices.reshape(4,4,2),ALL)
        axes=ALL
    r=P(axes,None); v=P(axes); c=P(None,axes)
    return jax.shard_map(functools.partial(body,sizes),mesh=mesh,in_specs=(r,v,v,r,r,r,c,P(),v,r,c,r),out_specs=(r,r,v,r,r,r,c,P(),v,r,c),check_vma=False)
```

```python
import math, functools
import jax, jax.numpy as jnp
from jax import lax
from jax.experimental import pallas as pl
from jax.experimental.pallas import tpu as pltpu
HEADS=12; HEAD_DIM=64; BUCKETS=32; MAX_DIST=128; BLOCK=512; LONG=500; SHORT=250
F32=jnp.float32; BF16=jnp.bfloat16
far=-2.0**30
NN=(((1,),(0,)),((),())); NT=(((1,),(1,)),((),())); TN=(((0,),(0,)),((),()))
def dot(a,b,dn=NN): return lax.dot_general(a,b,dn,preferred_element_type=F32)

def bucket_limits():
    exact_count = BUCKETS // 4
    half_count = BUCKETS // 2
    scale_log = math.log(MAX_DIST / exact_count)
    thresholds = []
    for target in range(1, half_count - exact_count):
        distance = exact_count
        while int(math.log(distance / exact_count) / scale_log * (half_count - exact_count)) < target:
            distance += 1
        thresholds.append(distance)
    return thresholds
def bucket_of(relative):
    distance=jnp.abs(relative)
    exact=BUCKETS//4
    beyond=jnp.full_like(distance,exact)
    for t in bucket_limits():
        beyond=beyond+jnp.where(distance>=t,1,0)
    inside=jnp.where(distance<exact,distance,beyond)
    return inside+jnp.where(relative>0,BUCKETS//2,0)

def bias_kernel(tT_ref, out_ref, ext_ref):
    h=pl.program_id(0)
    @pl.when(h==0)
    def _():
        t=lax.broadcasted_iota(jnp.int32,(1,2*BLOCK),1)
        rel=-jnp.where(t<BLOCK,t,t-2*BLOCK)
        b=bucket_of(rel)
        acc=jnp.zeros((HEADS,2*BLOCK),F32)
        for c in range(BUCKETS):
            acc=jnp.where(b==c,tT_ref[:,c:c+1],acc)
        ext_ref[...]=acc
    row=ext_ref[pl.ds(h,1),:]
    for s in range(4):
        x=jnp.broadcast_to(row,(128,2*BLOCK))
        y=pltpu.roll(x,128*s,axis=1,stride=1,stride_axis=0)
        out_ref[0,pl.ds(128*s,128),:]=y[:,:BLOCK]
def bias_call(table):
    return pl.pallas_call(bias_kernel,grid=(HEADS,),
        in_specs=[pl.BlockSpec((HEADS,BUCKETS),lambda h:(0,0))],
        out_specs=pl.BlockSpec((1,BLOCK,BLOCK),lambda h:(h,0,0)),
        out_shape=jax.ShapeDtypeStruct((HEADS,BLOCK,BLOCK),F32),
        scratch_shapes=[pltpu.VMEM((HEADS,2*BLOCK),F32)],name="bias")(table.T)

def seg_ids(flag):
    s=lax.broadcasted_iota(jnp.int32,(1,BLOCK),1)
    long_ids=jnp.where(s>=LONG,1,0)
    short_ids=jnp.where(s>=SHORT,1,0)+jnp.where(s>=2*SHORT,1,0)
    return jnp.where(flag==1,long_ids,short_ids)
def masks(flag):
    seg=seg_ids(flag)
    c=lax.broadcasted_iota(jnp.int32,(HEAD_DIM,BLOCK),0)
    qm=jnp.where(seg==c,1.0,0.0).astype(BF16)
    km=jnp.where((seg!=c)&(c<3),far,0.0).astype(BF16)
    return qm,km

def fwd_kernel(flags_ref,q_ref,k_ref,v_ref,bias_ref,o_ref,lse_ref,*,CH):
    n=pl.program_id(1)
    qm,km=masks(flags_ref[n])
    qa=jnp.concatenate([q_ref[...],qm],0)
    ka=jnp.concatenate([k_ref[...],km],0).T
    vT=v_ref[...]
    for c in range(BLOCK//CH):
        sl=slice(c*CH,(c+1)*CH)
        s=dot(ka,qa[:,sl])+bias_ref[0,:,sl]
        m=jnp.max(s,axis=0,keepdims=True)
        e=jnp.exp(s-m)
        l=jnp.sum(e,axis=0,keepdims=True)
        p=(e*(1.0/l)).astype(BF16)
        o_ref[:,sl]=dot(vT,p).astype(BF16)
        lse_ref[0,:,sl]=m+jnp.log(l)
def fwd_call(flags,qkvT,bias,CH=256):
    T=qkvT.shape[1]; n=T//BLOCK
    sp=lambda off: pl.BlockSpec((HEAD_DIM,BLOCK),lambda h,n,f:(h+off,n))
    return pl.pallas_call(functools.partial(fwd_kernel,CH=CH),
        grid_spec=pltpu.PrefetchScalarGridSpec(num_scalar_prefetch=1,grid=(HEADS,n),
        in_specs=[sp(0),sp(HEADS),sp(2*HEADS),pl.BlockSpec((1,BLOCK,BLOCK),lambda h,n,f:(h,0,0))],
        out_specs=[pl.BlockSpec((HEAD_DIM,BLOCK),lambda h,n,f:(h,n)),pl.BlockSpec((1,1,BLOCK),lambda h,n,f:(h,0,n))]),
        out_shape=[jax.ShapeDtypeStruct((HEADS*HEAD_DIM,T),BF16),jax.ShapeDtypeStruct((HEADS,1,T),F32)],
        name="attend",
        compiler_params=pltpu.CompilerParams(vmem_limit_bytes=48*2**20))(flags,qkvT,qkvT,qkvT,bias)

def bwd_kernel(flags_ref,q_ref,k_ref,v_ref,do_ref,lse_ref,bias_ref,dq_ref,dk_ref,dv_ref,tab_ref,acc_ref,*,CH,nb):
    n=pl.program_id(1)
    qm,km=masks(flags_ref[n])
    q=q_ref[...]; kT=k_ref[...]; doT=do_ref[...]
    qa=jnp.concatenate([q,qm],0)
    ka=jnp.concatenate([kT,km],0).T
    v=v_ref[...].T
    @pl.when(n==0)
    def _(): acc_ref[...]=jnp.zeros_like(acc_ref)
    dk=None; dv=None
    for c in range(BLOCK//CH):
        sl=slice(c*CH,(c+1)*CH)
        s=dot(ka,qa[:,sl])+bias_ref[0,:,sl]
        p=jnp.exp(s-lse_ref[0,:,sl])
        pb=p.astype(BF16)
        dvc=dot(doT[:,sl],pb,NT)
        dp=dot(v,doT[:,sl])
        t=p*dp
        d=jnp.sum(t,axis=0,keepdims=True)
        ds=(t-p*d).astype(BF16)
        dq_ref[:,sl]=dot(kT,ds).astype(BF16)
        dkc=dot(q[:,sl],ds,NT)
        dk=dkc if dk is None else dk+dkc
        dv=dvc if dv is None else dv+dvc
        acc_ref[:,sl]+=ds.astype(F32)
    dk_ref[...]=dk.astype(BF16); dv_ref[...]=dv.astype(BF16)
    @pl.when(n==nb-1)
    def _():
        tot=None
        zero=jnp.zeros((128,BLOCK),F32)
        for g in range(4):
            x=jnp.concatenate([acc_ref[pl.ds(128*g,128),:],zero],1)
            y=pltpu.roll(x,(2*BLOCK-128*g)%(2*BLOCK),axis=1,stride=2*BLOCK-1,stride_axis=0)
            r=jnp.sum(y,axis=0,keepdims=True)
            tot=r if tot is None else tot+r
        t=lax.broadcasted_iota(jnp.int32,(1,2*BLOCK),1)
        rel=-jnp.where(t<BLOCK,t,t-2*BLOCK)
        b=bucket_of(rel)
        cc=lax.broadcasted_iota(jnp.int32,(BUCKETS,2*BLOCK),0)
        tab_ref[0]=jnp.broadcast_to(jnp.sum(jnp.where(b==cc,tot,0.0),axis=1,keepdims=True),(BUCKETS,128))
def bwd_call(flags,qkvT,doT,lse,bias,CH=256):
    T=qkvT.shape[1]; n=T//BLOCK
    sp=lambda off: pl.BlockSpec((HEAD_DIM,BLOCK),lambda h,n,f:(h+off,n))
    D=HEADS*HEAD_DIM
    return pl.pallas_call(functools.partial(bwd_kernel,CH=CH,nb=n),
        grid_spec=pltpu.PrefetchScalarGridSpec(num_scalar_prefetch=1,grid=(HEADS,n),
        in_specs=[sp(0),sp(HEADS),sp(2*HEADS),sp(0),pl.BlockSpec((1,1,BLOCK),lambda h,n,f:(h,0,n)),pl.BlockSpec((1,BLOCK,BLOCK),lambda h,n,f:(h,0,0))],
        out_specs=[sp(0),sp(0),sp(0),pl.BlockSpec((1,BUCKETS,128),lambda h,n,f:(h,0,0))],
        scratch_shapes=[pltpu.VMEM((BLOCK,BLOCK),F32)]),
        out_shape=[jax.ShapeDtypeStruct((D,T),BF16)]*3+[jax.ShapeDtypeStruct((HEADS,BUCKETS,128),F32)],
        name="attend_back",
        compiler_params=pltpu.CompilerParams(vmem_limit_bytes=48*2**20))(flags,qkvT,qkvT,qkvT,doT,lse,bias)

def fwd2_kernel(flags_ref,q_ref,k_ref,v_ref,bias_ref,o_ref,lse_ref,*,HP,mode):
    n=pl.program_id(1)
    qm,km=masks(flags_ref[n])
    S=[]
    for u in range(HP):
        r=slice(u*64,(u+1)*64)
        qa=jnp.concatenate([q_ref[r,:],qm],0)
        ka=jnp.concatenate([k_ref[r,:],km],0).T
        S.append(dot(ka,qa))
    for u in range(HP):
        r=slice(u*64,(u+1)*64)
        s=S[u]+bias_ref[u]
        m=jnp.max(s,axis=0,keepdims=True)
        e=jnp.exp(s-m)
        if mode=="def":
            l=jnp.sum(e,axis=0,keepdims=True)
            o_ref[r,:]=(dot(v_ref[r,:],e.astype(BF16))*(1.0/l)).astype(BF16)
        elif mode=="ones":
            va=jnp.concatenate([v_ref[r,:],jnp.ones((16,BLOCK),BF16)],0)
            oa=dot(va,e.astype(BF16))
            l=oa[64:65,:]
            o_ref[r,:]=(oa[:64]*(1.0/l)).astype(BF16)
        elif mode=="nomm":
            l=jnp.sum(e,axis=0,keepdims=True)
            o_ref[r,:]=e[:64].astype(BF16)
        else:
            l=jnp.sum(e,axis=0,keepdims=True)
            p=(e*(1.0/l)).astype(BF16)
            o_ref[r,:]=dot(v_ref[r,:],p).astype(BF16)
        lse_ref[u,:,:]=m+jnp.log(l)
def fwd2_call(flags,qkvT,bias,HP=2,mode="norm"):
    T=qkvT.shape[1]; n=T//BLOCK
    G=HEADS//HP
    sp=lambda off: pl.BlockSpec((HP*HEAD_DIM,BLOCK),lambda h,n,f:(h+off,n))
    return pl.pallas_call(functools.partial(fwd2_kernel,HP=HP,mode=mode),
        grid_spec=pltpu.PrefetchScalarGridSpec(num_scalar_prefetch=1,grid=(G,n),
        in_specs=[sp(0),sp(G),sp(2*G),pl.BlockSpec((HP,BLOCK,BLOCK),lambda h,n,f:(h,0,0))],
        out_specs=[pl.BlockSpec((HP*HEAD_DIM,BLOCK),lambda h,n,f:(h,n)),pl.BlockSpec((HP,1,BLOCK),lambda h,n,f:(h,0,n))]),
        out_shape=[jax.ShapeDtypeStruct((HEADS*HEAD_DIM,T),BF16),jax.ShapeDtypeStruct((HEADS,1,T),F32)],
        name="attend",
        compiler_params=pltpu.CompilerParams(vmem_limit_bytes=56*2**20))(flags,qkvT,qkvT,qkvT,bias)
def fwdN_kernel(flags_ref,q_ref,k_ref,v_ref,bias_ref,o_ref,lse_ref,*,HP):
    n=pl.program_id(1)
    qm,km=masks(flags_ref[n])
    for u in range(HP):
        r=slice(u*64,(u+1)*64)
        qa=jnp.concatenate([q_ref[r,:],qm],0)
        ka=jnp.concatenate([k_ref[r,:],km],0).T
        s=dot(ka,qa)+bias_ref[u]
        m=jnp.max(s,axis=0,keepdims=True)
        e=jnp.exp(s-m)
        l=jnp.sum(e,axis=0,keepdims=True)
        o=lax.dot_general(e.astype(BF16),v_ref[r,:],(((0,),(1,)),((),())),preferred_element_type=F32)
        o_ref[r,:]=(o.T*(1.0/l)).astype(BF16)
        lse_ref[u,:,:]=m+jnp.log(l)

def left_by_row(x,width):
    row=lax.broadcasted_iota(jnp.int32,x.shape,0)
    for b in range(7):
        y=pltpu.roll(x,width-(1<<b),axis=1)
        x=jnp.where((row>>b)&1==1,y,x)
    return x
def bwd2_kernel(flags_ref,q_ref,k_ref,v_ref,do_ref,lse_ref,bias_ref,g_ref,tab_ref,band_ref,far_ref,*,HP,nb,tabmode):
    n=pl.program_id(1)
    qm,km=masks(flags_ref[n])
    @pl.when(n==0)
    def _():
        band_ref[...]=jnp.zeros_like(band_ref); far_ref[...]=jnp.zeros_like(far_ref)
    R=[slice(u*64,(u+1)*64) for u in range(HP)]
    S=[];DP=[]
    for u in range(HP):
        r=R[u]
        qa=jnp.concatenate([q_ref[r,:],qm],0)
        ka=jnp.concatenate([k_ref[r,:],km],0).T
        S.append(dot(ka,qa))
        DP.append(dot(v_ref[r,:].T,do_ref[r,:]))
    for u in range(HP):
        r=R[u]
        p=jnp.exp(S[u]+bias_ref[u]-lse_ref[u])
        pb=p.astype(BF16)
        g_ref[2,r,:]=dot(do_ref[r,:],pb,NT).astype(BF16)
        t=p*DP[u]
        d=jnp.sum(t,axis=0,keepdims=True)
        dsf=t-p*d
        ds=dsf.astype(BF16)
        g_ref[0,r,:]=dot(k_ref[r,:],ds).astype(BF16)
        g_ref[1,r,:]=dot(q_ref[r,:],ds,NT).astype(BF16)
        if tabmode:
            lo=None;hi=None;bl=[None]*3
            for g in range(4):
                for c in range(4):
                    tile=dsf[128*g:128*(g+1),128*c:128*(c+1)]
                    w=c-g+1
                    if 0<=w<3:
                        bl[w]=tile if bl[w] is None else bl[w]+tile
                    elif w<0:
                        lo=tile if lo is None else lo+tile
                    else:
                        hi=tile if hi is None else hi+tile
            for w in range(3): band_ref[u,:,128*w:128*(w+1)]+=bl[w]
            far_ref[u,0]+=jnp.sum(lo.reshape(16,8,128),axis=0)
            far_ref[u,1]+=jnp.sum(hi.reshape(16,8,128),axis=0)
    @pl.when(n==nb-1)
    def _():
        t=lax.broadcasted_iota(jnp.int32,(1,BLOCK),1)
        b=bucket_of(-jnp.where(t<384,t-128,t-640))
        cc=lax.broadcasted_iota(jnp.int32,(BUCKETS,BLOCK),0)
        c1=lax.broadcasted_iota(jnp.int32,(BUCKETS,128),0)
        for u in range(HP):
            x=jnp.concatenate([band_ref[u],jnp.zeros((128,128),F32)],1)
            tot=jnp.sum(left_by_row(x,BLOCK),axis=0,keepdims=True)
            lo=jnp.sum(far_ref[u,0],axis=0,keepdims=True); hi=jnp.sum(far_ref[u,1],axis=0,keepdims=True)
            val=jnp.where(b==cc,tot,0.0)
            val=val[:,:128]+val[:,128:256]+val[:,256:384]+val[:,384:]
            val=val+jnp.where(c1==BUCKETS-1,lo,0.0)+jnp.where(c1==BUCKETS//2-1,hi,0.0)
            col=jnp.broadcast_to(jnp.sum(val,axis=1,keepdims=True),(BUCKETS,128))
            col=jnp.concatenate([col,jnp.zeros((128-BUCKETS,128),F32)],0)
            tab_ref[u]=col.T[:8]
def bwd2_call(flags,qkvT,doT,lse,bias,HP=2,tabmode=1):
    T=qkvT.shape[1]; n=T//BLOCK; G=HEADS//HP
    sp=lambda off: pl.BlockSpec((HP*HEAD_DIM,BLOCK),lambda h,n,f:(h+off,n))
    D=HEADS*HEAD_DIM
    return pl.pallas_call(functools.partial(bwd2_kernel,HP=HP,nb=n,tabmode=tabmode),
        grid_spec=pltpu.PrefetchScalarGridSpec(num_scalar_prefetch=1,grid=(G,n),
        in_specs=[sp(0),sp(G),sp(2*G),sp(0),pl.BlockSpec((HP,1,BLOCK),lambda h,n,f:(h,0,n)),pl.BlockSpec((HP,BLOCK,BLOCK),lambda h,n,f:(h,0,0))],
        out_specs=[pl.BlockSpec((3,HP*HEAD_DIM,BLOCK),lambda h,n,f:(0,h,n)),pl.BlockSpec((HP,8,128),lambda h,n,f:(h,0,0))],
        scratch_shapes=[pltpu.VMEM((HP,128,384),F32),pltpu.VMEM((HP,2,8,128),F32)]),
        out_shape=[jax.ShapeDtypeStruct((3,D,T),BF16),jax.ShapeDtypeStruct((HEADS,8,128),F32)],
        name="attend_back",
        compiler_params=pltpu.CompilerParams(vmem_limit_bytes=60*2**20))(flags,qkvT,qkvT,qkvT,doT,lse,bias)

D=768
norm_eps=1e-6
def rms(x): return lax.rsqrt(jnp.mean(x*x,axis=-1,keepdims=True)+norm_eps)
GA=128
def row_of(gains,which):
    return gains.astype(F32).T[which:which+1,:]
def qkv_kernel(x_ref,w_ref,aT_ref,qkvT_ref,wT_ref):
    @pl.when(pl.program_id(0)==0)
    def _():
        for c in range(3):
            wT_ref[pl.ds(c*D,D),:]=w_ref[:,c*D:(c+1)*D].T
    x=x_ref[...].astype(F32)
    g=row_of(w_ref[:,3*D:3*D+GA],0)
    a=(x*rms(x)*g).astype(BF16)
    aT=a.T
    aT_ref[...]=aT
    qkvT_ref[...]=dot(wT_ref[...],aT).astype(BF16)
def qkv_call(x,w):
    T=x.shape[0]
    return pl.pallas_call(qkv_kernel,grid=(T//BLOCK,),
        in_specs=[pl.BlockSpec((BLOCK,D),lambda t:(t,0)),pl.BlockSpec(w.shape,lambda t:(0,0),pipeline_mode=pl.Buffered(1))],
        out_specs=[pl.BlockSpec((D,BLOCK),lambda t:(0,t)),pl.BlockSpec((3*D,BLOCK),lambda t:(0,t))],
        out_shape=[jax.ShapeDtypeStruct((D,T),BF16),jax.ShapeDtypeStruct((3*D,T),BF16)],
        scratch_shapes=[pltpu.VMEM((3*D,D),BF16)],name="project",
        compiler_params=pltpu.CompilerParams(vmem_limit_bytes=56*2**20))(x,w)
def mid_kernel(x_ref,oT_ref,wo_ref,ga_ref,m_ref,b_ref,bT_ref,*_):
    o=oT_ref[...].T
    m=x_ref[...].astype(F32)+dot(o,wo_ref[...],NT)
    m_ref[...]=m
    b=(m*rms(m)*row_of(ga_ref[...],1)).astype(BF16)
    b_ref[...]=b
    bT_ref[0]=b.T
def mid_call(x,oT,woT,gains):
    T=x.shape[0]
    return pl.pallas_call(mid_kernel,grid=(T//BLOCK,),
        in_specs=[pl.BlockSpec((BLOCK,D),lambda t:(t,0)),pl.BlockSpec((D,BLOCK),lambda t:(0,t)),
                  pl.BlockSpec((D,D),lambda t:(0,woT[1])),pl.BlockSpec((D,GA),lambda t:(0,gains[1]))],
        out_specs=[pl.BlockSpec((BLOCK,D),lambda t:(t,0)),pl.BlockSpec((BLOCK,D),lambda t:(t,0)),pl.BlockSpec((1,D,BLOCK),lambda t:(t,0,0))],
        out_shape=[jax.ShapeDtypeStruct((T,D),F32),jax.ShapeDtypeStruct((T,D),BF16),jax.ShapeDtypeStruct((T//BLOCK,D,BLOCK),BF16)],
        name="middle",
        compiler_params=pltpu.CompilerParams(vmem_limit_bytes=48*2**20))(x,oT,woT[0],gains[0])
def gate(u,mode):
    if mode=="erf":
        P=0.5*(1.0+lax.erf(u*(0.5**0.5)))
        z=jnp.exp(-0.5*u*u)
    else:
        z=jnp.exp(-0.5*u*u)
        t=1.0/(1.0+(0.3275911*0.5**0.5)*jnp.abs(u))
        q=((((0.5*1.061405429*t-0.5*1.453152027)*t+0.5*1.421413741)*t-0.5*0.284496736)*t+0.5*0.254829592)*t*z
        P=jnp.where(u>=0,1.0-q,q)
    return u*P, P+u*z*(2*math.pi)**-0.5
def ffn_kernel(b_ref,bT_ref,dy_ref,m_ref,win_ref,wout_ref,out_ref,db_ref,dw_ref,
               oacc,dacc,dyT,ain,aout,*,FC,SUB,nc,nt,mode,TB,order):
    c=pl.program_id(0); t=pl.program_id(1)
    rows=pl.ds(t*TB,TB)
    @pl.when(c==0)
    def _():
        oacc[rows,:]=m_ref[...]
        dacc[rows,:]=jnp.zeros((TB,D),F32)
        dyT[t]=dy_ref[rows,:].T
    b=b_ref[rows,:]; dy=dy_ref[rows,:]
    G=[];DU=[]
    U=[dot(b,win_ref[:,s*SUB:(s+1)*SUB]) for s in range(FC//SUB)]
    DG=[dot(dy,wout_ref[:,s*SUB:(s+1)*SUB]) for s in range(FC//SUB)]
    @pl.when(t==0)
    def _():
        ain[...]=jnp.zeros_like(ain); aout[...]=jnp.zeros_like(aout)
    for s in range(FC//SUB):
        g,pull=gate(U[s],mode)
        g=g.astype(BF16)
        du=(DG[s]*pull).astype(BF16)
        sl=slice(s*SUB,(s+1)*SUB)
        aout[:,sl]+=dot(dyT[t],g)
        ain[:,sl]+=dot(bT_ref[t],du)
        G.append(g);DU.append(du)
    g=jnp.concatenate(G,1);du=jnp.concatenate(DU,1)
    oacc[rows,:]+=dot(g,wout_ref[...],NT)
    dacc[rows,:]+=dot(du,win_ref[...],NT)
    @pl.when(t==nt-1)
    def _():
        dw_ref[:,:FC]=ain[...].astype(BF16)
        dw_ref[:,FC:]=aout[...].astype(BF16)
    @pl.when(c==nc-1)
    def _():
        out_ref[...]=oacc[rows,:].astype(BF16)
        db_ref[...]=dacc[rows,:]
def ffn_call(b,bT,dy,m,win,wout,FC=768,SUB=256,mode="erf",TB=512,order=0):
    T=b.shape[0]; nt=T//TB; FF=3072; nc=FF//FC
    bT3=bT
    last=lambda c,t:(jnp.where(c==nc-1,t,0),0)
    first=lambda c,t:(jnp.where(c==0,t,nt-1),0)
    one=pl.Buffered(1)
    return pl.pallas_call(functools.partial(ffn_kernel,FC=FC,SUB=SUB,nc=nc,nt=nt,mode=mode,TB=TB,order=order),grid=(nc,nt),
        in_specs=[pl.BlockSpec((T,D),lambda c,t:(0,0),pipeline_mode=one),pl.BlockSpec((nt,D,TB),lambda c,t:(0,0,0),pipeline_mode=one),
            pl.BlockSpec((T,D),lambda c,t:(0,0),pipeline_mode=one),
            pl.BlockSpec((TB,D),first),pl.BlockSpec((D,FC),lambda c,t:(0,c+win[1]*D//FC)),pl.BlockSpec((D,FC),lambda c,t:(0,c+wout[1]*D//FC))],
        out_specs=[pl.BlockSpec((TB,D),last),pl.BlockSpec((TB,D),last),pl.BlockSpec((D,2*FC),lambda c,t:(0,c))],
        out_shape=[jax.ShapeDtypeStruct((T,D),BF16),jax.ShapeDtypeStruct((T,D),F32),jax.ShapeDtypeStruct((D,2*FF),BF16)],
        scratch_shapes=[pltpu.VMEM((T,D),F32),pltpu.VMEM((T,D),F32),pltpu.VMEM((nt,D,TB),BF16),pltpu.VMEM((D,FC),F32),pltpu.VMEM((D,FC),F32)],
        name="feed_forward",
        compiler_params=pltpu.CompilerParams(vmem_limit_bytes=62*2**20))(b,bT3,dy,m,win[0],wout[0])

def post_kernel(dy_ref,db_ref,m_ref,oT_ref,wo_ref,ga_ref,dm_ref,doT_ref,dwo_ref,acc_ref,*,nt):
    t=pl.program_id(0)
    @pl.when(t==0)
    def _():
        acc_ref[...]=jnp.zeros_like(acc_ref)
    m=m_ref[...]; db=db_ref[...]
    r=rms(m); n2=m*r
    dn=db*row_of(ga_ref[...],1)
    dm=dy_ref[...].astype(F32)+r*(dn-n2*jnp.mean(dn*n2,axis=-1,keepdims=True))
    dm_ref[...]=dm
    dmb=dm.astype(BF16)
    acc_ref[...]+=dot(dmb.T,oT_ref[...],NT)
    doT_ref[...]=dot(dmb,wo_ref[...]).astype(BF16).T
    @pl.when(t==nt-1)
    def _(): dwo_ref[...]=acc_ref[...].astype(BF16)
def post_call(dy,db,m,oT,woT,gains):
    T=dy.shape[0]; nt=T//BLOCK
    row=pl.BlockSpec((BLOCK,D),lambda t:(t,0)); col=pl.BlockSpec((D,BLOCK),lambda t:(0,t))
    return pl.pallas_call(functools.partial(post_kernel,nt=nt),grid=(nt,),
        in_specs=[row,row,row,col,pl.BlockSpec((D,D),lambda t:(0,woT[1])),pl.BlockSpec((D,GA),lambda t:(0,gains[1]))],
        out_specs=[row,col,pl.BlockSpec((D,D),lambda t:(0,0))],
        out_shape=[jax.ShapeDtypeStruct((T,D),F32),jax.ShapeDtypeStruct((D,T),BF16),jax.ShapeDtypeStruct((D,D),BF16)],
        scratch_shapes=[pltpu.VMEM((D,D),F32)],name="middle_back",
        compiler_params=pltpu.CompilerParams(vmem_limit_bytes=48*2**20))(dy,db,m,oT,woT[0],gains[0])
def last_kernel(x_ref,dm_ref,g_ref,w_ref,dx_ref):
    da=None
    for c in range(3):
        z=dot(w_ref[:,c*D:(c+1)*D],g_ref[c])
        da=z if da is None else da+z
    da=da.T
    x=x_ref[...].astype(F32)
    r=rms(x); n1=x*r
    dn=da*row_of(w_ref[:,3*D:3*D+GA],0)
    dx_ref[...]=(dm_ref[...]+r*(dn-n1*jnp.mean(dn*n1,axis=-1,keepdims=True))).astype(BF16)
def last_call(x,dm,gT,w):
    T=x.shape[0]; nt=T//BLOCK
    row=pl.BlockSpec((BLOCK,D),lambda t:(t,0))
    return pl.pallas_call(last_kernel,grid=(nt,),
        in_specs=[row,row,pl.BlockSpec((3,D,BLOCK),lambda t:(0,0,t)),pl.BlockSpec(w.shape,lambda t:(0,0),pipeline_mode=pl.Buffered(1))],
        out_specs=row,out_shape=jax.ShapeDtypeStruct((T,D),BF16),name="project_back",
        cost_estimate=pl.CostEstimate(flops=2*T*D*3*D,bytes_accessed=20*T*D,transcendentals=0),
        compiler_params=pltpu.CompilerParams(vmem_limit_bytes=56*2**20))(x,dm,gT,w)

def block_kernel(at_ref,x_ref,oT_ref,dy_ref,ga_ref,wo_ref,win_ref,wout_ref,
                 out_ref,dm_ref,doT_ref,dwo_ref,*rest,FC,SUB,nc,nt,legs):
    dw_ref,b_s,bT_s,oacc,dacc,ain,aout,awo,m_s=rest
    c=pl.program_id(0); t=pl.program_id(1)
    rows=pl.ds(t*BLOCK,BLOCK)
    def middle():
        return x_ref[...].astype(F32)+dot(oT_ref[...].T,wo_ref[...],NT)
    @pl.when(c==0)
    def _():
        m=middle()
        b=(m*rms(m)*row_of(ga_ref[...],1)).astype(BF16)
        b_s[t]=b
        bT_s[t]=b.T
        oacc[rows,:]=m
        m_s[rows,:]=m
        dacc[rows,:]=jnp.zeros((BLOCK,D),F32)
    b=b_s[t]; dy=dy_ref[...]
    dyt=dy.T
    G=[];DU=[]
    n=FC//SUB
    U=[dot(b,win_ref[:,s*SUB:(s+1)*SUB]) for s in range(n)]
    DG=[dot(dy,wout_ref[:,s*SUB:(s+1)*SUB]) for s in range(n)]
    @pl.when(t==0)
    def _():
        ain[...]=jnp.zeros_like(ain); aout[...]=jnp.zeros_like(aout)
    for s in range(n):
        g,pull=gate(U[s],"erf")
        g=g.astype(BF16)
        du=(DG[s]*pull).astype(BF16)
        sl=slice(s*SUB,(s+1)*SUB)
        aout[:,sl]+=dot(dyt,g)
        ain[:,sl]+=dot(bT_s[t],du)
        G.append(g);DU.append(du)
    g=jnp.concatenate(G,1);du=jnp.concatenate(DU,1)
    oacc[rows,:]+=dot(g,wout_ref[...],NT)
    dacc[rows,:]+=dot(du,win_ref[...],NT)
    @pl.when(t==nt-1)
    def _():
        if legs:
            R=dw_ref.shape[1]
            for s in range(32):
                z=at_ref[0]^((s>>1)&1)^((s&1)<<1)
                at=pl.ds(pl.multiple_of((z*8+(s>>2))*R,8),R)
                dw_ref[s,:,:FC]=ain[at,:].astype(BF16)
                dw_ref[s,:,FC:]=aout[at,:].astype(BF16)
        else:
            dw_ref[:,:FC]=ain[...].astype(BF16)
            dw_ref[:,FC:]=aout[...].astype(BF16)
    @pl.when((c==nc-1)&(t==0))
    def _(): awo[...]=jnp.zeros_like(awo)
    @pl.when(c==nc-1)
    def _():
        out_ref[...]=oacc[rows,:].astype(BF16)
        m=m_s[rows,:]
        db=dacc[rows,:]
        r=rms(m); n2=m*r
        dn=db*row_of(ga_ref[...],1)
        dm=dy.astype(F32)+r*(dn-n2*jnp.mean(dn*n2,axis=-1,keepdims=True))
        dm_ref[...]=dm
        dmb=dm.astype(BF16)
        awo[...]+=dot(dmb.T,oT_ref[...],NT)
        doT_ref[...]=dot(dmb,wo_ref[...]).astype(BF16).T
    @pl.when((c==nc-1)&(t==nt-1))
    def _(): dwo_ref[...]=awo[...].astype(BF16)
def block_call(x,oT,dy,gains,wo,win,wout,core,legs,FC=768,SUB=256):
    T=x.shape[0]; nt=T//BLOCK; FF=3072; nc=FF//FC
    last=lambda c,t:jnp.where(c==nc-1,t,0)
    first=lambda c,t:jnp.where(c==0,t,nt-1)
    ends=lambda c,t:jnp.where((c==0)|(c==nc-1),t,nt-1)
    one=pl.Buffered(1)
    sd=jax.ShapeDtypeStruct; BS=pl.BlockSpec; R=D//32
    return pl.pallas_call(functools.partial(block_kernel,FC=FC,SUB=SUB,nc=nc,nt=nt,legs=legs),
        grid_spec=pltpu.PrefetchScalarGridSpec(num_scalar_prefetch=1,grid=(nc,nt),
        in_specs=[BS((BLOCK,D),lambda c,t,at:(first(c,t),0)),BS((D,BLOCK),lambda c,t,at:(0,ends(c,t))),
            BS((BLOCK,D),lambda c,t,at:(t,0)),
            BS((D,GA),lambda c,t,at:(0,gains[1]),pipeline_mode=one),BS((D,D),lambda c,t,at:(0,wo[1]),pipeline_mode=one),
            BS((D,FC),lambda c,t,at:(0,c+win[1]*D//FC)),BS((D,FC),lambda c,t,at:(0,c+wout[1]*D//FC))],
        out_specs=[BS((BLOCK,D),lambda c,t,at:(last(c,t),0)),BS((BLOCK,D),lambda c,t,at:(last(c,t),0)),BS((D,BLOCK),lambda c,t,at:(0,last(c,t))),
            BS((D,D),lambda c,t,at:(0,0),pipeline_mode=one)]+([BS((32,R,2*FC),lambda c,t,at:(0,0,c))] if legs else [BS((D,2*FC),lambda c,t,at:(0,c))]),
        scratch_shapes=[pltpu.VMEM((nt,BLOCK,D),BF16),pltpu.VMEM((nt,D,BLOCK),BF16),
            pltpu.VMEM((T,D),F32),pltpu.VMEM((T,D),F32),pltpu.VMEM((D,FC),F32),pltpu.VMEM((D,FC),F32),pltpu.VMEM((D,D),F32),pltpu.VMEM((T,D),F32)]),
        out_shape=[sd((T,D),BF16),sd((T,D),F32),sd((D,T),BF16),sd((D,D),BF16)]+([sd((32,R,2*FF),BF16)] if legs else [sd((D,2*FF),BF16)]),
        name="feed_forward",
        compiler_params=pltpu.CompilerParams(vmem_limit_bytes=62*2**20+2**19))(core,x,oT,dy,gains[0],wo[0],win[0],wout[0])

GW=3*D+GA
INNER=("yx","core")
def pack_a_kernel(q_ref,k_ref,v_ref,g1_ref,g2_ref,o_ref):
    for c,ref in enumerate((q_ref,k_ref,v_ref)):
        o_ref[:,c*D:(c+1)*D]=ref[...].astype(BF16)
    rows=o_ref.shape[0]
    g=jnp.concatenate([g1_ref[...],g2_ref[...],jnp.zeros((GA-2,rows),F32)],0)
    o_ref[:,3*D:]=g.T.astype(BF16)
def pack_a(q,k,v,g1,g2):
    return pl.pallas_call(pack_a_kernel,out_shape=jax.ShapeDtypeStruct((q.shape[0],GW),BF16),name="pack_attention")(q,k,v,g1[None],g2[None])
def pack_b_kernel(wo_ref,wi_ref,wu_ref,o_ref):
    F=wi_ref.shape[1]
    o_ref[:,:D]=wo_ref[...].astype(BF16)
    o_ref[:,D:D+F]=wi_ref[...].astype(BF16)
    o_ref[:,D+F:]=wu_ref[...].astype(BF16)
def pack_b(wo,wi,wu):
    return pl.pallas_call(pack_b_kernel,out_shape=jax.ShapeDtypeStruct((wi.shape[0],D+2*wi.shape[1]),BF16),name="pack_feed_forward")(wo.T,wi,wu.T)

def swap(x,axis,mask):
    n=8 if axis==INNER else 4
    f=mask if callable(mask) else (lambda i:mask)
    return lax.ppermute(x,axis,[(i,i^f(i)) for i in range(n)])
first_leg=lambda i: 4 if i&1 else 2
second_leg=lambda i: 2 if i&1 else 4
def gather_pieces(shard,beside):
    a=shard[None]
    a=jnp.concatenate([a,swap(a,"dp",2)],0)
    got=swap(a,"dp",1)
    got,beside=lax.optimization_barrier((got,beside))
    a=jnp.concatenate([a,got],0)
    a=jnp.concatenate([a,swap(a,INNER,first_leg)],0)
    b=swap(a,INNER,second_leg)
    c=swap(a,INNER,1)
    d=swap(b,INNER,1)
    return (a,b,c,d),beside
def place():
    f=lax.axis_index(INNER); z=lax.axis_index("dp")
    return jnp.stack([f,z]).astype(jnp.int32)
def assemble_rows(at_ref,pieces,put):
    f=at_ref[0]; z=at_ref[1]
    core=f&1; x=(f>>1)&1; y=f>>2
    for j in range(16):
        zj,yj,xj=j>>2,(j>>1)&1,j&1
        dz=zj^z; dx=xj^x; dy=yj^y
        low=(dz&1)*2+(dz>>1)
        halves=[]
        for cj in range(2):
            far_core=core^cj
            one=jnp.where(cj==0,dx,dy)
            two=jnp.where(cj==0,dy,dx)
            slot=one*4+low
            which=far_core*2+two
            halves.append((which,slot))
        put(j,halves)
def project2_kernel(at_ref,x_ref,a_ref,b_ref,c_ref,d_ref,aT_ref,qkvT_ref,w_ref,all_ref,wT_ref):
    R=a_ref.shape[1]
    @pl.when(pl.program_id(0)==0)
    def _():
        for i,ref in enumerate((a_ref,b_ref,c_ref,d_ref)): all_ref[pl.ds(8*i,8)]=ref[...]
        def put(j,halves):
            v=jnp.concatenate([all_ref[w*8+s].astype(F32) for w,s in halves],0)
            w_ref[pl.ds(j*2*R,2*R),:]=v.astype(BF16)
        assemble_rows(at_ref,None,put)
        for c in range(3):
            wT_ref[pl.ds(c*D,D),:]=w_ref[:,c*D:(c+1)*D].T
    x=x_ref[...].astype(F32)
    g=row_of(w_ref[:,3*D:3*D+GA],0)
    a=(x*rms(x)*g).astype(BF16)
    aT=a.T
    aT_ref[...]=aT
    qkvT_ref[...]=dot(wT_ref[...],aT).astype(BF16)
def project2_call(x,pieces,at):
    T=x.shape[0]; R=pieces[0].shape[1]
    one=pl.Buffered(1)
    ps=pl.BlockSpec((8,R,GW),lambda t,at:(0,0,0),pipeline_mode=one)
    return pl.pallas_call(project2_kernel,
        grid_spec=pltpu.PrefetchScalarGridSpec(num_scalar_prefetch=1,grid=(T//BLOCK,),
        in_specs=[pl.BlockSpec((BLOCK,D),lambda t,at:(t,0)),ps,ps,ps,ps],
        out_specs=[pl.BlockSpec((D,BLOCK),lambda t,at:(0,t)),pl.BlockSpec((3*D,BLOCK),lambda t,at:(0,t)),pl.BlockSpec((D,GW),lambda t,at:(0,0))],
        scratch_shapes=[pltpu.VMEM((32,R,GW),BF16),pltpu.VMEM((3*D,D),BF16)]),
        out_shape=[jax.ShapeDtypeStruct((D,T),BF16),jax.ShapeDtypeStruct((3*D,T),BF16),jax.ShapeDtypeStruct((D,GW),BF16)],
        name="project",
        compiler_params=pltpu.CompilerParams(vmem_limit_bytes=60*2**20))(at,x,*pieces)


def add(a,b): return (a.astype(F32)+b.astype(F32)).astype(BF16)
GN=4*D+128
def slot_rows(s,f,z,core):
    x=(f>>1)&1; y=f>>2
    one=s>>3; two=(s>>2)&1
    dx=jnp.where(core==0,one,two); dy=jnp.where(core==0,two,one)
    zz=z^((s>>1)&1)^((s&1)<<1)
    return (zz*8+(y^dy)*4+(x^dx)*2+core)
def slot_table():
    f=lax.axis_index(INNER); z=lax.axis_index("dp")
    s=jnp.arange(16,dtype=jnp.int32); core=f&1
    return jnp.stack([slot_rows(s,f,z,core),slot_rows(s,f,z,1-core)]).astype(jnp.int32)
def grads_kernel(at_ref,aT_ref,g_ref,wo_ref,tab_ref,keep_ref,send_ref,v_ref):
    c=pl.program_id(0)
    R=keep_ref.shape[1]
    @pl.when(c<3)
    def _(): v_ref[...]=dot(aT_ref[...],g_ref[0],NT)
    @pl.when(c==3)
    def _(): v_ref[...]=wo_ref[...].astype(F32)
    @pl.when(c<4)
    def _():
        for s in range(16):
            for q,ref in enumerate((keep_ref,send_ref)):
                ref[s]=v_ref[pl.ds(pl.multiple_of(at_ref[q,s]*R,8),R),:].astype(BF16)
    @pl.when(c==4)
    def _():
        t=jnp.concatenate([tab_ref[h,:1,:] for h in range(HEADS)]+[jnp.zeros((R-HEADS,128),F32)],0).astype(BF16)
        for s in range(16):
            keep_ref[s,:,:128]=t; send_ref[s,:,:128]=t
def grads_call(at,aT,gT,dwoT,tab):
    T=aT.shape[1]; R=D//32
    out=pl.BlockSpec((16,R,D),lambda c,at:(0,0,c))
    return pl.pallas_call(grads_kernel,
        grid_spec=pltpu.PrefetchScalarGridSpec(num_scalar_prefetch=1,grid=(5,),
        in_specs=[pl.BlockSpec((D,T),lambda c,at:(0,0),pipeline_mode=pl.Buffered(1)),
                  pl.BlockSpec((1,D,T),lambda c,at:(jnp.minimum(c,2),0,0)),
                  pl.BlockSpec((D,D),lambda c,at:(0,0),pipeline_mode=pl.Buffered(1)),
                  pl.BlockSpec((HEADS,8,128),lambda c,at:(0,0,0))],
        out_specs=[out,out],scratch_shapes=[pltpu.VMEM((D,D),F32)]),
        out_shape=[jax.ShapeDtypeStruct((16,R,GN),BF16)]*2,name="weight_grads",
        compiler_params=pltpu.CompilerParams(vmem_limit_bytes=48*2**20))(at,aT,gT,dwoT,tab)
def scatter_sum(keep,send,beside,other,rest):
    r=swap(send,INNER,1)
    for half,axis,leg in ((8,INNER,first_leg),(4,INNER,second_leg),(2,"dp",1),(1,"dp",2)):
        out=add(keep[half:],r[half:])
        keep=add(keep[:half],r[:half])
        r=swap(out,axis,leg)
        if half==8:
            r,beside,other=lax.optimization_barrier((r,beside,other))
            late=rest(other)
    r,late=lax.optimization_barrier((r,late))
    return keep[0],r[0],beside,late
def finish_kernel(a_ref,b_ref,wq_ref,wk_ref,wv_ref,g_ref,q_ref,k_ref,v_ref,o_ref,tab_ref,dg_ref):
    R=a_ref.shape[0]
    tot=None
    for c,(w,out) in enumerate(((wq_ref,q_ref),(wk_ref,k_ref),(wv_ref,v_ref),(None,o_ref))):
        sl=slice(c*D,(c+1)*D)
        s=a_ref[:,sl].astype(F32)+b_ref[:,sl].astype(F32)
        out[...]=s
        if w is not None:
            y=jnp.sum(s*w[...].astype(BF16).astype(F32),axis=1,keepdims=True)
            tot=y if tot is None else tot+y
    t=a_ref[:,4*D:4*D+128].astype(F32)+b_ref[:,4*D:4*D+128].astype(F32)
    tab_ref[...]=t[:HEADS,:BUCKETS]
    rowv=jnp.broadcast_to(tot,(R,128))
    rowv=jnp.concatenate([rowv,jnp.zeros((128-R,128),F32)],0).T[:1,:R]
    dg_ref[...]=rowv/g_ref[...].astype(BF16).astype(F32)
def finish_call(a,b,wq,wk,wv,g1):
    R=a.shape[0]; sd=jax.ShapeDtypeStruct
    return pl.pallas_call(finish_kernel,out_shape=[sd((R,D),F32)]*4+[sd((HEADS,BUCKETS),F32),sd((1,R),F32)],name="finish_attention")(a,b,wq,wk,wv,g1[None])
def finish_ffn_kernel(s_ref,t_ref,w_ref,g_ref,i_ref,o_ref,dg_ref,*,FC):
    R=s_ref.shape[0]
    tot=None
    for c in range(w_ref.shape[1]//FC):
        sl=slice(c*FC,(c+1)*FC)
        one=slice(2*c*FC,(2*c+1)*FC); two=slice((2*c+1)*FC,(2*c+2)*FC)
        s=s_ref[:,one].astype(F32)+t_ref[:,one].astype(F32)
        i_ref[:,sl]=s
        o_ref[:,sl]=s_ref[:,two].astype(F32)+t_ref[:,two].astype(F32)
        y=jnp.sum(s*w_ref[:,sl].astype(BF16).astype(F32),axis=1,keepdims=True)
        tot=y if tot is None else tot+y
    rowv=jnp.broadcast_to(tot,(R,128))
    rowv=jnp.concatenate([rowv,jnp.zeros((128-R,128),F32)],0).T[:1,:R]
    dg_ref[...]=rowv/g_ref[...].astype(BF16).astype(F32)
def finish_ffn_call(s,t,w,g2,FC):
    R,F=w.shape; sd=jax.ShapeDtypeStruct
    return pl.pallas_call(functools.partial(finish_ffn_kernel,FC=FC),out_shape=[sd((R,F),F32),sd((R,F),F32),sd((1,R),F32)],name="finish_feed_forward")(s,t,w,g2[None])

BOTH=("dp","fsdp")
ALL=("dp","yx","core")
FC=768
def low(v): return v.astype(BF16).astype(F32)
def body(sizes,hidden,long_flags,norm1_gain,query_w,key_w,value_w,out_w,bias_table,norm2_gain,ffn_in,ffn_out,out_grad):
    rows=norm1_gain.shape[0]
    FF=ffn_in.shape[1]
    legs=sizes==(4,8)
    if legs:
        pa=pack_a(query_w,key_w,value_w,norm1_gain,norm2_gain)
        pb=pack_b(out_w,ffn_in,ffn_out)
        wb=lax.all_gather(pb,ALL,axis=0,tiled=True)
        at=place()
        pieces,bias=gather_pieces(pa,bias_call(bias_table))
        aT,qkvT,wa=project2_call(hidden,pieces,at)
    else:
        bias=bias_call(bias_table)
        gains=jnp.concatenate([norm1_gain[:,None],norm2_gain[:,None],jnp.zeros((rows,GA-2),F32)],1)
        pa=jnp.concatenate([query_w,key_w,value_w,gains],1).astype(BF16)
        pb=jnp.concatenate([out_w.T,ffn_in,ffn_out.T],1).astype(BF16)
        wa=lax.all_gather(pa,BOTH,axis=0,tiled=True)
        wb=lax.all_gather(pb,BOTH,axis=0,tiled=True)
        aT,qkvT=qkv_call(hidden,wa)
    oT,lse=fwd2_call(long_flags,qkvT,bias,HP=4,mode="ones")
    GB=3*D//GA
    z=(lax.axis_index("dp") if legs else jnp.zeros((),jnp.int32)).reshape(1)
    out,dm,doT,dwoT,dffn=block_call(hidden,oT,out_grad,(wa,GB),(wb,0),(wb,1),(wb,5),z,legs,FC=FC)
    def rs(x,axes=BOTH): return lax.psum_scatter(x,axes,scatter_dimension=0,tiled=True)
    fsum=rs(dffn.reshape(D,2*FF),INNER if legs else BOTH)
    gT,tab=bwd2_call(long_flags,qkvT,doT,lse,bias,HP=4)
    if legs:
        keep,send=grads_call(slot_table(),aT,gT,dwoT,tab)
        h=fsum.reshape(4,rows,2*FF)
        h,dm=lax.optimization_barrier((h,dm))
        r=swap(h[2:],"dp",1)
        def rest(r):
            fa,fb=add(h[0],r[0]),swap(add(h[1],r[1]),"dp",2)
            return finish_ffn_call(fa,fb,ffn_in,norm2_gain,FC)
        a,b2,dx,(di,du,dg2)=scatter_sum(keep,send,last_call(hidden,dm,gT,wa),r,rest)
        dq,dk,dv,do,table,dg1=finish_call(a,b2,query_w,key_w,value_w,norm1_gain)
        dg1=dg1[0]; dg2=dg2[0]; table=table.T
    else:
        dx=last_call(hidden,dm,gT,wa)
        tabs=tab[:,0,:BUCKETS].reshape(-1)
        wide=tabs.shape[0]//rows
        tb=jnp.tile(tabs.reshape(rows,wide),(D//rows,1))
        parts=[lax.dot_general(aT,gT[c],NT,preferred_element_type=F32).astype(BF16) for c in range(3)]
        asum=rs(jnp.concatenate(parts+[dwoT,tb.astype(BF16)],1)).astype(F32)
        dq,dk,dv,do=[asum[:,c*D:(c+1)*D] for c in range(4)]
        table=asum[:,4*D:].reshape(HEADS,BUCKETS).T
        f=fsum.astype(F32).reshape(rows,FF//FC,2,FC)
        di=f[:,:,0].reshape(rows,FF); du=f[:,:,1].reshape(rows,FF)
        dg1=jnp.sum(dq*low(query_w)+dk*low(key_w)+dv*low(value_w),axis=1)/low(norm1_gain)
        dg2=jnp.sum(di*low(ffn_in),axis=1)/low(norm2_gain)
    return (out,dx,dg1,dq,dk,dv,do.T,table,dg2,di,du.T)

def solution(mesh):
    P=jax.sharding.PartitionSpec
    sizes=(mesh.shape["dp"],mesh.shape["fsdp"])
    axes=BOTH
    if sizes==(4,8):
        mesh=jax.sharding.Mesh(mesh.devices.reshape(4,4,2),ALL)
        axes=ALL
    r=P(axes,None); v=P(axes); c=P(None,axes)
    return jax.shard_map(functools.partial(body,sizes),mesh=mesh,in_specs=(r,v,v,r,r,r,c,P(),v,r,c,r),out_specs=(r,r,v,r,r,r,c,P(),v,r,c),check_vma=False)
```

```python
import math, functools
import jax, jax.numpy as jnp
from jax import lax
from jax.experimental import pallas as pl
from jax.experimental.pallas import tpu as pltpu
HEADS=12; HEAD_DIM=64; BUCKETS=32; MAX_DIST=128; BLOCK=512; LONG=500; SHORT=250
F32=jnp.float32; BF16=jnp.bfloat16
far=-2.0**30
NN=(((1,),(0,)),((),())); NT=(((1,),(1,)),((),())); TN=(((0,),(0,)),((),()))
def dot(a,b,dn=NN): return lax.dot_general(a,b,dn,preferred_element_type=F32)

def bucket_limits():
    exact_count = BUCKETS // 4
    half_count = BUCKETS // 2
    scale_log = math.log(MAX_DIST / exact_count)
    thresholds = []
    for target in range(1, half_count - exact_count):
        distance = exact_count
        while int(math.log(distance / exact_count) / scale_log * (half_count - exact_count)) < target:
            distance += 1
        thresholds.append(distance)
    return thresholds
def bucket_of(relative):
    distance=jnp.abs(relative)
    exact=BUCKETS//4
    beyond=jnp.full_like(distance,exact)
    for t in bucket_limits():
        beyond=beyond+jnp.where(distance>=t,1,0)
    inside=jnp.where(distance<exact,distance,beyond)
    return inside+jnp.where(relative>0,BUCKETS//2,0)

def bias_kernel(tT_ref, out_ref, ext_ref):
    h=pl.program_id(0)
    @pl.when(h==0)
    def _():
        t=lax.broadcasted_iota(jnp.int32,(1,2*BLOCK),1)
        rel=-jnp.where(t<BLOCK,t,t-2*BLOCK)
        b=bucket_of(rel)
        acc=jnp.zeros((HEADS,2*BLOCK),F32)
        for c in range(BUCKETS):
            acc=jnp.where(b==c,tT_ref[:,c:c+1],acc)
        ext_ref[...]=acc
    row=ext_ref[pl.ds(h,1),:]
    for s in range(4):
        x=jnp.broadcast_to(row,(128,2*BLOCK))
        y=pltpu.roll(x,128*s,axis=1,stride=1,stride_axis=0)
        out_ref[0,pl.ds(128*s,128),:]=y[:,:BLOCK]
def bias_call(table):
    return pl.pallas_call(bias_kernel,grid=(HEADS,),
        in_specs=[pl.BlockSpec((HEADS,BUCKETS),lambda h:(0,0))],
        out_specs=pl.BlockSpec((1,BLOCK,BLOCK),lambda h:(h,0,0)),
        out_shape=jax.ShapeDtypeStruct((HEADS,BLOCK,BLOCK),F32),
        scratch_shapes=[pltpu.VMEM((HEADS,2*BLOCK),F32)],name="bias")(table.T)

def seg_ids(flag):
    s=lax.broadcasted_iota(jnp.int32,(1,BLOCK),1)
    long_ids=jnp.where(s>=LONG,1,0)
    short_ids=jnp.where(s>=SHORT,1,0)+jnp.where(s>=2*SHORT,1,0)
    return jnp.where(flag==1,long_ids,short_ids)
def masks(flag):
    seg=seg_ids(flag)
    c=lax.broadcasted_iota(jnp.int32,(HEAD_DIM,BLOCK),0)
    qm=jnp.where(seg==c,1.0,0.0).astype(BF16)
    km=jnp.where((seg!=c)&(c<3),far,0.0).astype(BF16)
    return qm,km

def fwd_kernel(flags_ref,q_ref,k_ref,v_ref,bias_ref,o_ref,lse_ref,*,CH):
    n=pl.program_id(1)
    qm,km=masks(flags_ref[n])
    qa=jnp.concatenate([q_ref[...],qm],0)
    ka=jnp.concatenate([k_ref[...],km],0).T
    vT=v_ref[...]
    for c in range(BLOCK//CH):
        sl=slice(c*CH,(c+1)*CH)
        s=dot(ka,qa[:,sl])+bias_ref[0,:,sl]
        m=jnp.max(s,axis=0,keepdims=True)
        e=jnp.exp(s-m)
        l=jnp.sum(e,axis=0,keepdims=True)
        p=(e*(1.0/l)).astype(BF16)
        o_ref[:,sl]=dot(vT,p).astype(BF16)
        lse_ref[0,:,sl]=m+jnp.log(l)
def fwd_call(flags,qkvT,bias,CH=256):
    T=qkvT.shape[1]; n=T//BLOCK
    sp=lambda off: pl.BlockSpec((HEAD_DIM,BLOCK),lambda h,n,f:(h+off,n))
    return pl.pallas_call(functools.partial(fwd_kernel,CH=CH),
        grid_spec=pltpu.PrefetchScalarGridSpec(num_scalar_prefetch=1,grid=(HEADS,n),
        in_specs=[sp(0),sp(HEADS),sp(2*HEADS),pl.BlockSpec((1,BLOCK,BLOCK),lambda h,n,f:(h,0,0))],
        out_specs=[pl.BlockSpec((HEAD_DIM,BLOCK),lambda h,n,f:(h,n)),pl.BlockSpec((1,1,BLOCK),lambda h,n,f:(h,0,n))]),
        out_shape=[jax.ShapeDtypeStruct((HEADS*HEAD_DIM,T),BF16),jax.ShapeDtypeStruct((HEADS,1,T),F32)],
        name="attend",
        compiler_params=pltpu.CompilerParams(vmem_limit_bytes=48*2**20))(flags,qkvT,qkvT,qkvT,bias)

def bwd_kernel(flags_ref,q_ref,k_ref,v_ref,do_ref,lse_ref,bias_ref,dq_ref,dk_ref,dv_ref,tab_ref,acc_ref,*,CH,nb):
    n=pl.program_id(1)
    qm,km=masks(flags_ref[n])
    q=q_ref[...]; kT=k_ref[...]; doT=do_ref[...]
    qa=jnp.concatenate([q,qm],0)
    ka=jnp.concatenate([kT,km],0).T
    v=v_ref[...].T
    @pl.when(n==0)
    def _(): acc_ref[...]=jnp.zeros_like(acc_ref)
    dk=None; dv=None
    for c in range(BLOCK//CH):
        sl=slice(c*CH,(c+1)*CH)
        s=dot(ka,qa[:,sl])+bias_ref[0,:,sl]
        p=jnp.exp(s-lse_ref[0,:,sl])
        pb=p.astype(BF16)
        dvc=dot(doT[:,sl],pb,NT)
        dp=dot(v,doT[:,sl])
        t=p*dp
        d=jnp.sum(t,axis=0,keepdims=True)
        ds=(t-p*d).astype(BF16)
        dq_ref[:,sl]=dot(kT,ds).astype(BF16)
        dkc=dot(q[:,sl],ds,NT)
        dk=dkc if dk is None else dk+dkc
        dv=dvc if dv is None else dv+dvc
        acc_ref[:,sl]+=ds.astype(F32)
    dk_ref[...]=dk.astype(BF16); dv_ref[...]=dv.astype(BF16)
    @pl.when(n==nb-1)
    def _():
        tot=None
        zero=jnp.zeros((128,BLOCK),F32)
        for g in range(4):
            x=jnp.concatenate([acc_ref[pl.ds(128*g,128),:],zero],1)
            y=pltpu.roll(x,(2*BLOCK-128*g)%(2*BLOCK),axis=1,stride=2*BLOCK-1,stride_axis=0)
            r=jnp.sum(y,axis=0,keepdims=True)
            tot=r if tot is None else tot+r
        t=lax.broadcasted_iota(jnp.int32,(1,2*BLOCK),1)
        rel=-jnp.where(t<BLOCK,t,t-2*BLOCK)
        b=bucket_of(rel)
        cc=lax.broadcasted_iota(jnp.int32,(BUCKETS,2*BLOCK),0)
        tab_ref[0]=jnp.broadcast_to(jnp.sum(jnp.where(b==cc,tot,0.0),axis=1,keepdims=True),(BUCKETS,128))
def bwd_call(flags,qkvT,doT,lse,bias,CH=256):
    T=qkvT.shape[1]; n=T//BLOCK
    sp=lambda off: pl.BlockSpec((HEAD_DIM,BLOCK),lambda h,n,f:(h+off,n))
    D=HEADS*HEAD_DIM
    return pl.pallas_call(functools.partial(bwd_kernel,CH=CH,nb=n),
        grid_spec=pltpu.PrefetchScalarGridSpec(num_scalar_prefetch=1,grid=(HEADS,n),
        in_specs=[sp(0),sp(HEADS),sp(2*HEADS),sp(0),pl.BlockSpec((1,1,BLOCK),lambda h,n,f:(h,0,n)),pl.BlockSpec((1,BLOCK,BLOCK),lambda h,n,f:(h,0,0))],
        out_specs=[sp(0),sp(0),sp(0),pl.BlockSpec((1,BUCKETS,128),lambda h,n,f:(h,0,0))],
        scratch_shapes=[pltpu.VMEM((BLOCK,BLOCK),F32)]),
        out_shape=[jax.ShapeDtypeStruct((D,T),BF16)]*3+[jax.ShapeDtypeStruct((HEADS,BUCKETS,128),F32)],
        name="attend_back",
        compiler_params=pltpu.CompilerParams(vmem_limit_bytes=48*2**20))(flags,qkvT,qkvT,qkvT,doT,lse,bias)

def fwd2_kernel(flags_ref,q_ref,k_ref,v_ref,bias_ref,o_ref,lse_ref,*,HP,mode):
    n=pl.program_id(1)
    qm,km=masks(flags_ref[n])
    S=[]
    for u in range(HP):
        r=slice(u*64,(u+1)*64)
        qa=jnp.concatenate([q_ref[r,:],qm],0)
        ka=jnp.concatenate([k_ref[r,:],km],0).T
        S.append(dot(ka,qa))
    for u in range(HP):
        r=slice(u*64,(u+1)*64)
        s=S[u]+bias_ref[u]
        m=jnp.max(s,axis=0,keepdims=True)
        e=jnp.exp(s-m)
        if mode=="def":
            l=jnp.sum(e,axis=0,keepdims=True)
            o_ref[r,:]=(dot(v_ref[r,:],e.astype(BF16))*(1.0/l)).astype(BF16)
        elif mode=="ones":
            va=jnp.concatenate([v_ref[r,:],jnp.ones((16,BLOCK),BF16)],0)
            oa=dot(va,e.astype(BF16))
            l=oa[64:65,:]
            o_ref[r,:]=(oa[:64]*(1.0/l)).astype(BF16)
        elif mode=="nomm":
            l=jnp.sum(e,axis=0,keepdims=True)
            o_ref[r,:]=e[:64].astype(BF16)
        else:
            l=jnp.sum(e,axis=0,keepdims=True)
            p=(e*(1.0/l)).astype(BF16)
            o_ref[r,:]=dot(v_ref[r,:],p).astype(BF16)
        lse_ref[u,:,:]=m+jnp.log(l)
def fwd2_call(flags,qkvT,bias,HP=2,mode="norm"):
    T=qkvT.shape[1]; n=T//BLOCK
    G=HEADS//HP
    sp=lambda off: pl.BlockSpec((HP*HEAD_DIM,BLOCK),lambda h,n,f:(h+off,n))
    return pl.pallas_call(functools.partial(fwd2_kernel,HP=HP,mode=mode),
        grid_spec=pltpu.PrefetchScalarGridSpec(num_scalar_prefetch=1,grid=(G,n),
        in_specs=[sp(0),sp(G),sp(2*G),pl.BlockSpec((HP,BLOCK,BLOCK),lambda h,n,f:(h,0,0))],
        out_specs=[pl.BlockSpec((HP*HEAD_DIM,BLOCK),lambda h,n,f:(h,n)),pl.BlockSpec((HP,1,BLOCK),lambda h,n,f:(h,0,n))]),
        out_shape=[jax.ShapeDtypeStruct((HEADS*HEAD_DIM,T),BF16),jax.ShapeDtypeStruct((HEADS,1,T),F32)],
        name="attend",
        compiler_params=pltpu.CompilerParams(vmem_limit_bytes=56*2**20))(flags,qkvT,qkvT,qkvT,bias)
def fwdN_kernel(flags_ref,q_ref,k_ref,v_ref,bias_ref,o_ref,lse_ref,*,HP):
    n=pl.program_id(1)
    qm,km=masks(flags_ref[n])
    for u in range(HP):
        r=slice(u*64,(u+1)*64)
        qa=jnp.concatenate([q_ref[r,:],qm],0)
        ka=jnp.concatenate([k_ref[r,:],km],0).T
        s=dot(ka,qa)+bias_ref[u]
        m=jnp.max(s,axis=0,keepdims=True)
        e=jnp.exp(s-m)
        l=jnp.sum(e,axis=0,keepdims=True)
        o=lax.dot_general(e.astype(BF16),v_ref[r,:],(((0,),(1,)),((),())),preferred_element_type=F32)
        o_ref[r,:]=(o.T*(1.0/l)).astype(BF16)
        lse_ref[u,:,:]=m+jnp.log(l)

def left_by_row(x,width):
    row=lax.broadcasted_iota(jnp.int32,x.shape,0)
    for b in range(7):
        y=pltpu.roll(x,width-(1<<b),axis=1)
        x=jnp.where((row>>b)&1==1,y,x)
    return x
def bwd2_kernel(flags_ref,q_ref,k_ref,v_ref,do_ref,lse_ref,bias_ref,g_ref,tab_ref,band_ref,far_ref,*,HP,nb,tabmode):
    n=pl.program_id(1)
    qm,km=masks(flags_ref[n])
    @pl.when(n==0)
    def _():
        band_ref[...]=jnp.zeros_like(band_ref); far_ref[...]=jnp.zeros_like(far_ref)
    R=[slice(u*64,(u+1)*64) for u in range(HP)]
    S=[];DP=[]
    for u in range(HP):
        r=R[u]
        qa=jnp.concatenate([q_ref[r,:],qm],0)
        ka=jnp.concatenate([k_ref[r,:],km],0).T
        S.append(dot(ka,qa))
        DP.append(dot(v_ref[r,:].T,do_ref[r,:]))
    for u in range(HP):
        r=R[u]
        p=jnp.exp(S[u]+bias_ref[u]-lse_ref[u])
        pb=p.astype(BF16)
        g_ref[2,r,:]=dot(do_ref[r,:],pb,NT).astype(BF16)
        t=p*DP[u]
        d=jnp.sum(t,axis=0,keepdims=True)
        dsf=t-p*d
        ds=dsf.astype(BF16)
        g_ref[0,r,:]=dot(k_ref[r,:],ds).astype(BF16)
        g_ref[1,r,:]=dot(q_ref[r,:],ds,NT).astype(BF16)
        if tabmode:
            lo=None;hi=None;bl=[None]*3
            for g in range(4):
                for c in range(4):
                    tile=dsf[128*g:128*(g+1),128*c:128*(c+1)]
                    w=c-g+1
                    if 0<=w<3:
                        bl[w]=tile if bl[w] is None else bl[w]+tile
                    elif w<0:
                        lo=tile if lo is None else lo+tile
                    else:
                        hi=tile if hi is None else hi+tile
            for w in range(3): band_ref[u,:,128*w:128*(w+1)]+=bl[w]
            far_ref[u,0]+=jnp.sum(lo.reshape(16,8,128),axis=0)
            far_ref[u,1]+=jnp.sum(hi.reshape(16,8,128),axis=0)
    @pl.when(n==nb-1)
    def _():
        t=lax.broadcasted_iota(jnp.int32,(1,BLOCK),1)
        b=bucket_of(-jnp.where(t<384,t-128,t-640))
        cc=lax.broadcasted_iota(jnp.int32,(BUCKETS,BLOCK),0)
        c1=lax.broadcasted_iota(jnp.int32,(BUCKETS,128),0)
        for u in range(HP):
            x=jnp.concatenate([band_ref[u],jnp.zeros((128,128),F32)],1)
            tot=jnp.sum(left_by_row(x,BLOCK),axis=0,keepdims=True)
            lo=jnp.sum(far_ref[u,0],axis=0,keepdims=True); hi=jnp.sum(far_ref[u,1],axis=0,keepdims=True)
            val=jnp.where(b==cc,tot,0.0)
            val=val[:,:128]+val[:,128:256]+val[:,256:384]+val[:,384:]
            val=val+jnp.where(c1==BUCKETS-1,lo,0.0)+jnp.where(c1==BUCKETS//2-1,hi,0.0)
            col=jnp.broadcast_to(jnp.sum(val,axis=1,keepdims=True),(BUCKETS,128))
            col=jnp.concatenate([col,jnp.zeros((128-BUCKETS,128),F32)],0)
            tab_ref[u]=col.T[:8]
def bwd2_call(flags,qkvT,doT,lse,bias,HP=2,tabmode=1):
    T=qkvT.shape[1]; n=T//BLOCK; G=HEADS//HP
    sp=lambda off: pl.BlockSpec((HP*HEAD_DIM,BLOCK),lambda h,n,f:(h+off,n))
    D=HEADS*HEAD_DIM
    return pl.pallas_call(functools.partial(bwd2_kernel,HP=HP,nb=n,tabmode=tabmode),
        grid_spec=pltpu.PrefetchScalarGridSpec(num_scalar_prefetch=1,grid=(G,n),
        in_specs=[sp(0),sp(G),sp(2*G),sp(0),pl.BlockSpec((HP,1,BLOCK),lambda h,n,f:(h,0,n)),pl.BlockSpec((HP,BLOCK,BLOCK),lambda h,n,f:(h,0,0))],
        out_specs=[pl.BlockSpec((3,HP*HEAD_DIM,BLOCK),lambda h,n,f:(0,h,n)),pl.BlockSpec((HP,8,128),lambda h,n,f:(h,0,0))],
        scratch_shapes=[pltpu.VMEM((HP,128,384),F32),pltpu.VMEM((HP,2,8,128),F32)]),
        out_shape=[jax.ShapeDtypeStruct((3,D,T),BF16),jax.ShapeDtypeStruct((HEADS,8,128),F32)],
        name="attend_back",
        compiler_params=pltpu.CompilerParams(vmem_limit_bytes=60*2**20))(flags,qkvT,qkvT,qkvT,doT,lse,bias)

D=768
norm_eps=1e-6
def rms(x): return lax.rsqrt(jnp.mean(x*x,axis=-1,keepdims=True)+norm_eps)
GA=128
def row_of(gains,which):
    return gains.astype(F32).T[which:which+1,:]
def qkv_kernel(x_ref,w_ref,aT_ref,qkvT_ref,wT_ref):
    @pl.when(pl.program_id(0)==0)
    def _():
        for c in range(3):
            wT_ref[pl.ds(c*D,D),:]=w_ref[:,c*D:(c+1)*D].T
    x=x_ref[...].astype(F32)
    g=row_of(w_ref[:,3*D:3*D+GA],0)
    a=(x*rms(x)*g).astype(BF16)
    aT=a.T
    aT_ref[...]=aT
    qkvT_ref[...]=dot(wT_ref[...],aT).astype(BF16)
def qkv_call(x,w):
    T=x.shape[0]
    return pl.pallas_call(qkv_kernel,grid=(T//BLOCK,),
        in_specs=[pl.BlockSpec((BLOCK,D),lambda t:(t,0)),pl.BlockSpec(w.shape,lambda t:(0,0),pipeline_mode=pl.Buffered(1))],
        out_specs=[pl.BlockSpec((D,BLOCK),lambda t:(0,t)),pl.BlockSpec((3*D,BLOCK),lambda t:(0,t))],
        out_shape=[jax.ShapeDtypeStruct((D,T),BF16),jax.ShapeDtypeStruct((3*D,T),BF16)],
        scratch_shapes=[pltpu.VMEM((3*D,D),BF16)],name="project",
        compiler_params=pltpu.CompilerParams(vmem_limit_bytes=56*2**20))(x,w)
def mid_kernel(x_ref,oT_ref,wo_ref,ga_ref,m_ref,b_ref,bT_ref,*_):
    o=oT_ref[...].T
    m=x_ref[...].astype(F32)+dot(o,wo_ref[...],NT)
    m_ref[...]=m
    b=(m*rms(m)*row_of(ga_ref[...],1)).astype(BF16)
    b_ref[...]=b
    bT_ref[0]=b.T
def mid_call(x,oT,woT,gains):
    T=x.shape[0]
    return pl.pallas_call(mid_kernel,grid=(T//BLOCK,),
        in_specs=[pl.BlockSpec((BLOCK,D),lambda t:(t,0)),pl.BlockSpec((D,BLOCK),lambda t:(0,t)),
                  pl.BlockSpec((D,D),lambda t:(0,woT[1])),pl.BlockSpec((D,GA),lambda t:(0,gains[1]))],
        out_specs=[pl.BlockSpec((BLOCK,D),lambda t:(t,0)),pl.BlockSpec((BLOCK,D),lambda t:(t,0)),pl.BlockSpec((1,D,BLOCK),lambda t:(t,0,0))],
        out_shape=[jax.ShapeDtypeStruct((T,D),F32),jax.ShapeDtypeStruct((T,D),BF16),jax.ShapeDtypeStruct((T//BLOCK,D,BLOCK),BF16)],
        name="middle",
        compiler_params=pltpu.CompilerParams(vmem_limit_bytes=48*2**20))(x,oT,woT[0],gains[0])
def gate(u,mode):
    if mode=="erf":
        P=0.5*(1.0+lax.erf(u*(0.5**0.5)))
        z=jnp.exp(-0.5*u*u)
    else:
        z=jnp.exp(-0.5*u*u)
        t=1.0/(1.0+(0.3275911*0.5**0.5)*jnp.abs(u))
        q=((((0.5*1.061405429*t-0.5*1.453152027)*t+0.5*1.421413741)*t-0.5*0.284496736)*t+0.5*0.254829592)*t*z
        P=jnp.where(u>=0,1.0-q,q)
    return u*P, P+u*z*(2*math.pi)**-0.5
def ffn_kernel(b_ref,bT_ref,dy_ref,m_ref,win_ref,wout_ref,out_ref,db_ref,dw_ref,
               oacc,dacc,dyT,ain,aout,*,FC,SUB,nc,nt,mode,TB,order):
    c=pl.program_id(0); t=pl.program_id(1)
    rows=pl.ds(t*TB,TB)
    @pl.when(c==0)
    def _():
        oacc[rows,:]=m_ref[...]
        dacc[rows,:]=jnp.zeros((TB,D),F32)
        dyT[t]=dy_ref[rows,:].T
    b=b_ref[rows,:]; dy=dy_ref[rows,:]
    G=[];DU=[]
    U=[dot(b,win_ref[:,s*SUB:(s+1)*SUB]) for s in range(FC//SUB)]
    DG=[dot(dy,wout_ref[:,s*SUB:(s+1)*SUB]) for s in range(FC//SUB)]
    @pl.when(t==0)
    def _():
        ain[...]=jnp.zeros_like(ain); aout[...]=jnp.zeros_like(aout)
    for s in range(FC//SUB):
        g,pull=gate(U[s],mode)
        g=g.astype(BF16)
        du=(DG[s]*pull).astype(BF16)
        sl=slice(s*SUB,(s+1)*SUB)
        aout[:,sl]+=dot(dyT[t],g)
        ain[:,sl]+=dot(bT_ref[t],du)
        G.append(g);DU.append(du)
    g=jnp.concatenate(G,1);du=jnp.concatenate(DU,1)
    oacc[rows,:]+=dot(g,wout_ref[...],NT)
    dacc[rows,:]+=dot(du,win_ref[...],NT)
    @pl.when(t==nt-1)
    def _():
        dw_ref[:,:FC]=ain[...].astype(BF16)
        dw_ref[:,FC:]=aout[...].astype(BF16)
    @pl.when(c==nc-1)
    def _():
        out_ref[...]=oacc[rows,:].astype(BF16)
        db_ref[...]=dacc[rows,:]
def ffn_call(b,bT,dy,m,win,wout,FC=768,SUB=256,mode="erf",TB=512,order=0):
    T=b.shape[0]; nt=T//TB; FF=3072; nc=FF//FC
    bT3=bT
    last=lambda c,t:(jnp.where(c==nc-1,t,0),0)
    first=lambda c,t:(jnp.where(c==0,t,nt-1),0)
    one=pl.Buffered(1)
    return pl.pallas_call(functools.partial(ffn_kernel,FC=FC,SUB=SUB,nc=nc,nt=nt,mode=mode,TB=TB,order=order),grid=(nc,nt),
        in_specs=[pl.BlockSpec((T,D),lambda c,t:(0,0),pipeline_mode=one),pl.BlockSpec((nt,D,TB),lambda c,t:(0,0,0),pipeline_mode=one),
            pl.BlockSpec((T,D),lambda c,t:(0,0),pipeline_mode=one),
            pl.BlockSpec((TB,D),first),pl.BlockSpec((D,FC),lambda c,t:(0,c+win[1]*D//FC)),pl.BlockSpec((D,FC),lambda c,t:(0,c+wout[1]*D//FC))],
        out_specs=[pl.BlockSpec((TB,D),last),pl.BlockSpec((TB,D),last),pl.BlockSpec((D,2*FC),lambda c,t:(0,c))],
        out_shape=[jax.ShapeDtypeStruct((T,D),BF16),jax.ShapeDtypeStruct((T,D),F32),jax.ShapeDtypeStruct((D,2*FF),BF16)],
        scratch_shapes=[pltpu.VMEM((T,D),F32),pltpu.VMEM((T,D),F32),pltpu.VMEM((nt,D,TB),BF16),pltpu.VMEM((D,FC),F32),pltpu.VMEM((D,FC),F32)],
        name="feed_forward",
        compiler_params=pltpu.CompilerParams(vmem_limit_bytes=62*2**20))(b,bT3,dy,m,win[0],wout[0])

def post_kernel(dy_ref,db_ref,m_ref,oT_ref,wo_ref,ga_ref,dm_ref,doT_ref,dwo_ref,acc_ref,*,nt):
    t=pl.program_id(0)
    @pl.when(t==0)
    def _():
        acc_ref[...]=jnp.zeros_like(acc_ref)
    m=m_ref[...]; db=db_ref[...]
    r=rms(m); n2=m*r
    dn=db*row_of(ga_ref[...],1)
    dm=dy_ref[...].astype(F32)+r*(dn-n2*jnp.mean(dn*n2,axis=-1,keepdims=True))
    dm_ref[...]=dm
    dmb=dm.astype(BF16)
    acc_ref[...]+=dot(dmb.T,oT_ref[...],NT)
    doT_ref[...]=dot(dmb,wo_ref[...]).astype(BF16).T
    @pl.when(t==nt-1)
    def _(): dwo_ref[...]=acc_ref[...].astype(BF16)
def post_call(dy,db,m,oT,woT,gains):
    T=dy.shape[0]; nt=T//BLOCK
    row=pl.BlockSpec((BLOCK,D),lambda t:(t,0)); col=pl.BlockSpec((D,BLOCK),lambda t:(0,t))
    return pl.pallas_call(functools.partial(post_kernel,nt=nt),grid=(nt,),
        in_specs=[row,row,row,col,pl.BlockSpec((D,D),lambda t:(0,woT[1])),pl.BlockSpec((D,GA),lambda t:(0,gains[1]))],
        out_specs=[row,col,pl.BlockSpec((D,D),lambda t:(0,0))],
        out_shape=[jax.ShapeDtypeStruct((T,D),F32),jax.ShapeDtypeStruct((D,T),BF16),jax.ShapeDtypeStruct((D,D),BF16)],
        scratch_shapes=[pltpu.VMEM((D,D),F32)],name="middle_back",
        compiler_params=pltpu.CompilerParams(vmem_limit_bytes=48*2**20))(dy,db,m,oT,woT[0],gains[0])
def last_kernel(x_ref,dm_ref,g_ref,w_ref,dx_ref):
    da=None
    for c in range(3):
        z=dot(w_ref[:,c*D:(c+1)*D],g_ref[c])
        da=z if da is None else da+z
    da=da.T
    x=x_ref[...].astype(F32)
    r=rms(x); n1=x*r
    dn=da*row_of(w_ref[:,3*D:3*D+GA],0)
    dx_ref[...]=(dm_ref[...]+r*(dn-n1*jnp.mean(dn*n1,axis=-1,keepdims=True))).astype(BF16)
def last_call(x,dm,gT,w):
    T=x.shape[0]; nt=T//BLOCK
    row=pl.BlockSpec((BLOCK,D),lambda t:(t,0))
    return pl.pallas_call(last_kernel,grid=(nt,),
        in_specs=[row,row,pl.BlockSpec((3,D,BLOCK),lambda t:(0,0,t)),pl.BlockSpec(w.shape,lambda t:(0,0),pipeline_mode=pl.Buffered(1))],
        out_specs=row,out_shape=jax.ShapeDtypeStruct((T,D),BF16),name="project_back",
        cost_estimate=pl.CostEstimate(flops=2*T*D*3*D,bytes_accessed=20*T*D,transcendentals=0),
        compiler_params=pltpu.CompilerParams(vmem_limit_bytes=56*2**20))(x,dm,gT,w)

def block_kernel(at_ref,x_ref,oT_ref,dy_ref,ga_ref,wo_ref,win_ref,wout_ref,
                 out_ref,dm_ref,doT_ref,dwo_ref,*rest,FC,SUB,nc,nt,legs):
    dw_ref,b_s,oacc,dacc,ain,aout,awo,m_s=rest
    c=pl.program_id(0); t=pl.program_id(1)
    rows=pl.ds(t*BLOCK,BLOCK)
    def middle():
        return x_ref[...].astype(F32)+dot(oT_ref[...].T,wo_ref[...],NT)
    @pl.when(t==0)
    def _():
        ain[...]=jnp.zeros_like(ain); aout[...]=jnp.zeros_like(aout)
    @pl.when((c==nc-1)&(t==0))
    def _(): awo[...]=jnp.zeros_like(awo)
    n=FC//SUB
    def inner(dy):
        return [dot(dy,wout_ref[:,s*SUB:(s+1)*SUB]) for s in range(n)]
    def gates(b,DG):
        U=[dot(b,win_ref[:,s*SUB:(s+1)*SUB]) for s in range(n)]
        G=[];DU=[]
        for s in range(n):
            g,pull=gate(U[s],"erf")
            G.append(g.astype(BF16)); DU.append((DG[s]*pull).astype(BF16))
        return G,DU
    def sums(bt,dyt,G,DU):
        for s in range(n):
            sl=slice(s*SUB,(s+1)*SUB)
            aout[:,sl]+=dot(dyt,G[s])
            ain[:,sl]+=dot(bt,DU[s])
    def outer(G,DU):
        return dot(jnp.concatenate(G,1),wout_ref[...],NT),dot(jnp.concatenate(DU,1),win_ref[...],NT)
    @pl.when(c==0)
    def _():
        dy=dy_ref[...]
        DG=inner(dy)
        m=middle()
        b=(m*rms(m)*row_of(ga_ref[...],1)).astype(BF16)
        b_s[t]=b
        m_s[rows,:]=m
        G,DU=gates(b,DG)
        o,d=outer(G,DU)
        sums(b.T,dy.T,G,DU)
        oacc[rows,:]=m+o
        dacc[rows,:]=d
    @pl.when((c>0)&(c<nc-1))
    def _():
        dy=dy_ref[...]; b=b_s[t]
        G,DU=gates(b,inner(dy))
        sums(b.T,dy.T,G,DU)
        o,d=outer(G,DU)
        oacc[rows,:]+=o
        dacc[rows,:]+=d
    @pl.when(c==nc-1)
    def _():
        dy=dy_ref[...]; b=b_s[t]
        G,DU=gates(b,inner(dy))
        o,d=outer(G,DU)
        db=dacc[rows,:]+d
        out_ref[...]=(oacc[rows,:]+o).astype(BF16)
        sums(b.T,dy.T,G,DU)
        m=m_s[rows,:]
        r=rms(m); n2=m*r
        dn=db*row_of(ga_ref[...],1)
        dm=dy.astype(F32)+r*(dn-n2*jnp.mean(dn*n2,axis=-1,keepdims=True))
        dm_ref[...]=dm
        dmb=dm.astype(BF16)
        awo[...]+=dot(dmb.T,oT_ref[...],NT)
        doT_ref[...]=dot(dmb,wo_ref[...]).astype(BF16).T
    @pl.when(t==nt-1)
    def _():
        if legs:
            R=dw_ref.shape[1]
            for s in range(32):
                z=at_ref[0]^((s>>1)&1)^((s&1)<<1)
                at=pl.ds(pl.multiple_of((z*8+(s>>2))*R,8),R)
                dw_ref[s,:,:FC]=ain[at,:].astype(BF16)
                dw_ref[s,:,FC:]=aout[at,:].astype(BF16)
        else:
            dw_ref[:,:FC]=ain[...].astype(BF16)
            dw_ref[:,FC:]=aout[...].astype(BF16)
    @pl.when((c==nc-1)&(t==nt-1))
    def _(): dwo_ref[...]=awo[...].astype(BF16)
def block_call(x,oT,dy,gains,wo,win,wout,core,legs,FC=768,SUB=256):
    T=x.shape[0]; nt=T//BLOCK; FF=3072; nc=FF//FC
    last=lambda c,t:jnp.where(c==nc-1,t,0)
    first=lambda c,t:jnp.where(c==0,t,nt-1)
    ends=lambda c,t:jnp.where((c==0)|(c==nc-1),t,nt-1)
    one=pl.Buffered(1)
    sd=jax.ShapeDtypeStruct; BS=pl.BlockSpec; R=D//32
    return pl.pallas_call(functools.partial(block_kernel,FC=FC,SUB=SUB,nc=nc,nt=nt,legs=legs),
        grid_spec=pltpu.PrefetchScalarGridSpec(num_scalar_prefetch=1,grid=(nc,nt),
        in_specs=[BS((BLOCK,D),lambda c,t,at:(first(c,t),0)),BS((D,BLOCK),lambda c,t,at:(0,ends(c,t))),
            BS((BLOCK,D),lambda c,t,at:(t,0)),
            BS((D,GA),lambda c,t,at:(0,gains[1]),pipeline_mode=one),BS((D,D),lambda c,t,at:(0,wo[1]),pipeline_mode=one),
            BS((D,FC),lambda c,t,at:(0,c+win[1])),BS((D,FC),lambda c,t,at:(0,c+wout[1]))],
        out_specs=[BS((BLOCK,D),lambda c,t,at:(last(c,t),0)),BS((BLOCK,D),lambda c,t,at:(last(c,t),0)),BS((D,BLOCK),lambda c,t,at:(0,last(c,t))),
            BS((D,D),lambda c,t,at:(0,0),pipeline_mode=one)]+([BS((32,R,2*FC),lambda c,t,at:(0,0,c))] if legs else [BS((D,2*FC),lambda c,t,at:(0,c))]),
        scratch_shapes=[pltpu.VMEM((nt,BLOCK,D),BF16),
            pltpu.VMEM((T,D),F32),pltpu.VMEM((T,D),F32),pltpu.VMEM((D,FC),F32),pltpu.VMEM((D,FC),F32),pltpu.VMEM((D,D),F32),pltpu.VMEM((T,D),F32)]),
        out_shape=[sd((T,D),BF16),sd((T,D),F32),sd((D,T),BF16),sd((D,D),BF16)]+([sd((32,R,2*FF),BF16)] if legs else [sd((D,2*FF),BF16)]),
        name="feed_forward",
        compiler_params=pltpu.CompilerParams(vmem_limit_bytes=62*2**20+2**19))(core,x,oT,dy,gains[0],wo[0],win[0],wout[0])

GW=3*D+GA
INNER=("yx","core")
def pack_a_kernel(q_ref,k_ref,v_ref,g1_ref,g2_ref,o_ref):
    for c,ref in enumerate((q_ref,k_ref,v_ref)):
        o_ref[:,c*D:(c+1)*D]=ref[...].astype(BF16)
    rows=o_ref.shape[0]
    g=jnp.concatenate([g1_ref[...],g2_ref[...],jnp.zeros((GA-2,rows),F32)],0)
    o_ref[:,3*D:]=g.T.astype(BF16)
def pack_a(q,k,v,g1,g2):
    return pl.pallas_call(pack_a_kernel,out_shape=jax.ShapeDtypeStruct((q.shape[0],GW),BF16),name="pack_attention")(q,k,v,g1[None],g2[None])
def pack_b_kernel(wo_ref,wi_ref,wu_ref,o_ref):
    F=wi_ref.shape[1]
    o_ref[:,:F]=wi_ref[...].astype(BF16)
    o_ref[:,F:2*F]=wu_ref[...].astype(BF16)
    o_ref[:,2*F:]=wo_ref[...].astype(BF16)
def pack_b(wo,wi,wu):
    return pl.pallas_call(pack_b_kernel,out_shape=jax.ShapeDtypeStruct((wi.shape[0],D+2*wi.shape[1]),BF16),name="pack_feed_forward")(wo.T,wi,wu.T)

def swap(x,axis,mask):
    n=8 if axis==INNER else 4
    f=mask if callable(mask) else (lambda i:mask)
    return lax.ppermute(x,axis,[(i,i^f(i)) for i in range(n)])
first_leg=lambda i: 4 if i&1 else 2
second_leg=lambda i: 2 if i&1 else 4
def gather_pieces(shard,beside):
    a=shard[None]
    a=jnp.concatenate([a,swap(a,"dp",2)],0)
    got=swap(a,"dp",1)
    got,beside=lax.optimization_barrier((got,beside))
    a=jnp.concatenate([a,got],0)
    a=jnp.concatenate([a,swap(a,INNER,first_leg)],0)
    b=swap(a,INNER,second_leg)
    c=swap(a,INNER,1)
    d=swap(b,INNER,1)
    return (a,b,c,d),beside
def place():
    f=lax.axis_index(INNER); z=lax.axis_index("dp")
    return jnp.stack([f,z]).astype(jnp.int32)
def assemble_rows(at_ref,pieces,put):
    f=at_ref[0]; z=at_ref[1]
    core=f&1; x=(f>>1)&1; y=f>>2
    for j in range(16):
        zj,yj,xj=j>>2,(j>>1)&1,j&1
        dz=zj^z; dx=xj^x; dy=yj^y
        low=(dz&1)*2+(dz>>1)
        halves=[]
        for cj in range(2):
            far_core=core^cj
            one=jnp.where(cj==0,dx,dy)
            two=jnp.where(cj==0,dy,dx)
            slot=one*4+low
            which=far_core*2+two
            halves.append((which,slot))
        put(j,halves)
def project2_kernel(at_ref,x_ref,a_ref,b_ref,c_ref,d_ref,aT_ref,qkvT_ref,w_ref,all_ref,wT_ref):
    R=a_ref.shape[1]
    @pl.when(pl.program_id(0)==0)
    def _():
        for i,ref in enumerate((a_ref,b_ref,c_ref,d_ref)): all_ref[pl.ds(8*i,8)]=ref[...]
        def put(j,halves):
            v=jnp.concatenate([all_ref[w*8+s].astype(F32) for w,s in halves],0)
            w_ref[pl.ds(j*2*R,2*R),:]=v.astype(BF16)
        assemble_rows(at_ref,None,put)
        for c in range(3):
            wT_ref[pl.ds(c*D,D),:]=w_ref[:,c*D:(c+1)*D].T
    x=x_ref[...].astype(F32)
    g=row_of(w_ref[:,3*D:3*D+GA],0)
    a=(x*rms(x)*g).astype(BF16)
    aT=a.T
    aT_ref[...]=aT
    qkvT_ref[...]=dot(wT_ref[...],aT).astype(BF16)
def project2_call(x,pieces,at):
    T=x.shape[0]; R=pieces[0].shape[1]
    one=pl.Buffered(1)
    ps=pl.BlockSpec((8,R,GW),lambda t,at:(0,0,0),pipeline_mode=one)
    return pl.pallas_call(project2_kernel,
        grid_spec=pltpu.PrefetchScalarGridSpec(num_scalar_prefetch=1,grid=(T//BLOCK,),
        in_specs=[pl.BlockSpec((BLOCK,D),lambda t,at:(t,0)),ps,ps,ps,ps],
        out_specs=[pl.BlockSpec((D,BLOCK),lambda t,at:(0,t)),pl.BlockSpec((3*D,BLOCK),lambda t,at:(0,t)),pl.BlockSpec((D,GW),lambda t,at:(0,0))],
        scratch_shapes=[pltpu.VMEM((32,R,GW),BF16),pltpu.VMEM((3*D,D),BF16)]),
        out_shape=[jax.ShapeDtypeStruct((D,T),BF16),jax.ShapeDtypeStruct((3*D,T),BF16),jax.ShapeDtypeStruct((D,GW),BF16)],
        name="project",
        compiler_params=pltpu.CompilerParams(vmem_limit_bytes=60*2**20))(at,x,*pieces)


def add(a,b): return (a.astype(F32)+b.astype(F32)).astype(BF16)
GN=4*D+128
def slot_rows(s,f,z,core):
    x=(f>>1)&1; y=f>>2
    one=s>>3; two=(s>>2)&1
    dx=jnp.where(core==0,one,two); dy=jnp.where(core==0,two,one)
    zz=z^((s>>1)&1)^((s&1)<<1)
    return (zz*8+(y^dy)*4+(x^dx)*2+core)
def slot_table():
    f=lax.axis_index(INNER); z=lax.axis_index("dp")
    s=jnp.arange(16,dtype=jnp.int32); core=f&1
    return jnp.stack([slot_rows(s,f,z,core),slot_rows(s,f,z,1-core)]).astype(jnp.int32)
def grads_kernel(at_ref,aT_ref,g_ref,wo_ref,tab_ref,keep_ref,send_ref,v_ref):
    c=pl.program_id(0)
    R=keep_ref.shape[1]
    @pl.when(c<3)
    def _(): v_ref[...]=dot(aT_ref[...],g_ref[0],NT)
    @pl.when(c==3)
    def _(): v_ref[...]=wo_ref[...].astype(F32)
    @pl.when(c<4)
    def _():
        for s in range(16):
            for q,ref in enumerate((keep_ref,send_ref)):
                ref[s]=v_ref[pl.ds(pl.multiple_of(at_ref[q,s]*R,8),R),:].astype(BF16)
    @pl.when(c==4)
    def _():
        t=jnp.concatenate([tab_ref[h,:1,:] for h in range(HEADS)]+[jnp.zeros((R-HEADS,128),F32)],0).astype(BF16)
        for s in range(16):
            keep_ref[s,:,:128]=t; send_ref[s,:,:128]=t
def grads_call(at,aT,gT,dwoT,tab):
    T=aT.shape[1]; R=D//32
    out=pl.BlockSpec((16,R,D),lambda c,at:(0,0,c))
    return pl.pallas_call(grads_kernel,
        grid_spec=pltpu.PrefetchScalarGridSpec(num_scalar_prefetch=1,grid=(5,),
        in_specs=[pl.BlockSpec((D,T),lambda c,at:(0,0),pipeline_mode=pl.Buffered(1)),
                  pl.BlockSpec((1,D,T),lambda c,at:(jnp.minimum(c,2),0,0)),
                  pl.BlockSpec((D,D),lambda c,at:(0,0),pipeline_mode=pl.Buffered(1)),
                  pl.BlockSpec((HEADS,8,128),lambda c,at:(0,0,0))],
        out_specs=[out,out],scratch_shapes=[pltpu.VMEM((D,D),F32)]),
        out_shape=[jax.ShapeDtypeStruct((16,R,GN),BF16)]*2,name="weight_grads",
        compiler_params=pltpu.CompilerParams(vmem_limit_bytes=48*2**20))(at,aT,gT,dwoT,tab)
def scatter_sum(keep,send,beside,other,rest):
    r=swap(send,INNER,1)
    for half,axis,leg in ((8,INNER,first_leg),(4,INNER,second_leg),(2,"dp",1),(1,"dp",2)):
        out=add(keep[half:],r[half:])
        keep=add(keep[:half],r[:half])
        r=swap(out,axis,leg)
        if half==8:
            r,beside,other=lax.optimization_barrier((r,beside,other))
            late=rest[0](other)
        if half==2:
            r,late=lax.optimization_barrier((r,late))
            late=rest[1](late)
    r,late=lax.optimization_barrier((r,late))
    return keep[0],r[0],beside,late
def finish_kernel(a_ref,b_ref,wq_ref,wk_ref,wv_ref,g_ref,q_ref,k_ref,v_ref,o_ref,tab_ref,dg_ref):
    R=a_ref.shape[0]
    tot=None
    for c,(w,out) in enumerate(((wq_ref,q_ref),(wk_ref,k_ref),(wv_ref,v_ref),(None,o_ref))):
        sl=slice(c*D,(c+1)*D)
        s=a_ref[:,sl].astype(F32)+b_ref[:,sl].astype(F32)
        out[...]=s
        if w is not None:
            y=jnp.sum(s*w[...].astype(BF16).astype(F32),axis=1,keepdims=True)
            tot=y if tot is None else tot+y
    t=a_ref[:,4*D:4*D+128].astype(F32)+b_ref[:,4*D:4*D+128].astype(F32)
    tab_ref[...]=t[:HEADS,:BUCKETS]
    rowv=jnp.broadcast_to(tot,(R,128))
    rowv=jnp.concatenate([rowv,jnp.zeros((128-R,128),F32)],0).T[:1,:R]
    dg_ref[...]=rowv/g_ref[...].astype(BF16).astype(F32)
def finish_call(a,b,wq,wk,wv,g1):
    R=a.shape[0]; sd=jax.ShapeDtypeStruct
    return pl.pallas_call(finish_kernel,out_shape=[sd((R,D),F32)]*4+[sd((HEADS,BUCKETS),F32),sd((1,R),F32)],name="finish_attention")(a,b,wq,wk,wv,g1[None])
def finish_ffn_kernel(s_ref,t_ref,w_ref,g_ref,i_ref,o_ref,dg_ref,*,FC):
    R=s_ref.shape[0]
    tot=None
    for c in range(w_ref.shape[1]//FC):
        sl=slice(c*FC,(c+1)*FC)
        one=slice(2*c*FC,(2*c+1)*FC); two=slice((2*c+1)*FC,(2*c+2)*FC)
        s=s_ref[:,one].astype(F32)+t_ref[:,one].astype(F32)
        i_ref[:,sl]=s
        o_ref[:,sl]=s_ref[:,two].astype(F32)+t_ref[:,two].astype(F32)
        y=jnp.sum(s*w_ref[:,sl].astype(BF16).astype(F32),axis=1,keepdims=True)
        tot=y if tot is None else tot+y
    rowv=jnp.broadcast_to(tot,(R,128))
    rowv=jnp.concatenate([rowv,jnp.zeros((128-R,128),F32)],0).T[:1,:R]
    dg_ref[...]=rowv/g_ref[...].astype(BF16).astype(F32)
def finish_ffn_call(s,t,w,g2,FC):
    R,F=w.shape; sd=jax.ShapeDtypeStruct
    return pl.pallas_call(functools.partial(finish_ffn_kernel,FC=FC),out_shape=[sd((R,F),F32),sd((R,F),F32),sd((1,R),F32)],name="finish_feed_forward")(s,t,w,g2[None])

BOTH=("dp","fsdp")
ALL=("dp","yx","core")
FC=768
def low(v): return v.astype(BF16).astype(F32)
def body(sizes,hidden,long_flags,norm1_gain,query_w,key_w,value_w,out_w,bias_table,norm2_gain,ffn_in,ffn_out,out_grad):
    rows=norm1_gain.shape[0]
    FF=ffn_in.shape[1]
    legs=sizes==(4,8)
    if legs:
        pa=pack_a(query_w,key_w,value_w,norm1_gain,norm2_gain)
        pb=pack_b(out_w,ffn_in,ffn_out)
        wb=lax.all_gather(pb,ALL,axis=0,tiled=True)
        at=place()
        pieces,bias=gather_pieces(pa,bias_call(bias_table))
        aT,qkvT,wa=project2_call(hidden,pieces,at)
    else:
        bias=bias_call(bias_table)
        gains=jnp.concatenate([norm1_gain[:,None],norm2_gain[:,None],jnp.zeros((rows,GA-2),F32)],1)
        pa=jnp.concatenate([query_w,key_w,value_w,gains],1).astype(BF16)
        pb=jnp.concatenate([ffn_in,ffn_out.T,out_w.T],1).astype(BF16)
        wa=lax.all_gather(pa,BOTH,axis=0,tiled=True)
        wb=lax.all_gather(pb,BOTH,axis=0,tiled=True)
        aT,qkvT=qkv_call(hidden,wa)
    oT,lse=fwd2_call(long_flags,qkvT,bias,HP=4,mode="ones")
    GB=3*D//GA
    z=(lax.axis_index("dp") if legs else jnp.zeros((),jnp.int32)).reshape(1)
    out,dm,doT,dwoT,dffn=block_call(hidden,oT,out_grad,(wa,GB),(wb,2*FF//D),(wb,0),(wb,FF//FC),z,legs,FC=FC)
    def rs(x,axes=BOTH): return lax.psum_scatter(x,axes,scatter_dimension=0,tiled=True)
    fsum=rs(dffn.reshape(D,2*FF),INNER if legs else BOTH)
    gT,tab=bwd2_call(long_flags,qkvT,doT,lse,bias,HP=4)
    if legs:
        keep,send=grads_call(slot_table(),aT,gT,dwoT,tab)
        h=fsum.reshape(4,rows,2*FF)
        h,dm=lax.optimization_barrier((h,dm))
        r=swap(h[2:],"dp",1)
        rest=(lambda r:(add(h[0],r[0]),swap(add(h[1],r[1]),"dp",2)),lambda z:finish_ffn_call(*z,ffn_in,norm2_gain,FC))
        a,b2,dx,(di,du,dg2)=scatter_sum(keep,send,last_call(hidden,dm,gT,wa),r,rest)
        dq,dk,dv,do,table,dg1=finish_call(a,b2,query_w,key_w,value_w,norm1_gain)
        dg1=dg1[0]; dg2=dg2[0]; table=table.T
    else:
        dx=last_call(hidden,dm,gT,wa)
        tabs=tab[:,0,:BUCKETS].reshape(-1)
        wide=tabs.shape[0]//rows
        tb=jnp.tile(tabs.reshape(rows,wide),(D//rows,1))
        parts=[lax.dot_general(aT,gT[c],NT,preferred_element_type=F32).astype(BF16) for c in range(3)]
        asum=rs(jnp.concatenate(parts+[dwoT,tb.astype(BF16)],1)).astype(F32)
        dq,dk,dv,do=[asum[:,c*D:(c+1)*D] for c in range(4)]
        table=asum[:,4*D:].reshape(HEADS,BUCKETS).T
        f=fsum.astype(F32).reshape(rows,FF//FC,2,FC)
        di=f[:,:,0].reshape(rows,FF); du=f[:,:,1].reshape(rows,FF)
        dg1=jnp.sum(dq*low(query_w)+dk*low(key_w)+dv*low(value_w),axis=1)/low(norm1_gain)
        dg2=jnp.sum(di*low(ffn_in),axis=1)/low(norm2_gain)
    return (out,dx,dg1,dq,dk,dv,do.T,table,dg2,di,du.T)

def solution(mesh):
    P=jax.sharding.PartitionSpec
    sizes=(mesh.shape["dp"],mesh.shape["fsdp"])
    axes=BOTH
    if sizes==(4,8):
        mesh=jax.sharding.Mesh(mesh.devices.reshape(4,4,2),ALL)
        axes=ALL
    r=P(axes,None); v=P(axes); c=P(None,axes)
    return jax.shard_map(functools.partial(body,sizes),mesh=mesh,in_specs=(r,v,v,r,r,r,c,P(),v,r,c,r),out_specs=(r,r,v,r,r,r,c,P(),v,r,c),check_vma=False)
```

```python
import math, functools
import jax, jax.numpy as jnp
from jax import lax
from jax.experimental import pallas as pl
from jax.experimental.pallas import tpu as pltpu
HEADS=12; HEAD_DIM=64; BUCKETS=32; MAX_DIST=128; BLOCK=512; LONG=500; SHORT=250
F32=jnp.float32; BF16=jnp.bfloat16
far=-2.0**30
NN=(((1,),(0,)),((),())); NT=(((1,),(1,)),((),())); TN=(((0,),(0,)),((),()))
def dot(a,b,dn=NN): return lax.dot_general(a,b,dn,preferred_element_type=F32)

def bucket_limits():
    exact_count = BUCKETS // 4
    half_count = BUCKETS // 2
    scale_log = math.log(MAX_DIST / exact_count)
    thresholds = []
    for target in range(1, half_count - exact_count):
        distance = exact_count
        while int(math.log(distance / exact_count) / scale_log * (half_count - exact_count)) < target:
            distance += 1
        thresholds.append(distance)
    return thresholds
def bucket_of(relative):
    distance=jnp.abs(relative)
    exact=BUCKETS//4
    beyond=jnp.full_like(distance,exact)
    for t in bucket_limits():
        beyond=beyond+jnp.where(distance>=t,1,0)
    inside=jnp.where(distance<exact,distance,beyond)
    return inside+jnp.where(relative>0,BUCKETS//2,0)

def bias_kernel(tT_ref, out_ref, ext_ref):
    h=pl.program_id(0)
    @pl.when(h==0)
    def _():
        t=lax.broadcasted_iota(jnp.int32,(1,2*BLOCK),1)
        rel=-jnp.where(t<BLOCK,t,t-2*BLOCK)
        b=bucket_of(rel)
        acc=jnp.zeros((HEADS,2*BLOCK),F32)
        for c in range(BUCKETS):
            acc=jnp.where(b==c,tT_ref[:,c:c+1],acc)
        ext_ref[...]=acc
    row=ext_ref[pl.ds(h,1),:]
    for s in range(4):
        x=jnp.broadcast_to(row,(128,2*BLOCK))
        y=pltpu.roll(x,128*s,axis=1,stride=1,stride_axis=0)
        out_ref[0,pl.ds(128*s,128),:]=y[:,:BLOCK]
def bias_call(table):
    return pl.pallas_call(bias_kernel,grid=(HEADS,),
        in_specs=[pl.BlockSpec((HEADS,BUCKETS),lambda h:(0,0))],
        out_specs=pl.BlockSpec((1,BLOCK,BLOCK),lambda h:(h,0,0)),
        out_shape=jax.ShapeDtypeStruct((HEADS,BLOCK,BLOCK),F32),
        scratch_shapes=[pltpu.VMEM((HEADS,2*BLOCK),F32)],name="bias")(table.T)

def seg_ids(flag):
    s=lax.broadcasted_iota(jnp.int32,(1,BLOCK),1)
    long_ids=jnp.where(s>=LONG,1,0)
    short_ids=jnp.where(s>=SHORT,1,0)+jnp.where(s>=2*SHORT,1,0)
    return jnp.where(flag==1,long_ids,short_ids)
def masks(flag):
    seg=seg_ids(flag)
    c=lax.broadcasted_iota(jnp.int32,(HEAD_DIM,BLOCK),0)
    qm=jnp.where(seg==c,1.0,0.0).astype(BF16)
    km=jnp.where((seg!=c)&(c<3),far,0.0).astype(BF16)
    return qm,km

def fwd_kernel(flags_ref,q_ref,k_ref,v_ref,bias_ref,o_ref,lse_ref,*,CH):
    n=pl.program_id(1)
    qm,km=masks(flags_ref[n])
    qa=jnp.concatenate([q_ref[...],qm],0)
    ka=jnp.concatenate([k_ref[...],km],0).T
    vT=v_ref[...]
    for c in range(BLOCK//CH):
        sl=slice(c*CH,(c+1)*CH)
        s=dot(ka,qa[:,sl])+bias_ref[0,:,sl]
        m=jnp.max(s,axis=0,keepdims=True)
        e=jnp.exp(s-m)
        l=jnp.sum(e,axis=0,keepdims=True)
        p=(e*(1.0/l)).astype(BF16)
        o_ref[:,sl]=dot(vT,p).astype(BF16)
        lse_ref[0,:,sl]=m+jnp.log(l)
def fwd_call(flags,qkvT,bias,CH=256):
    T=qkvT.shape[1]; n=T//BLOCK
    sp=lambda off: pl.BlockSpec((HEAD_DIM,BLOCK),lambda h,n,f:(h+off,n))
    return pl.pallas_call(functools.partial(fwd_kernel,CH=CH),
        grid_spec=pltpu.PrefetchScalarGridSpec(num_scalar_prefetch=1,grid=(HEADS,n),
        in_specs=[sp(0),sp(HEADS),sp(2*HEADS),pl.BlockSpec((1,BLOCK,BLOCK),lambda h,n,f:(h,0,0))],
        out_specs=[pl.BlockSpec((HEAD_DIM,BLOCK),lambda h,n,f:(h,n)),pl.BlockSpec((1,1,BLOCK),lambda h,n,f:(h,0,n))]),
        out_shape=[jax.ShapeDtypeStruct((HEADS*HEAD_DIM,T),BF16),jax.ShapeDtypeStruct((HEADS,1,T),F32)],
        name="attend",
        compiler_params=pltpu.CompilerParams(vmem_limit_bytes=48*2**20))(flags,qkvT,qkvT,qkvT,bias)

def bwd_kernel(flags_ref,q_ref,k_ref,v_ref,do_ref,lse_ref,bias_ref,dq_ref,dk_ref,dv_ref,tab_ref,acc_ref,*,CH,nb):
    n=pl.program_id(1)
    qm,km=masks(flags_ref[n])
    q=q_ref[...]; kT=k_ref[...]; doT=do_ref[...]
    qa=jnp.concatenate([q,qm],0)
    ka=jnp.concatenate([kT,km],0).T
    v=v_ref[...].T
    @pl.when(n==0)
    def _(): acc_ref[...]=jnp.zeros_like(acc_ref)
    dk=None; dv=None
    for c in range(BLOCK//CH):
        sl=slice(c*CH,(c+1)*CH)
        s=dot(ka,qa[:,sl])+bias_ref[0,:,sl]
        p=jnp.exp(s-lse_ref[0,:,sl])
        pb=p.astype(BF16)
        dvc=dot(doT[:,sl],pb,NT)
        dp=dot(v,doT[:,sl])
        t=p*dp
        d=jnp.sum(t,axis=0,keepdims=True)
        ds=(t-p*d).astype(BF16)
        dq_ref[:,sl]=dot(kT,ds).astype(BF16)
        dkc=dot(q[:,sl],ds,NT)
        dk=dkc if dk is None else dk+dkc
        dv=dvc if dv is None else dv+dvc
        acc_ref[:,sl]+=ds.astype(F32)
    dk_ref[...]=dk.astype(BF16); dv_ref[...]=dv.astype(BF16)
    @pl.when(n==nb-1)
    def _():
        tot=None
        zero=jnp.zeros((128,BLOCK),F32)
        for g in range(4):
            x=jnp.concatenate([acc_ref[pl.ds(128*g,128),:],zero],1)
            y=pltpu.roll(x,(2*BLOCK-128*g)%(2*BLOCK),axis=1,stride=2*BLOCK-1,stride_axis=0)
            r=jnp.sum(y,axis=0,keepdims=True)
            tot=r if tot is None else tot+r
        t=lax.broadcasted_iota(jnp.int32,(1,2*BLOCK),1)
        rel=-jnp.where(t<BLOCK,t,t-2*BLOCK)
        b=bucket_of(rel)
        cc=lax.broadcasted_iota(jnp.int32,(BUCKETS,2*BLOCK),0)
        tab_ref[0]=jnp.broadcast_to(jnp.sum(jnp.where(b==cc,tot,0.0),axis=1,keepdims=True),(BUCKETS,128))
def bwd_call(flags,qkvT,doT,lse,bias,CH=256):
    T=qkvT.shape[1]; n=T//BLOCK
    sp=lambda off: pl.BlockSpec((HEAD_DIM,BLOCK),lambda h,n,f:(h+off,n))
    D=HEADS*HEAD_DIM
    return pl.pallas_call(functools.partial(bwd_kernel,CH=CH,nb=n),
        grid_spec=pltpu.PrefetchScalarGridSpec(num_scalar_prefetch=1,grid=(HEADS,n),
        in_specs=[sp(0),sp(HEADS),sp(2*HEADS),sp(0),pl.BlockSpec((1,1,BLOCK),lambda h,n,f:(h,0,n)),pl.BlockSpec((1,BLOCK,BLOCK),lambda h,n,f:(h,0,0))],
        out_specs=[sp(0),sp(0),sp(0),pl.BlockSpec((1,BUCKETS,128),lambda h,n,f:(h,0,0))],
        scratch_shapes=[pltpu.VMEM((BLOCK,BLOCK),F32)]),
        out_shape=[jax.ShapeDtypeStruct((D,T),BF16)]*3+[jax.ShapeDtypeStruct((HEADS,BUCKETS,128),F32)],
        name="attend_back",
        compiler_params=pltpu.CompilerParams(vmem_limit_bytes=48*2**20))(flags,qkvT,qkvT,qkvT,doT,lse,bias)

def fwd2_kernel(flags_ref,q_ref,k_ref,v_ref,bias_ref,o_ref,lse_ref,*,HP,mode):
    n=pl.program_id(1)
    qm,km=masks(flags_ref[n])
    S=[]
    for u in range(HP):
        r=slice(u*64,(u+1)*64)
        qa=jnp.concatenate([q_ref[r,:],qm],0)
        ka=jnp.concatenate([k_ref[r,:],km],0).T
        S.append(dot(ka,qa))
    for u in range(HP):
        r=slice(u*64,(u+1)*64)
        s=S[u]+bias_ref[u]
        m=jnp.max(s,axis=0,keepdims=True)
        e=jnp.exp(s-m)
        if mode=="def":
            l=jnp.sum(e,axis=0,keepdims=True)
            o_ref[r,:]=(dot(v_ref[r,:],e.astype(BF16))*(1.0/l)).astype(BF16)
        elif mode=="ones":
            va=jnp.concatenate([v_ref[r,:],jnp.ones((16,BLOCK),BF16)],0)
            oa=dot(va,e.astype(BF16))
            l=oa[64:65,:]
            o_ref[r,:]=(oa[:64]*(1.0/l)).astype(BF16)
        elif mode=="nomm":
            l=jnp.sum(e,axis=0,keepdims=True)
            o_ref[r,:]=e[:64].astype(BF16)
        else:
            l=jnp.sum(e,axis=0,keepdims=True)
            p=(e*(1.0/l)).astype(BF16)
            o_ref[r,:]=dot(v_ref[r,:],p).astype(BF16)
        lse_ref[u,:,:]=m+jnp.log(l)
def fwd2_call(flags,qkvT,bias,HP=2,mode="norm"):
    T=qkvT.shape[1]; n=T//BLOCK
    G=HEADS//HP
    sp=lambda off: pl.BlockSpec((HP*HEAD_DIM,BLOCK),lambda h,n,f:(h+off,n))
    return pl.pallas_call(functools.partial(fwd2_kernel,HP=HP,mode=mode),
        grid_spec=pltpu.PrefetchScalarGridSpec(num_scalar_prefetch=1,grid=(G,n),
        in_specs=[sp(0),sp(G),sp(2*G),pl.BlockSpec((HP,BLOCK,BLOCK),lambda h,n,f:(h,0,0))],
        out_specs=[pl.BlockSpec((HP*HEAD_DIM,BLOCK),lambda h,n,f:(h,n)),pl.BlockSpec((HP,1,BLOCK),lambda h,n,f:(h,0,n))]),
        out_shape=[jax.ShapeDtypeStruct((HEADS*HEAD_DIM,T),BF16),jax.ShapeDtypeStruct((HEADS,1,T),F32)],
        name="attend",
        compiler_params=pltpu.CompilerParams(vmem_limit_bytes=56*2**20))(flags,qkvT,qkvT,qkvT,bias)
def fwdN_kernel(flags_ref,q_ref,k_ref,v_ref,bias_ref,o_ref,lse_ref,*,HP):
    n=pl.program_id(1)
    qm,km=masks(flags_ref[n])
    for u in range(HP):
        r=slice(u*64,(u+1)*64)
        qa=jnp.concatenate([q_ref[r,:],qm],0)
        ka=jnp.concatenate([k_ref[r,:],km],0).T
        s=dot(ka,qa)+bias_ref[u]
        m=jnp.max(s,axis=0,keepdims=True)
        e=jnp.exp(s-m)
        l=jnp.sum(e,axis=0,keepdims=True)
        o=lax.dot_general(e.astype(BF16),v_ref[r,:],(((0,),(1,)),((),())),preferred_element_type=F32)
        o_ref[r,:]=(o.T*(1.0/l)).astype(BF16)
        lse_ref[u,:,:]=m+jnp.log(l)

def left_by_row(x,width):
    row=lax.broadcasted_iota(jnp.int32,x.shape,0)
    for b in range(7):
        y=pltpu.roll(x,width-(1<<b),axis=1)
        x=jnp.where((row>>b)&1==1,y,x)
    return x
def bwd2_kernel(flags_ref,q_ref,k_ref,v_ref,do_ref,lse_ref,bias_ref,g_ref,tab_ref,band_ref,far_ref,*,HP,nb,tabmode):
    n=pl.program_id(1)
    qm,km=masks(flags_ref[n])
    @pl.when(n==0)
    def _():
        band_ref[...]=jnp.zeros_like(band_ref); far_ref[...]=jnp.zeros_like(far_ref)
    R=[slice(u*64,(u+1)*64) for u in range(HP)]
    S=[];DP=[]
    for u in range(HP):
        r=R[u]
        qa=jnp.concatenate([q_ref[r,:],qm],0)
        ka=jnp.concatenate([k_ref[r,:],km],0).T
        S.append(dot(ka,qa))
        DP.append(dot(v_ref[r,:].T,do_ref[r,:]))
    for u in range(HP):
        r=R[u]
        p=jnp.exp(S[u]+bias_ref[u]-lse_ref[u])
        pb=p.astype(BF16)
        g_ref[2,r,:]=dot(do_ref[r,:],pb,NT).astype(BF16)
        t=p*DP[u]
        d=jnp.sum(t,axis=0,keepdims=True)
        dsf=t-p*d
        ds=dsf.astype(BF16)
        g_ref[0,r,:]=dot(k_ref[r,:],ds).astype(BF16)
        g_ref[1,r,:]=dot(q_ref[r,:],ds,NT).astype(BF16)
        if tabmode:
            lo=None;hi=None;bl=[None]*3
            for g in range(4):
                for c in range(4):
                    tile=dsf[128*g:128*(g+1),128*c:128*(c+1)]
                    w=c-g+1
                    if 0<=w<3:
                        bl[w]=tile if bl[w] is None else bl[w]+tile
                    elif w<0:
                        lo=tile if lo is None else lo+tile
                    else:
                        hi=tile if hi is None else hi+tile
            for w in range(3): band_ref[u,:,128*w:128*(w+1)]+=bl[w]
            far_ref[u,0]+=jnp.sum(lo.reshape(16,8,128),axis=0)
            far_ref[u,1]+=jnp.sum(hi.reshape(16,8,128),axis=0)
    @pl.when(n==nb-1)
    def _():
        t=lax.broadcasted_iota(jnp.int32,(1,BLOCK),1)
        b=bucket_of(-jnp.where(t<384,t-128,t-640))
        cc=lax.broadcasted_iota(jnp.int32,(BUCKETS,BLOCK),0)
        c1=lax.broadcasted_iota(jnp.int32,(BUCKETS,128),0)
        for u in range(HP):
            x=jnp.concatenate([band_ref[u],jnp.zeros((128,128),F32)],1)
            tot=jnp.sum(left_by_row(x,BLOCK),axis=0,keepdims=True)
            lo=jnp.sum(far_ref[u,0],axis=0,keepdims=True); hi=jnp.sum(far_ref[u,1],axis=0,keepdims=True)
            val=jnp.where(b==cc,tot,0.0)
            val=val[:,:128]+val[:,128:256]+val[:,256:384]+val[:,384:]
            val=val+jnp.where(c1==BUCKETS-1,lo,0.0)+jnp.where(c1==BUCKETS//2-1,hi,0.0)
            col=jnp.broadcast_to(jnp.sum(val,axis=1,keepdims=True),(BUCKETS,128))
            col=jnp.concatenate([col,jnp.zeros((128-BUCKETS,128),F32)],0)
            tab_ref[u]=col.T[:8]
def bwd2_call(flags,qkvT,doT,lse,bias,HP=2,tabmode=1):
    T=qkvT.shape[1]; n=T//BLOCK; G=HEADS//HP
    sp=lambda off: pl.BlockSpec((HP*HEAD_DIM,BLOCK),lambda h,n,f:(h+off,n))
    D=HEADS*HEAD_DIM
    return pl.pallas_call(functools.partial(bwd2_kernel,HP=HP,nb=n,tabmode=tabmode),
        grid_spec=pltpu.PrefetchScalarGridSpec(num_scalar_prefetch=1,grid=(G,n),
        in_specs=[sp(0),sp(G),sp(2*G),sp(0),pl.BlockSpec((HP,1,BLOCK),lambda h,n,f:(h,0,n)),pl.BlockSpec((HP,BLOCK,BLOCK),lambda h,n,f:(h,0,0))],
        out_specs=[pl.BlockSpec((3,HP*HEAD_DIM,BLOCK),lambda h,n,f:(0,h,n)),pl.BlockSpec((HP,8,128),lambda h,n,f:(h,0,0))],
        scratch_shapes=[pltpu.VMEM((HP,128,384),F32),pltpu.VMEM((HP,2,8,128),F32)]),
        out_shape=[jax.ShapeDtypeStruct((3,D,T),BF16),jax.ShapeDtypeStruct((HEADS,8,128),F32)],
        name="attend_back",
        compiler_params=pltpu.CompilerParams(vmem_limit_bytes=60*2**20))(flags,qkvT,qkvT,qkvT,doT,lse,bias)

D=768
norm_eps=1e-6
def rms(x): return lax.rsqrt(jnp.mean(x*x,axis=-1,keepdims=True)+norm_eps)
GA=128
def row_of(gains,which):
    return gains.astype(F32).T[which:which+1,:]
def qkv_kernel(x_ref,w_ref,aT_ref,qkvT_ref,wT_ref):
    @pl.when(pl.program_id(0)==0)
    def _():
        for c in range(3):
            wT_ref[pl.ds(c*D,D),:]=w_ref[:,c*D:(c+1)*D].T
    x=x_ref[...].astype(F32)
    g=row_of(w_ref[:,3*D:3*D+GA],0)
    a=(x*rms(x)*g).astype(BF16)
    aT=a.T
    aT_ref[...]=aT
    qkvT_ref[...]=dot(wT_ref[...],aT).astype(BF16)
def qkv_call(x,w):
    T=x.shape[0]
    return pl.pallas_call(qkv_kernel,grid=(T//BLOCK,),
        in_specs=[pl.BlockSpec((BLOCK,D),lambda t:(t,0)),pl.BlockSpec(w.shape,lambda t:(0,0),pipeline_mode=pl.Buffered(1))],
        out_specs=[pl.BlockSpec((D,BLOCK),lambda t:(0,t)),pl.BlockSpec((3*D,BLOCK),lambda t:(0,t))],
        out_shape=[jax.ShapeDtypeStruct((D,T),BF16),jax.ShapeDtypeStruct((3*D,T),BF16)],
        scratch_shapes=[pltpu.VMEM((3*D,D),BF16)],name="project",
        compiler_params=pltpu.CompilerParams(vmem_limit_bytes=56*2**20))(x,w)
def mid_kernel(x_ref,oT_ref,wo_ref,ga_ref,m_ref,b_ref,bT_ref,*_):
    o=oT_ref[...].T
    m=x_ref[...].astype(F32)+dot(o,wo_ref[...],NT)
    m_ref[...]=m
    b=(m*rms(m)*row_of(ga_ref[...],1)).astype(BF16)
    b_ref[...]=b
    bT_ref[0]=b.T
def mid_call(x,oT,woT,gains):
    T=x.shape[0]
    return pl.pallas_call(mid_kernel,grid=(T//BLOCK,),
        in_specs=[pl.BlockSpec((BLOCK,D),lambda t:(t,0)),pl.BlockSpec((D,BLOCK),lambda t:(0,t)),
                  pl.BlockSpec((D,D),lambda t:(0,woT[1])),pl.BlockSpec((D,GA),lambda t:(0,gains[1]))],
        out_specs=[pl.BlockSpec((BLOCK,D),lambda t:(t,0)),pl.BlockSpec((BLOCK,D),lambda t:(t,0)),pl.BlockSpec((1,D,BLOCK),lambda t:(t,0,0))],
        out_shape=[jax.ShapeDtypeStruct((T,D),F32),jax.ShapeDtypeStruct((T,D),BF16),jax.ShapeDtypeStruct((T//BLOCK,D,BLOCK),BF16)],
        name="middle",
        compiler_params=pltpu.CompilerParams(vmem_limit_bytes=48*2**20))(x,oT,woT[0],gains[0])
def gate(u,mode):
    if mode=="erf":
        P=0.5*(1.0+lax.erf(u*(0.5**0.5)))
        z=jnp.exp(-0.5*u*u)
    else:
        z=jnp.exp(-0.5*u*u)
        t=1.0/(1.0+(0.3275911*0.5**0.5)*jnp.abs(u))
        q=((((0.5*1.061405429*t-0.5*1.453152027)*t+0.5*1.421413741)*t-0.5*0.284496736)*t+0.5*0.254829592)*t*z
        P=jnp.where(u>=0,1.0-q,q)
    return u*P, P+u*z*(2*math.pi)**-0.5
def ffn_kernel(b_ref,bT_ref,dy_ref,m_ref,win_ref,wout_ref,out_ref,db_ref,dw_ref,
               oacc,dacc,dyT,ain,aout,*,FC,SUB,nc,nt,mode,TB,order):
    c=pl.program_id(0); t=pl.program_id(1)
    rows=pl.ds(t*TB,TB)
    @pl.when(c==0)
    def _():
        oacc[rows,:]=m_ref[...]
        dacc[rows,:]=jnp.zeros((TB,D),F32)
        dyT[t]=dy_ref[rows,:].T
    b=b_ref[rows,:]; dy=dy_ref[rows,:]
    G=[];DU=[]
    U=[dot(b,win_ref[:,s*SUB:(s+1)*SUB]) for s in range(FC//SUB)]
    DG=[dot(dy,wout_ref[:,s*SUB:(s+1)*SUB]) for s in range(FC//SUB)]
    @pl.when(t==0)
    def _():
        ain[...]=jnp.zeros_like(ain); aout[...]=jnp.zeros_like(aout)
    for s in range(FC//SUB):
        g,pull=gate(U[s],mode)
        g=g.astype(BF16)
        du=(DG[s]*pull).astype(BF16)
        sl=slice(s*SUB,(s+1)*SUB)
        aout[:,sl]+=dot(dyT[t],g)
        ain[:,sl]+=dot(bT_ref[t],du)
        G.append(g);DU.append(du)
    g=jnp.concatenate(G,1);du=jnp.concatenate(DU,1)
    oacc[rows,:]+=dot(g,wout_ref[...],NT)
    dacc[rows,:]+=dot(du,win_ref[...],NT)
    @pl.when(t==nt-1)
    def _():
        dw_ref[:,:FC]=ain[...].astype(BF16)
        dw_ref[:,FC:]=aout[...].astype(BF16)
    @pl.when(c==nc-1)
    def _():
        out_ref[...]=oacc[rows,:].astype(BF16)
        db_ref[...]=dacc[rows,:]
def ffn_call(b,bT,dy,m,win,wout,FC=768,SUB=256,mode="erf",TB=512,order=0):
    T=b.shape[0]; nt=T//TB; FF=3072; nc=FF//FC
    bT3=bT
    last=lambda c,t:(jnp.where(c==nc-1,t,0),0)
    first=lambda c,t:(jnp.where(c==0,t,nt-1),0)
    one=pl.Buffered(1)
    return pl.pallas_call(functools.partial(ffn_kernel,FC=FC,SUB=SUB,nc=nc,nt=nt,mode=mode,TB=TB,order=order),grid=(nc,nt),
        in_specs=[pl.BlockSpec((T,D),lambda c,t:(0,0),pipeline_mode=one),pl.BlockSpec((nt,D,TB),lambda c,t:(0,0,0),pipeline_mode=one),
            pl.BlockSpec((T,D),lambda c,t:(0,0),pipeline_mode=one),
            pl.BlockSpec((TB,D),first),pl.BlockSpec((D,FC),lambda c,t:(0,c+win[1]*D//FC)),pl.BlockSpec((D,FC),lambda c,t:(0,c+wout[1]*D//FC))],
        out_specs=[pl.BlockSpec((TB,D),last),pl.BlockSpec((TB,D),last),pl.BlockSpec((D,2*FC),lambda c,t:(0,c))],
        out_shape=[jax.ShapeDtypeStruct((T,D),BF16),jax.ShapeDtypeStruct((T,D),F32),jax.ShapeDtypeStruct((D,2*FF),BF16)],
        scratch_shapes=[pltpu.VMEM((T,D),F32),pltpu.VMEM((T,D),F32),pltpu.VMEM((nt,D,TB),BF16),pltpu.VMEM((D,FC),F32),pltpu.VMEM((D,FC),F32)],
        name="feed_forward",
        compiler_params=pltpu.CompilerParams(vmem_limit_bytes=62*2**20))(b,bT3,dy,m,win[0],wout[0])

def post_kernel(dy_ref,db_ref,m_ref,oT_ref,wo_ref,ga_ref,dm_ref,doT_ref,dwo_ref,acc_ref,*,nt):
    t=pl.program_id(0)
    @pl.when(t==0)
    def _():
        acc_ref[...]=jnp.zeros_like(acc_ref)
    m=m_ref[...]; db=db_ref[...]
    r=rms(m); n2=m*r
    dn=db*row_of(ga_ref[...],1)
    dm=dy_ref[...].astype(F32)+r*(dn-n2*jnp.mean(dn*n2,axis=-1,keepdims=True))
    dm_ref[...]=dm
    dmb=dm.astype(BF16)
    acc_ref[...]+=dot(dmb.T,oT_ref[...],NT)
    doT_ref[...]=dot(dmb,wo_ref[...]).astype(BF16).T
    @pl.when(t==nt-1)
    def _(): dwo_ref[...]=acc_ref[...].astype(BF16)
def post_call(dy,db,m,oT,woT,gains):
    T=dy.shape[0]; nt=T//BLOCK
    row=pl.BlockSpec((BLOCK,D),lambda t:(t,0)); col=pl.BlockSpec((D,BLOCK),lambda t:(0,t))
    return pl.pallas_call(functools.partial(post_kernel,nt=nt),grid=(nt,),
        in_specs=[row,row,row,col,pl.BlockSpec((D,D),lambda t:(0,woT[1])),pl.BlockSpec((D,GA),lambda t:(0,gains[1]))],
        out_specs=[row,col,pl.BlockSpec((D,D),lambda t:(0,0))],
        out_shape=[jax.ShapeDtypeStruct((T,D),F32),jax.ShapeDtypeStruct((D,T),BF16),jax.ShapeDtypeStruct((D,D),BF16)],
        scratch_shapes=[pltpu.VMEM((D,D),F32)],name="middle_back",
        compiler_params=pltpu.CompilerParams(vmem_limit_bytes=48*2**20))(dy,db,m,oT,woT[0],gains[0])
def last_kernel(x_ref,dm_ref,g_ref,w_ref,dx_ref):
    da=None
    for c in range(3):
        z=dot(w_ref[:,c*D:(c+1)*D],g_ref[c])
        da=z if da is None else da+z
    da=da.T
    x=x_ref[...].astype(F32)
    r=rms(x); n1=x*r
    dn=da*row_of(w_ref[:,3*D:3*D+GA],0)
    dx_ref[...]=(dm_ref[...]+r*(dn-n1*jnp.mean(dn*n1,axis=-1,keepdims=True))).astype(BF16)
def last_call(x,dm,gT,w):
    T=x.shape[0]; nt=T//BLOCK
    row=pl.BlockSpec((BLOCK,D),lambda t:(t,0))
    return pl.pallas_call(last_kernel,grid=(nt,),
        in_specs=[row,row,pl.BlockSpec((3,D,BLOCK),lambda t:(0,0,t)),pl.BlockSpec(w.shape,lambda t:(0,0),pipeline_mode=pl.Buffered(1))],
        out_specs=row,out_shape=jax.ShapeDtypeStruct((T,D),BF16),name="project_back",
        cost_estimate=pl.CostEstimate(flops=2*T*D*3*D,bytes_accessed=20*T*D,transcendentals=0),
        compiler_params=pltpu.CompilerParams(vmem_limit_bytes=56*2**20))(x,dm,gT,w)

def block_kernel(at_ref,x_ref,oT_ref,dy_ref,ga_ref,wo_ref,win_ref,wout_ref,
                 out_ref,dm_ref,doT_ref,dwo_ref,*rest,FC,SUB,nc,nt,legs):
    dw_ref,b_s,oacc,dacc,ain,aout,awo,m_s=rest
    c=pl.program_id(0); t=pl.program_id(1)
    rows=pl.ds(t*BLOCK,BLOCK)
    def middle():
        return x_ref[...].astype(F32)+dot(oT_ref[...].T,wo_ref[...],NT)
    @pl.when(t==0)
    def _():
        ain[...]=jnp.zeros_like(ain); aout[...]=jnp.zeros_like(aout)
    @pl.when((c==nc-1)&(t==0))
    def _(): awo[...]=jnp.zeros_like(awo)
    n=FC//SUB
    def inner(dy):
        return [dot(dy,wout_ref[:,s*SUB:(s+1)*SUB]) for s in range(n)]
    def gates(b,DG):
        U=[dot(b,win_ref[:,s*SUB:(s+1)*SUB]) for s in range(n)]
        G=[];DU=[]
        for s in range(n):
            g,pull=gate(U[s],"erf")
            G.append(g.astype(BF16)); DU.append((DG[s]*pull).astype(BF16))
        return G,DU
    def sums(bt,dyt,G,DU):
        for s in range(n):
            sl=slice(s*SUB,(s+1)*SUB)
            aout[:,sl]+=dot(dyt,G[s])
            ain[:,sl]+=dot(bt,DU[s])
    def outer(G,DU):
        return dot(jnp.concatenate(G,1),wout_ref[...],NT),dot(jnp.concatenate(DU,1),win_ref[...],NT)
    @pl.when(c==0)
    def _():
        dy=dy_ref[...]
        DG=inner(dy)
        m=middle()
        b=(m*rms(m)*row_of(ga_ref[...],1)).astype(BF16)
        b_s[t]=b
        m_s[rows,:]=m
        G,DU=gates(b,DG)
        o,d=outer(G,DU)
        sums(b.T,dy.T,G,DU)
        oacc[rows,:]=m+o
        dacc[rows,:]=d
    @pl.when((c>0)&(c<nc-1))
    def _():
        dy=dy_ref[...]; b=b_s[t]
        G,DU=gates(b,inner(dy))
        sums(b.T,dy.T,G,DU)
        o,d=outer(G,DU)
        oacc[rows,:]+=o
        dacc[rows,:]+=d
    @pl.when(c==nc-1)
    def _():
        dy=dy_ref[...]; b=b_s[t]
        G,DU=gates(b,inner(dy))
        o,d=outer(G,DU)
        db=dacc[rows,:]+d
        out_ref[...]=(oacc[rows,:]+o).astype(BF16)
        sums(b.T,dy.T,G,DU)
        m=m_s[rows,:]
        r=rms(m); n2=m*r
        dn=db*row_of(ga_ref[...],1)
        dm=dy.astype(F32)+r*(dn-n2*jnp.mean(dn*n2,axis=-1,keepdims=True))
        dm_ref[...]=dm
        dmb=dm.astype(BF16)
        awo[...]+=dot(dmb.T,oT_ref[...],NT)
        doT_ref[...]=dot(dmb,wo_ref[...]).astype(BF16).T
    @pl.when(t==nt-1)
    def _():
        if legs:
            R=dw_ref.shape[1]
            for s in range(32):
                z=at_ref[0]^((s>>1)&1)^((s&1)<<1)
                at=pl.ds(pl.multiple_of((z*8+(s>>2))*R,8),R)
                dw_ref[s,:,:FC]=ain[at,:].astype(BF16)
                dw_ref[s,:,FC:]=aout[at,:].astype(BF16)
        else:
            dw_ref[:,:FC]=ain[...].astype(BF16)
            dw_ref[:,FC:]=aout[...].astype(BF16)
    @pl.when((c==nc-1)&(t==nt-1))
    def _(): dwo_ref[...]=awo[...].astype(BF16)
def block_call(x,oT,dy,gains,wo,win,wout,core,legs,FC=768,SUB=256):
    T=x.shape[0]; nt=T//BLOCK; FF=3072; nc=FF//FC
    last=lambda c,t:jnp.where(c==nc-1,t,0)
    first=lambda c,t:jnp.where(c==0,t,nt-1)
    ends=lambda c,t:jnp.where((c==0)|(c==nc-1),t,nt-1)
    one=pl.Buffered(1)
    sd=jax.ShapeDtypeStruct; BS=pl.BlockSpec; R=D//32
    return pl.pallas_call(functools.partial(block_kernel,FC=FC,SUB=SUB,nc=nc,nt=nt,legs=legs),
        grid_spec=pltpu.PrefetchScalarGridSpec(num_scalar_prefetch=1,grid=(nc,nt),
        in_specs=[BS((BLOCK,D),lambda c,t,at:(first(c,t),0)),BS((D,BLOCK),lambda c,t,at:(0,ends(c,t))),
            BS((BLOCK,D),lambda c,t,at:(t,0)),
            BS((D,GA),lambda c,t,at:(0,gains[1]),pipeline_mode=one),BS((D,D),lambda c,t,at:(0,wo[1]),pipeline_mode=one),
            BS((D,FC),lambda c,t,at:(0,c+win[1])),BS((D,FC),lambda c,t,at:(0,c+wout[1]))],
        out_specs=[BS((BLOCK,D),lambda c,t,at:(last(c,t),0)),BS((BLOCK,D),lambda c,t,at:(last(c,t),0)),BS((D,BLOCK),lambda c,t,at:(0,last(c,t))),
            BS((D,D),lambda c,t,at:(0,0),pipeline_mode=one)]+([BS((32,R,2*FC),lambda c,t,at:(0,0,c))] if legs else [BS((D,2*FC),lambda c,t,at:(0,c))]),
        scratch_shapes=[pltpu.VMEM((nt,BLOCK,D),BF16),
            pltpu.VMEM((T,D),F32),pltpu.VMEM((T,D),F32),pltpu.VMEM((D,FC),F32),pltpu.VMEM((D,FC),F32),pltpu.VMEM((D,D),F32),pltpu.VMEM((T,D),F32)]),
        out_shape=[sd((T,D),BF16),sd((T,D),F32),sd((D,T),BF16),sd((D,D),BF16)]+([sd((32,R,2*FF),BF16)] if legs else [sd((D,2*FF),BF16)]),
        name="feed_forward",
        compiler_params=pltpu.CompilerParams(vmem_limit_bytes=62*2**20+2**19))(core,x,oT,dy,gains[0],wo[0],win[0],wout[0])

GW=3*D+GA
INNER=("yx","core")
def pack_a_kernel(q_ref,k_ref,v_ref,g1_ref,g2_ref,o_ref):
    for c,ref in enumerate((q_ref,k_ref,v_ref)):
        o_ref[:,c*D:(c+1)*D]=ref[...].astype(BF16)
    rows=o_ref.shape[0]
    g=jnp.concatenate([g1_ref[...],g2_ref[...],jnp.zeros((GA-2,rows),F32)],0)
    o_ref[:,3*D:]=g.T.astype(BF16)
def pack_a(q,k,v,g1,g2):
    return pl.pallas_call(pack_a_kernel,out_shape=jax.ShapeDtypeStruct((q.shape[0],GW),BF16),name="pack_attention")(q,k,v,g1[None],g2[None])
def pack_b_kernel(wo_ref,wi_ref,wu_ref,o_ref):
    F=wi_ref.shape[1]
    o_ref[:,:F]=wi_ref[...].astype(BF16)
    o_ref[:,F:2*F]=wu_ref[...].astype(BF16)
    o_ref[:,2*F:]=wo_ref[...].astype(BF16)
def pack_b(wo,wi,wu):
    return pl.pallas_call(pack_b_kernel,out_shape=jax.ShapeDtypeStruct((wi.shape[0],D+2*wi.shape[1]),BF16),name="pack_feed_forward")(wo.T,wi,wu.T)

def swap(x,axis,mask):
    n=8 if axis==INNER else 4
    f=mask if callable(mask) else (lambda i:mask)
    return lax.ppermute(x,axis,[(i,i^f(i)) for i in range(n)])
first_leg=lambda i: 4 if i&1 else 2
second_leg=lambda i: 2 if i&1 else 4
def gather_pieces(shard,beside):
    a=shard[None]
    a=jnp.concatenate([a,swap(a,"dp",2)],0)
    got=swap(a,"dp",1)
    got,beside=lax.optimization_barrier((got,beside))
    a=jnp.concatenate([a,got],0)
    a=jnp.concatenate([a,swap(a,INNER,first_leg)],0)
    b=swap(a,INNER,second_leg)
    c=swap(a,INNER,1)
    d=swap(b,INNER,1)
    return (a,b,c,d),beside
def place():
    f=lax.axis_index(INNER); z=lax.axis_index("dp")
    return jnp.stack([f,z]).astype(jnp.int32)
def assemble_rows(at_ref,pieces,put):
    f=at_ref[0]; z=at_ref[1]
    core=f&1; x=(f>>1)&1; y=f>>2
    for j in range(16):
        zj,yj,xj=j>>2,(j>>1)&1,j&1
        dz=zj^z; dx=xj^x; dy=yj^y
        low=(dz&1)*2+(dz>>1)
        halves=[]
        for cj in range(2):
            far_core=core^cj
            one=jnp.where(cj==0,dx,dy)
            two=jnp.where(cj==0,dy,dx)
            slot=one*4+low
            which=far_core*2+two
            halves.append((which,slot))
        put(j,halves)
def project2_kernel(at_ref,x_ref,a_ref,b_ref,c_ref,d_ref,aT_ref,qkvT_ref,w_ref,all_ref,wT_ref):
    R=a_ref.shape[1]
    @pl.when(pl.program_id(0)==0)
    def _():
        for i,ref in enumerate((a_ref,b_ref,c_ref,d_ref)): all_ref[pl.ds(8*i,8)]=ref[...]
        def put(j,halves):
            v=jnp.concatenate([all_ref[w*8+s].astype(F32) for w,s in halves],0)
            w_ref[pl.ds(j*2*R,2*R),:]=v.astype(BF16)
        assemble_rows(at_ref,None,put)
        for c in range(3):
            wT_ref[pl.ds(c*D,D),:]=w_ref[:,c*D:(c+1)*D].T
    x=x_ref[...].astype(F32)
    g=row_of(w_ref[:,3*D:3*D+GA],0)
    a=(x*rms(x)*g).astype(BF16)
    aT=a.T
    aT_ref[...]=aT
    qkvT_ref[...]=dot(wT_ref[...],aT).astype(BF16)
def project2_call(x,pieces,at):
    T=x.shape[0]; R=pieces[0].shape[1]
    one=pl.Buffered(1)
    ps=pl.BlockSpec((8,R,GW),lambda t,at:(0,0,0),pipeline_mode=one)
    return pl.pallas_call(project2_kernel,
        grid_spec=pltpu.PrefetchScalarGridSpec(num_scalar_prefetch=1,grid=(T//BLOCK,),
        in_specs=[pl.BlockSpec((BLOCK,D),lambda t,at:(t,0)),ps,ps,ps,ps],
        out_specs=[pl.BlockSpec((D,BLOCK),lambda t,at:(0,t)),pl.BlockSpec((3*D,BLOCK),lambda t,at:(0,t)),pl.BlockSpec((D,GW),lambda t,at:(0,0))],
        scratch_shapes=[pltpu.VMEM((32,R,GW),BF16),pltpu.VMEM((3*D,D),BF16)]),
        out_shape=[jax.ShapeDtypeStruct((D,T),BF16),jax.ShapeDtypeStruct((3*D,T),BF16),jax.ShapeDtypeStruct((D,GW),BF16)],
        name="project",
        compiler_params=pltpu.CompilerParams(vmem_limit_bytes=60*2**20))(at,x,*pieces)


def add(a,b): return (a.astype(F32)+b.astype(F32)).astype(BF16)
GN=4*D+128
def slot_rows(s,f,z,core):
    x=(f>>1)&1; y=f>>2
    one=s>>3; two=(s>>2)&1
    dx=jnp.where(core==0,one,two); dy=jnp.where(core==0,two,one)
    zz=z^((s>>1)&1)^((s&1)<<1)
    return (zz*8+(y^dy)*4+(x^dx)*2+core)
def slot_table():
    f=lax.axis_index(INNER); z=lax.axis_index("dp")
    s=jnp.arange(16,dtype=jnp.int32); core=f&1
    return jnp.stack([slot_rows(s,f,z,core),slot_rows(s,f,z,1-core)]).astype(jnp.int32)
def grads_kernel(at_ref,aT_ref,g_ref,wo_ref,tab_ref,keep_ref,send_ref,v_ref):
    c=pl.program_id(0)
    R=keep_ref.shape[1]
    @pl.when(c<3)
    def _(): v_ref[...]=dot(aT_ref[...],g_ref[0],NT)
    @pl.when(c==3)
    def _(): v_ref[...]=wo_ref[...].astype(F32)
    @pl.when(c<4)
    def _():
        for s in range(16):
            for q,ref in enumerate((keep_ref,send_ref)):
                ref[s]=v_ref[pl.ds(pl.multiple_of(at_ref[q,s]*R,8),R),:].astype(BF16)
    @pl.when(c==4)
    def _():
        t=jnp.concatenate([tab_ref[h,:1,:] for h in range(HEADS)]+[jnp.zeros((R-HEADS,128),F32)],0).astype(BF16)
        for s in range(16):
            keep_ref[s,:,:128]=t; send_ref[s,:,:128]=t
def grads_call(at,aT,gT,dwoT,tab):
    T=aT.shape[1]; R=D//32
    out=pl.BlockSpec((16,R,D),lambda c,at:(0,0,c))
    return pl.pallas_call(grads_kernel,
        grid_spec=pltpu.PrefetchScalarGridSpec(num_scalar_prefetch=1,grid=(5,),
        in_specs=[pl.BlockSpec((D,T),lambda c,at:(0,0),pipeline_mode=pl.Buffered(1)),
                  pl.BlockSpec((1,D,T),lambda c,at:(jnp.minimum(c,2),0,0)),
                  pl.BlockSpec((D,D),lambda c,at:(0,0),pipeline_mode=pl.Buffered(1)),
                  pl.BlockSpec((HEADS,8,128),lambda c,at:(0,0,0))],
        out_specs=[out,out],scratch_shapes=[pltpu.VMEM((D,D),F32)]),
        out_shape=[jax.ShapeDtypeStruct((16,R,GN),BF16)]*2,name="weight_grads",
        compiler_params=pltpu.CompilerParams(vmem_limit_bytes=48*2**20))(at,aT,gT,dwoT,tab)
def scatter_sum(keep,send,dm,beside,other,rest):
    r=swap(send,INNER,1)
    for half,axis,leg in ((8,INNER,first_leg),(4,INNER,second_leg),(2,"dp",1),(1,"dp",2)):
        out=add(keep[half:],r[half:])
        keep=add(keep[:half],r[:half])
        if half==4:
            out,dm=lax.optimization_barrier((out,dm))
            dx=beside(dm)
        r=swap(out,axis,leg)
        if half==4:
            r,dx,other=lax.optimization_barrier((r,dx,other))
            late=rest[0](other)
        if half==2:
            r,late=lax.optimization_barrier((r,late))
            late=rest[1](late)
    r,late=lax.optimization_barrier((r,late))
    return keep[0],r[0],dx,late
def finish_kernel(a_ref,b_ref,wq_ref,wk_ref,wv_ref,g_ref,q_ref,k_ref,v_ref,o_ref,tab_ref,dg_ref):
    R=a_ref.shape[0]
    tot=None
    for c,(w,out) in enumerate(((wq_ref,q_ref),(wk_ref,k_ref),(wv_ref,v_ref),(None,o_ref))):
        sl=slice(c*D,(c+1)*D)
        s=a_ref[:,sl].astype(F32)+b_ref[:,sl].astype(F32)
        out[...]=s
        if w is not None:
            y=jnp.sum(s*w[...].astype(BF16).astype(F32),axis=1,keepdims=True)
            tot=y if tot is None else tot+y
    t=a_ref[:,4*D:4*D+128].astype(F32)+b_ref[:,4*D:4*D+128].astype(F32)
    tab_ref[...]=t[:HEADS,:BUCKETS]
    rowv=jnp.broadcast_to(tot,(R,128))
    rowv=jnp.concatenate([rowv,jnp.zeros((128-R,128),F32)],0).T[:1,:R]
    dg_ref[...]=rowv/g_ref[...].astype(BF16).astype(F32)
def finish_call(a,b,wq,wk,wv,g1):
    R=a.shape[0]; sd=jax.ShapeDtypeStruct
    return pl.pallas_call(finish_kernel,out_shape=[sd((R,D),F32)]*4+[sd((HEADS,BUCKETS),F32),sd((1,R),F32)],name="finish_attention")(a,b,wq,wk,wv,g1[None])
def finish_ffn_kernel(s_ref,t_ref,w_ref,g_ref,i_ref,o_ref,dg_ref,*,FC):
    R=s_ref.shape[0]
    tot=None
    for c in range(w_ref.shape[1]//FC):
        sl=slice(c*FC,(c+1)*FC)
        one=slice(2*c*FC,(2*c+1)*FC); two=slice((2*c+1)*FC,(2*c+2)*FC)
        s=s_ref[:,one].astype(F32)+t_ref[:,one].astype(F32)
        i_ref[:,sl]=s
        o_ref[:,sl]=s_ref[:,two].astype(F32)+t_ref[:,two].astype(F32)
        y=jnp.sum(s*w_ref[:,sl].astype(BF16).astype(F32),axis=1,keepdims=True)
        tot=y if tot is None else tot+y
    rowv=jnp.broadcast_to(tot,(R,128))
    rowv=jnp.concatenate([rowv,jnp.zeros((128-R,128),F32)],0).T[:1,:R]
    dg_ref[...]=rowv/g_ref[...].astype(BF16).astype(F32)
def finish_ffn_call(s,t,w,g2,FC):
    R,F=w.shape; sd=jax.ShapeDtypeStruct
    return pl.pallas_call(functools.partial(finish_ffn_kernel,FC=FC),out_shape=[sd((R,F),F32),sd((R,F),F32),sd((1,R),F32)],name="finish_feed_forward")(s,t,w,g2[None])

BOTH=("dp","fsdp")
ALL=("dp","yx","core")
FC=768
def low(v): return v.astype(BF16).astype(F32)
def body(sizes,hidden,long_flags,norm1_gain,query_w,key_w,value_w,out_w,bias_table,norm2_gain,ffn_in,ffn_out,out_grad):
    rows=norm1_gain.shape[0]
    FF=ffn_in.shape[1]
    legs=sizes==(4,8)
    if legs:
        pa=pack_a(query_w,key_w,value_w,norm1_gain,norm2_gain)
        pb=pack_b(out_w,ffn_in,ffn_out)
        wb=lax.all_gather(pb,ALL,axis=0,tiled=True)
        at=place()
        pieces,bias=gather_pieces(pa,bias_call(bias_table))
        aT,qkvT,wa=project2_call(hidden,pieces,at)
    else:
        bias=bias_call(bias_table)
        gains=jnp.concatenate([norm1_gain[:,None],norm2_gain[:,None],jnp.zeros((rows,GA-2),F32)],1)
        pa=jnp.concatenate([query_w,key_w,value_w,gains],1).astype(BF16)
        pb=jnp.concatenate([ffn_in,ffn_out.T,out_w.T],1).astype(BF16)
        wa=lax.all_gather(pa,BOTH,axis=0,tiled=True)
        wb=lax.all_gather(pb,BOTH,axis=0,tiled=True)
        aT,qkvT=qkv_call(hidden,wa)
    oT,lse=fwd2_call(long_flags,qkvT,bias,HP=4,mode="ones")
    GB=3*D//GA
    z=(lax.axis_index("dp") if legs else jnp.zeros((),jnp.int32)).reshape(1)
    out,dm,doT,dwoT,dffn=block_call(hidden,oT,out_grad,(wa,GB),(wb,2*FF//D),(wb,0),(wb,FF//FC),z,legs,FC=FC)
    def rs(x,axes=BOTH): return lax.psum_scatter(x,axes,scatter_dimension=0,tiled=True)
    fsum=rs(dffn.reshape(D,2*FF),INNER if legs else BOTH)
    gT,tab=bwd2_call(long_flags,qkvT,doT,lse,bias,HP=4)
    if legs:
        keep,send=grads_call(slot_table(),aT,gT,dwoT,tab)
        h=fsum.reshape(4,rows,2*FF)
        h,dm=lax.optimization_barrier((h,dm))
        r=swap(h[2:],"dp",1)
        rest=(lambda r:(add(h[0],r[0]),swap(add(h[1],r[1]),"dp",2)),lambda z:finish_ffn_call(*z,ffn_in,norm2_gain,FC))
        a,b2,dx,(di,du,dg2)=scatter_sum(keep,send,dm,lambda dm:last_call(hidden,dm,gT,wa),r,rest)
        dq,dk,dv,do,table,dg1=finish_call(a,b2,query_w,key_w,value_w,norm1_gain)
        dg1=dg1[0]; dg2=dg2[0]; table=table.T
    else:
        dx=last_call(hidden,dm,gT,wa)
        tabs=tab[:,0,:BUCKETS].reshape(-1)
        wide=tabs.shape[0]//rows
        tb=jnp.tile(tabs.reshape(rows,wide),(D//rows,1))
        parts=[lax.dot_general(aT,gT[c],NT,preferred_element_type=F32).astype(BF16) for c in range(3)]
        asum=rs(jnp.concatenate(parts+[dwoT,tb.astype(BF16)],1)).astype(F32)
        dq,dk,dv,do=[asum[:,c*D:(c+1)*D] for c in range(4)]
        table=asum[:,4*D:].reshape(HEADS,BUCKETS).T
        f=fsum.astype(F32).reshape(rows,FF//FC,2,FC)
        di=f[:,:,0].reshape(rows,FF); du=f[:,:,1].reshape(rows,FF)
        dg1=jnp.sum(dq*low(query_w)+dk*low(key_w)+dv*low(value_w),axis=1)/low(norm1_gain)
        dg2=jnp.sum(di*low(ffn_in),axis=1)/low(norm2_gain)
    return (out,dx,dg1,dq,dk,dv,do.T,table,dg2,di,du.T)

def solution(mesh):
    P=jax.sharding.PartitionSpec
    sizes=(mesh.shape["dp"],mesh.shape["fsdp"])
    axes=BOTH
    if sizes==(4,8):
        mesh=jax.sharding.Mesh(mesh.devices.reshape(4,4,2),ALL)
        axes=ALL
    r=P(axes,None); v=P(axes); c=P(None,axes)
    return jax.shard_map(functools.partial(body,sizes),mesh=mesh,in_specs=(r,v,v,r,r,r,c,P(),v,r,c,r),out_specs=(r,r,v,r,r,r,c,P(),v,r,c),check_vma=False)
```
